32 devices in a mesh: rep: 2 (over core), batch: 4 (over z), ctx: 4 (over y, x).
Axes of the slice: x: 2, y: 2, z: 4, core: 2. Of those that a mesh axis runs over, the one named last changes fastest.
Arguments:
- tokens: bfloat16 [8, 2304, 1024], P(('rep', 'batch'), 'ctx'), may hold values from -6 to 6
- cotangent: bfloat16 [8, 2304, 1024], P(('rep', 'batch'), 'ctx'), may hold values from -6 to 6
- segment_ids: int32 [8, 2304], P(('rep', 'batch')), may hold values from 0 to 3, never falling along the last dimension, each value on 1 to 1152 neighbouring positions
- first_gain: bfloat16 [1024], P('ctx'), may hold values from 0.099609375 to 1.8984375
- first_shift: bfloat16 [1024], P('ctx'), may hold values from -1.1953125 to 1.1953125
- second_gain: bfloat16 [1024], P('ctx'), may hold values from 0.099609375 to 1.8984375
- second_shift: bfloat16 [1024], P('ctx'), may hold values from -1.1953125 to 1.1953125
- final_gain: bfloat16 [1024], P('ctx'), may hold values from 0.099609375 to 1.8984375
- final_shift: bfloat16 [1024], P('ctx'), may hold values from -1.1953125 to 1.1953125
- project_weight: bfloat16 [1024, 3072], P('ctx'), may hold values from -0.1875 to 0.1875
- output_weight: bfloat16 [1024, 1024], P('ctx'), may hold values from -0.75 to 0.75
- upward_weight: bfloat16 [1024, 4096], P('ctx'), may hold values from -0.1875 to 0.1875
- downward_weight: bfloat16 [4096, 1024], P('ctx'), may hold values from -0.09375 to 0.09375
- store_keys: bfloat16 [32768, 1024], P(('batch', 'ctx')), may hold values from -6 to 6
- store_values: int32 [32768], P(('batch', 'ctx')), may hold values from 0 to 267743, as said below
- owners: int32 [8, 2304, 4], P(('rep', 'batch'), 'ctx'), may hold values from 0 to 15, all different within a row; in each aligned block of 576 rows (0 to 575, 576 to 1151, ..., all dimensions but the last counted through in order) at most 288 rows name the same one
- neighbours: int32 [2, 16, 16, 288, 256], P('rep', ('batch', 'ctx')), may hold values from 0 to 2047, as said below
- targets: int32 [8, 2304], P(('rep', 'batch'), 'ctx'), may hold values from 0 to 267743, as said below
- model_prob: float32 [8, 2304], P(('rep', 'batch'), 'ctx'), may hold values from 0.05 to 0.5
Outputs:
- hidden_out: bfloat16 [8, 2304, 1024], P(('rep', 'batch'), 'ctx')
- losses: float32 [8, 2304], P(('rep', 'batch'), 'ctx')
- query_grad: float32 [8, 2304, 1024], P(('rep', 'batch'), 'ctx')
- input_grad: float32 [8, 2304, 1024], P(('rep', 'batch'), 'ctx')
- project_grad: float32 [1024, 3072], P('ctx')
- output_grad: float32 [1024, 1024], P('ctx')
- upward_grad: float32 [1024, 4096], P('ctx')
- downward_grad: float32 [4096, 1024], P('ctx')
- first_gain_grad: float32 [1024], P('ctx')
- first_shift_grad: float32 [1024], P('ctx')
- second_gain_grad: float32 [1024], P('ctx')
- second_shift_grad: float32 [1024], P('ctx')
- final_gain_grad: float32 [1024], P('ctx')
- final_shift_grad: float32 [1024], P('ctx')
The draws below stay inside these ranges and needn't reach their ends.
Inputs may be any that keep to these rules, and one draw needn't show every extreme that they name: Each token names 4 different owners; in each aligned block of 576 positions of a sequence (the positions of one sequence on one device) no owner is named by more than 288 tokens. Entry [r, o, s, c, n] is the n-th neighbour, an index among owner o's 2048 keys, of the c-th request that device s of replica r sends to owner o, its requests counted in order of sequence, position and owner rank. The 256 neighbours of a slot are different, the n-th among keys n * 8 to (n + 1) * 8 - 1. Slots that no request fills hold unused indices. `store_values`: word ids; about half of them are four frequent words, the same four for the targets. `targets`: word ids; about half of them are four frequent words, the same four for the datastore's values.
All inputs are finite; a program needn't handle non-finite values.
Results may differ from the reference program's by a relative error of at most 0.02.
Values may be sent and summed in bfloat16 or wider, within the bound.
No kernel may reach another device: no remote copies, remote signals or barrier semaphores. Data moves between devices by JAX's collectives and lax.ppermute only.
A program may use at most 512 MiB of HBM per device.

```python
import math
import jax
import jax.numpy as jnp
import numpy as np
from jax import lax

D = 1024
HEADS = 16
FF = 4096
VOCAB = 267744
LEN = 2304
SEQ_GRP = 1
KEYS_DEV = 2048
TOP = 4
NBR = 256
SEQS = 8
BLK = 576
SHARDS = 16
MOST = 288
CAP = 288
N_REP = 2
N_BATCH = 4
N_CTX = 4


def frequent_words(base_key, out_shape, salt_value):
    common_words = jax.random.randint(jax.random.fold_in(base_key, 977), (4,), 0, VOCAB)
    own_key = jax.random.fold_in(base_key, salt_value)
    coin_key, pick_key, rare_key = jax.random.split(own_key, 3)
    coin_flip = jax.random.randint(coin_key, out_shape, 0, 2)
    pick_index = jax.random.randint(pick_key, out_shape, 0, 4)
    rare_word = jax.random.randint(rare_key, out_shape, 0, VOCAB)
    return jnp.where(coin_flip == 0, common_words[pick_index], rare_word).astype(jnp.int32)


def draw_store_values(key, part):
    return frequent_words(key, (SHARDS * KEYS_DEV,), 11)


def draw_targets(key, part):
    return frequent_words(key, (SEQS, LEN), 13)


def draw_neighbours(key, part):
    spacing = KEYS_DEV // NBR
    offsets = jax.random.randint(jax.random.fold_in(key, 17), (N_REP, SHARDS, SHARDS, CAP, NBR), 0, spacing)
    return (offsets + spacing * jnp.arange(NBR, dtype=jnp.int32)).astype(jnp.int32)


def shard_levels(key, shape, pieces, smallest, top_value):
    factor_of = 1.0
    for dim, parts in pieces:
        heights = jax.random.uniform(jax.random.fold_in(jax.random.fold_in(key, 6), dim), (parts,), jnp.float32, smallest / len(pieces), top_value / len(pieces))
        factor_of = factor_of * jnp.repeat(jnp.exp(heights), shape[dim] // parts).reshape((-1,) + (1,) * (len(shape) - 1 - dim))
    return factor_of


def profile(number_of, total, bound, skew):
    weights = [(1 << 20) // math.isqrt(grade ** skew) + 1 for grade in range(2, number_of + 1)]
    rest, holding = total - bound - (number_of - 1), [1] * (number_of - 1)
    while rest > 0:
        movable = [i for i in range(number_of - 1) if holding[i] < bound]
        mass, remaining = sum([weights[i] for i in movable]), rest
        for i in movable:
            extra = min(bound - holding[i], max(1, remaining * weights[i] // mass), rest)
            holding[i] = holding[i] + extra
            rest = rest - extra
    return np.array([bound] + holding)


def ragged_sizes(key, amount, total, reach, lean):
    if amount == 2:
        one = jax.random.randint(key, (), max(1, total - reach), min(reach, total - 1) + 1)
        return jnp.stack([one, total - one])
    sizes = jnp.asarray(profile(amount, total, reach, lean), jnp.int32)
    twos = (amount - 1) // 2
    giver, sink = sizes[1:1 + 2 * twos:2], sizes[2:2 + 2 * twos:2]
    slack = jnp.minimum(giver - 1, reach - sink)
    passed = jax.random.randint(jax.random.fold_in(key, 1), (twos,), 0, 1 << 20) % (slack + 1)
    sizes = sizes.at[1:1 + 2 * twos:2].set(giver - passed).at[2:2 + 2 * twos:2].set(sink + passed)
    return sizes[jax.random.permutation(jax.random.fold_in(key, 2), amount)]


def deal_out(stream_key, own, number, rows, amount, top, reach, lean):
    ranking = jax.random.permutation(stream_key, amount)
    packed, ordinary = load_shares(amount, rows * top, reach, lean, True), load_shares(amount, rows * top, reach, lean, False)
    places = jnp.arange(amount)

    def named(tallies, rotation):
        used = int((tallies > 0).sum())
        fixed = max(1, used // 4)
        passed = fixed + (places - fixed + rotation * (used - fixed)) % max(1, amount - fixed)
        return jnp.zeros((amount,), jnp.int32).at[ranking[jnp.where(places < fixed, places, passed)]].set(jnp.asarray(tallies, jnp.int32))

    tallies = jnp.where(number % 4 == 0, named(packed, number // 4), named(ordinary, number - number // 4 - 1))
    mixed = jax.random.permutation(jax.random.fold_in(own, 3), amount)
    giver, sink = mixed[0:amount // 2 * 2:2], mixed[1:amount // 2 * 2:2]
    room = jnp.minimum(tallies[giver] - 1, reach - tallies[sink]) // 2
    room = jnp.where((giver == ranking[0]) | (sink == ranking[0]) | (tallies[sink] == 0), 0, jnp.maximum(room, 0))
    passed = jax.random.randint(jax.random.fold_in(own, 4), (amount // 2,), 0, 1 << 20) % (room + 1)
    tallies = tallies.at[giver].add(-passed).at[sink].add(passed)
    items = jnp.searchsorted(jnp.cumsum(tallies), jnp.arange(rows * top), side="right").astype(jnp.int32)
    listing = items.reshape(top, rows).T
    listing = listing[jax.random.permutation(jax.random.fold_in(own, 1), rows)]
    rotation = jax.random.randint(jax.random.fold_in(own, 2), (rows, 1), 0, top)
    return jnp.take_along_axis(listing, (jnp.arange(top)[None, :] + rotation) % top, axis=1)


def load_shares(count, total, bound, skew, full):
    weights = [(1 << 20) // math.isqrt(grade ** skew) + 1 for grade in range(1, count + 1)]
    largest = bound if full else min(bound, max(-(-total // count), total * weights[0] // sum(weights)))
    least = 1 if total - largest >= count - 1 else 0
    holding, spare = [largest] + [least] * (count - 1), total - largest - least * (count - 1)
    while spare > 0:
        movable = [i for i in range(1, count) if holding[i] < largest] or [i for i in range(1, count) if holding[i] < bound]
        pool, left = sum([weights[i] for i in movable]), spare
        for i in movable:
            addition = min(bound - holding[i], max(1, left * weights[i] // pool), spare)
            holding[i] = holding[i] + addition
            spare = spare - addition
    return np.array(holding)


def noise(key, extent, width, reach, pieces=(), kind=jnp.bfloat16):
    drawn = jax.random.normal(key, extent, jnp.float32) * width
    if len(pieces) > 0:
        drawn = shard_levels(key, extent, pieces, -0.22, 0.18) * drawn
    return jnp.clip(drawn, min=-reach, max=reach).astype(kind)


def setup_inputs(seed: int = 0) -> dict:
    splits = jax.random.split(jax.random.key(seed), 20)
    tokens = noise(splits[0], (SEQS, LEN, D), 1.0, 6.0, ((0, 8), (1, 4)))
    cotangent = noise(splits[1], (SEQS, LEN, D), 1.0, 6.0, ((0, 8), (1, 4)))
    segment_ids = jax.vmap(lambda own: jnp.searchsorted(jnp.cumsum(ragged_sizes(own, 4, LEN, LEN // 2, 0)), jnp.arange(LEN), side="right"))(jax.random.split(splits[2], SEQS)).reshape((SEQS, LEN)).astype(jnp.int32)
    first_gain = jnp.clip(1.0 + 0.18 * jax.random.normal(splits[3], (D,), jnp.float32), 0.099609375, 1.8984375).astype(jnp.bfloat16)
    first_shift = noise(splits[4], (D,), 0.3, 1.1953125, ((0, 4),))
    second_gain = jnp.clip(1.0 + 0.18 * jax.random.normal(splits[5], (D,), jnp.float32), 0.099609375, 1.8984375).astype(jnp.bfloat16)
    second_shift = noise(splits[6], (D,), 0.3, 1.1953125, ((0, 4),))
    final_gain = jnp.clip(1.0 + 0.18 * jax.random.normal(splits[7], (D,), jnp.float32), 0.099609375, 1.8984375).astype(jnp.bfloat16)
    final_shift = noise(splits[8], (D,), 0.3, 1.1953125, ((0, 4),))
    project_weight = noise(splits[9], (D, 3 * D), D ** -0.5, 0.1875, ((0, 4),))
    output_weight = noise(splits[10], (D, D), (D // 16) ** -0.5, 0.75, ((0, 4),))
    upward_weight = noise(splits[11], (D, FF), D ** -0.5, 0.1875, ((0, 4),))
    downward_weight = noise(splits[12], (FF, D), FF ** -0.5, 0.09375, ((0, 4),))
    store_keys = noise(splits[13], (SHARDS * KEYS_DEV, D), 1.0, 6.0, ((0, 16),))
    store_values = draw_store_values(jax.random.fold_in(splits[19], 71), 0)
    owners_keys = jax.random.split(jax.random.fold_in(splits[15], 1), SEQS * LEN // BLK)
    owners_turns = jax.random.permutation(jax.random.fold_in(splits[15], 3), SEQS * LEN // BLK)
    owners = jax.vmap(lambda own, number: deal_out(jax.random.fold_in(splits[15], 2), own, number, BLK, SHARDS, TOP, MOST, 1))(owners_keys, owners_turns).reshape((SEQS, LEN, TOP))
    neighbours = draw_neighbours(jax.random.fold_in(splits[19], 71), 0)
    targets = draw_targets(jax.random.fold_in(splits[19], 71), 0)
    model_prob = jnp.clip(jnp.exp(math.log(0.5) - 2.3025851 * jax.random.uniform(splits[18], (SEQS, LEN), jnp.float32) ** shard_levels(splits[18], (SEQS, LEN), ((0, 8), (1, 4)), -0.2, 0.2)), 0.05, 0.5)
    return dict(tokens=tokens, cotangent=cotangent, segment_ids=segment_ids, first_gain=first_gain, first_shift=first_shift, second_gain=second_gain, second_shift=second_shift, final_gain=final_gain, final_shift=final_shift, project_weight=project_weight, output_weight=output_weight, upward_weight=upward_weight, downward_weight=downward_weight, store_keys=store_keys, store_values=store_values, owners=owners, neighbours=neighbours, targets=targets, model_prob=model_prob)


norm_eps = 1e-05
mix_weight = 0.25
masked_value = -1e+30
highest = lax.Precision.HIGHEST
token_block = 16

@jax.custom_vjp
def low(v):
    return lax.optimization_barrier(v.astype(jnp.bfloat16)).astype(jnp.float32)

@jax.custom_vjp
def low_back(v):
    return v

def low_keep(v):
    return (low(v), None)

def low_pass(kept, grad):
    return (grad,)

def back_keep(v):
    return (v, None)

def back_low(kept, grad):
    return (low(grad),)
low.defvjp(low_keep, low_pass)
low_back.defvjp(back_keep, back_low)

def norm_rows(values, scale_gain, shift_term):
    average = lax.optimization_barrier(jnp.mean(values, axis=-1, keepdims=True))
    centred = values - average
    spread = lax.optimization_barrier(jnp.mean(centred * centred, axis=-1, keepdims=True))
    return centred * lax.rsqrt(spread + norm_eps) * scale_gain + shift_term

def one_sequence(params, row_tokens, row_segments):
    project_weight, output_weight, upward_weight, downward_weight, first_gain, first_shift, second_gain, second_shift, final_gain, final_shift = params
    head_size = D // HEADS
    normed_one = low(norm_rows(row_tokens, first_gain, first_shift))
    projected = low(low_back(jnp.dot(normed_one, project_weight, precision=highest)))
    query_heads = projected[:, :D].reshape(LEN, HEADS, head_size)
    key_heads = projected[:, D:2 * D].reshape(LEN, HEADS, head_size)
    value_heads = projected[:, 2 * D:].reshape(LEN, HEADS, head_size)
    positions = jnp.arange(LEN, dtype=jnp.int32)
    allowed = (positions[None, :] <= positions[:, None]) & (row_segments[None, :] == row_segments[:, None])
    raw_scores = low_back(jnp.einsum('qhd,khd->hqk', query_heads, key_heads, precision=highest) * head_size ** (-0.5))
    raw_scores = jnp.where(allowed[None], raw_scores, jnp.full_like(raw_scores, masked_value))
    weights_low = low(jax.nn.softmax(raw_scores, axis=-1))
    attended = jnp.einsum('hqk,khd->qhd', weights_low, value_heads, precision=highest).reshape(LEN, D)
    attended = low(low_back(attended))
    hidden = row_tokens + low_back(jnp.dot(attended, output_weight, precision=highest))
    normed_two = low(norm_rows(hidden, second_gain, second_shift))
    upper_rows = low_back(jnp.dot(normed_two, upward_weight, precision=highest))
    active = low(jax.nn.gelu(upper_rows))
    summed = hidden + low_back(jnp.dot(active, downward_weight, precision=highest))
    return low(norm_rows(summed, final_gain, final_shift))

def block(params, token_rows, segment_ids):
    step_fn = jax.checkpoint(one_sequence)
    return lax.map(lambda block_args: step_fn(params, block_args[0], block_args[1]), (token_rows, segment_ids))

def request_rows(owners):
    blk_len = LEN // N_CTX
    per_device = owners.astype(jnp.int32).reshape(N_REP * N_BATCH, SEQ_GRP, N_CTX, blk_len, TOP)
    per_device = jnp.transpose(per_device, (0, 2, 1, 3, 4)).reshape(N_REP * N_BATCH * N_CTX, SEQ_GRP * blk_len * TOP)
    onehot = (per_device[:, :, None] == jnp.arange(SHARDS, dtype=jnp.int32)[None, None, :]).astype(jnp.int32)
    running = jnp.cumsum(onehot, axis=1).astype(jnp.int32) - jnp.int32(1)
    slots = lax.optimization_barrier(jnp.sum(running * onehot, axis=2)).astype(jnp.int32)
    slots = slots.reshape(N_REP * N_BATCH, N_CTX, SEQ_GRP, blk_len, TOP)
    slots = jnp.transpose(slots, (0, 2, 1, 3, 4)).reshape(SEQS, LEN, TOP).astype(jnp.int32)
    seq_index = jnp.arange(SEQS, dtype=jnp.int32)[:, None, None]
    group_index = seq_index // SEQ_GRP
    rep_index = group_index // N_BATCH
    batch_index = group_index % N_BATCH
    ctx_index = (jnp.arange(LEN, dtype=jnp.int32) // blk_len)[None, :, None]
    sender = (batch_index * N_CTX + ctx_index).astype(jnp.int32)
    return (((rep_index * SHARDS + owners.astype(jnp.int32)) * SHARDS + sender) * CAP + slots).astype(jnp.int32)

def knn_block(query_block, row_block, owner_block, target_block, prob_block, store_keys, store_values, key_square, near_table):
    near_ids = near_table[row_block].astype(jnp.int32)
    key_index = (owner_block.astype(jnp.int32)[..., None] * KEYS_DEV + near_ids).astype(jnp.int32)
    gathered = store_keys[key_index].astype(jnp.float32)
    inner_dots = low_back(jnp.einsum('bd,btnd->btn', query_block, gathered, precision=highest))
    near_scores = ((2.0 * inner_dots - key_square[key_index]) * D ** (-0.5)).reshape(query_block.shape[0], TOP * NBR)
    weights_near = jax.nn.softmax(near_scores, axis=-1)
    matched = (store_values[key_index] == target_block[:, None, None]).reshape(query_block.shape[0], TOP * NBR)
    knn_prob = lax.optimization_barrier(jnp.sum(jnp.where(matched, weights_near, jnp.zeros_like(weights_near)), axis=-1))
    return -jnp.log(mix_weight * knn_prob + (1.0 - mix_weight) * prob_block)

def knn_losses(query_all, table_rows, owners, targets, model_prob, store_keys, store_values, key_square, near_table):
    block_count = SEQS * LEN // token_block
    operands = (query_all.reshape(block_count, token_block, D), table_rows.reshape(block_count, token_block, TOP), owners.reshape(block_count, token_block, TOP), targets.reshape(block_count, token_block), model_prob.astype(jnp.float32).reshape(block_count, token_block))
    step_fn = jax.checkpoint(knn_block)
    losses = lax.map(lambda block_args: step_fn(block_args[0], block_args[1], block_args[2], block_args[3], block_args[4], store_keys, store_values, key_square, near_table), operands)
    return losses.reshape(SEQS, LEN)

def reference(tokens, cotangent, segment_ids, first_gain, first_shift, second_gain, second_shift, final_gain, final_shift, project_weight, output_weight, upward_weight, downward_weight, store_keys, store_values, owners, neighbours, targets, model_prob):
    params = tuple((weight.astype(jnp.float32) for weight in (project_weight, output_weight, upward_weight, downward_weight, first_gain, first_shift, second_gain, second_shift, final_gain, final_shift)))
    inputs = tokens.astype(jnp.float32)

    def whole_block(weights_all, token_rows):
        return block(weights_all, token_rows, segment_ids)
    hidden_out, block_vjp = jax.vjp(whole_block, params, inputs)
    key_square = lax.map(lambda shard_keys: lax.optimization_barrier(jnp.sum(jnp.square(shard_keys.astype(jnp.float32)), axis=1)), store_keys.reshape(SHARDS, KEYS_DEV, D)).reshape(SHARDS * KEYS_DEV)
    near_table = neighbours.astype(jnp.int32).reshape(N_REP * SHARDS * SHARDS * CAP, NBR)
    table_rows = request_rows(owners)

    def knn_part(query_all):
        return knn_losses(query_all, table_rows, owners, targets, model_prob, store_keys, store_values, key_square, near_table)
    losses, knn_vjp = jax.vjp(knn_part, hidden_out)
    query_grad, = knn_vjp(jnp.ones_like(losses))
    param_grads, input_grad = block_vjp(cotangent.astype(jnp.float32) + query_grad)
    return (hidden_out.astype(jnp.bfloat16), losses, query_grad, input_grad, param_grads[0], param_grads[1], param_grads[2], param_grads[3], param_grads[4], param_grads[5], param_grads[6], param_grads[7], param_grads[8], param_grads[9])
```

```python
import functools

import jax
import jax.numpy as jnp
from jax import lax
from jax.experimental import pallas as pl
from jax.experimental.pallas import tpu as pltpu
from jax.sharding import PartitionSpec as P

HEADS = 16


norm_eps = 1e-05
mix_weight = 0.25
masked_value = -1e30
vmem_limit = 60 * 1024 * 1024


def norm_rows(values, scale_gain, shift_term):
    average = jnp.mean(values, axis=-1, keepdims=True)
    centred = values - average
    spread = jnp.mean(centred * centred, axis=-1, keepdims=True)
    return centred * lax.rsqrt(spread + norm_eps) * scale_gain + shift_term


def row_dot(left_side, right_side):
    return jnp.dot(left_side, right_side, preferred_element_type=jnp.float32)


def left_dot(left_side, right_side):
    return lax.dot_general(
        left_side, right_side, (((0,), (0,)), ((), ())), preferred_element_type=jnp.float32
    )


def right_dot(left_side, right_side):
    return lax.dot_general(
        left_side, right_side, (((1,), (1,)), ((), ())), preferred_element_type=jnp.float32
    )


def spec(shape, index_map):
    return pl.BlockSpec(shape, index_map)


def kernel_params(dims=1):
    return pltpu.CompilerParams(
        vmem_limit_bytes=vmem_limit, dimension_semantics=("arbitrary",) * dims
    )


def head_rows(head, size):
    return slice(head * size, (head + 1) * size)


def masked_heads(block, head_count, axis):
    size = block.shape[axis] // head_count
    index = lax.broadcasted_iota(jnp.int32, block.shape, axis) // size
    zero = jnp.zeros((), block.dtype)
    return [jnp.where(index == head, block, zero) for head in range(head_count)]


def block_mask(key_block, query_block, size, start_row):
    key_pos = key_block * size + lax.broadcasted_iota(jnp.int32, (size, size), 0)
    query_pos = query_block * size + lax.broadcasted_iota(jnp.int32, (size, size), 1)
    return (key_pos <= query_pos) & (key_pos >= start_row)


def attend_kernel(
    head_count, low_ref, q_ref, k_ref, v_ref, start_ref, o_ref, lse_ref, vt_ref, acc_ref
):
    step = pl.program_id(0)
    size, width = q_ref.shape
    head_size = width // head_count
    blocks = k_ref.shape[0] // size

    @pl.when(step == 0)
    def _():
        for block in range(blocks):
            rows = slice(block * size, (block + 1) * size)
            vt_ref[:, rows] = v_ref[rows, :].astype(jnp.float32).T.astype(jnp.bfloat16)

    scaled = q_ref[...].astype(jnp.float32) * (head_size ** (-0.5))
    turned = masked_heads(scaled.T, head_count, 0)
    turned = [part.astype(jnp.bfloat16) for part in turned]
    start_row = start_ref[0:1, :]
    acc_ref[...] = jnp.zeros_like(acc_ref)
    first = (
        tuple(jnp.full((1, size), masked_value, jnp.float32) for _ in range(head_count)),
        tuple(jnp.zeros((1, size), jnp.float32) for _ in range(head_count)),
    )

    def body(block, state):
        peaks, totals = state
        rows = pl.ds(pl.multiple_of(block * size, size), size)
        keys = k_ref[rows, :]
        allowed = block_mask(block, step, size, start_row)
        new_peaks, new_totals = [], []
        for head in range(head_count):
            scores = jnp.where(allowed, row_dot(keys, turned[head]), masked_value)
            peak = jnp.maximum(peaks[head], jnp.max(scores, axis=0, keepdims=True))
            fade = jnp.exp(peaks[head] - peak)
            weights = jnp.exp(scores - peak)
            new_peaks.append(peak)
            new_totals.append(totals[head] * fade + jnp.sum(weights, axis=0, keepdims=True))
            part = head_rows(head, head_size)
            acc_ref[part, :] = acc_ref[part, :] * fade + row_dot(
                vt_ref[part, rows], weights.astype(jnp.bfloat16)
            )
        return tuple(new_peaks), tuple(new_totals)

    peaks, totals = lax.fori_loop(low_ref[step], step + 1, body, first)
    for head in range(head_count):
        part = head_rows(head, head_size)
        acc_ref[part, :] = acc_ref[part, :] / totals[head]
        lse_ref[head : head + 1, :] = peaks[head] + jnp.log(totals[head])
    o_ref[...] = acc_ref[...].T.astype(jnp.bfloat16)


def attend(query, key, value, start_rows, low_blocks, head_count, size):
    length, width = query.shape
    blocks = length // size
    stat_rows = -(-head_count // 8) * 8
    return pl.pallas_call(
        functools.partial(attend_kernel, head_count),
        grid_spec=pltpu.PrefetchScalarGridSpec(
            num_scalar_prefetch=1,
            grid=(blocks,),
            in_specs=[
                spec((size, width), lambda i, low: (i, 0)),
                spec((length, width), lambda i, low: (0, 0)),
                spec((length, width), lambda i, low: (0, 0)),
                spec((8, size), lambda i, low: (0, i)),
            ],
            out_specs=[
                spec((size, width), lambda i, low: (i, 0)),
                spec((stat_rows, size), lambda i, low: (0, i)),
            ],
            scratch_shapes=[
                pltpu.VMEM((width, length), jnp.bfloat16),
                pltpu.VMEM((width, size), jnp.float32),
            ],
        ),
        out_shape=[
            jax.ShapeDtypeStruct((length, width), jnp.bfloat16),
            jax.ShapeDtypeStruct((stat_rows, length), jnp.float32),
        ],
        compiler_params=kernel_params(),
        cost_estimate=pl.CostEstimate(
            flops=2 * length * length * width,
            bytes_accessed=8 * length * width,
            transcendentals=length * length * head_count // 3,
        ),
        name="attend",
    )(low_blocks, query, key, value, start_rows)


def attend_back_kernel(
    head_count,
    low_ref,
    q_ref,
    k_ref,
    v_ref,
    grad_ref,
    o_ref,
    lse_ref,
    start_ref,
    dq_ref,
    dk_ref,
    dv_ref,
    kt_ref,
    dkey_ref,
    dvalue_ref,
    dqt_ref,
    score_ref,
    weight_ref,
):
    step = pl.program_id(0)
    size, width = q_ref.shape
    head_size = width // head_count
    score_scale = head_size ** (-0.5)
    blocks = k_ref.shape[0] // size

    @pl.when(step == 0)
    def _():
        dkey_ref[...] = jnp.zeros_like(dkey_ref)
        dvalue_ref[...] = jnp.zeros_like(dvalue_ref)
        for block in range(blocks):
            rows = slice(block * size, (block + 1) * size)
            kt_ref[:, rows] = k_ref[rows, :].astype(jnp.float32).T.astype(jnp.bfloat16)

    scaled = q_ref[...].astype(jnp.float32) * score_scale
    grads = grad_ref[...].astype(jnp.float32)
    dots = (grads * o_ref[...].astype(jnp.float32)).T
    query_turned = [p.astype(jnp.bfloat16) for p in masked_heads(scaled.T, head_count, 0)]
    grad_turned = [p.astype(jnp.bfloat16) for p in masked_heads(grads.T, head_count, 0)]
    query_stack = jnp.concatenate(
        [p.astype(jnp.bfloat16) for p in masked_heads(scaled, head_count, 1)], axis=0
    )
    grad_stack = jnp.concatenate(
        [p.astype(jnp.bfloat16) for p in masked_heads(grads, head_count, 1)], axis=0
    )
    row_dots = [
        jnp.sum(dots[head_rows(head, head_size), :], axis=0, keepdims=True)
        for head in range(head_count)
    ]
    start_row = start_ref[0:1, :]
    dqt_ref[...] = jnp.zeros_like(dqt_ref)

    def body(block, carry):
        rows = pl.ds(pl.multiple_of(block * size, size), size)
        keys = k_ref[rows, :]
        values = v_ref[rows, :]
        allowed = block_mask(block, step, size, start_row)
        for head in range(head_count):
            lanes = slice(head * size, (head + 1) * size)
            part = head_rows(head, head_size)
            scores = jnp.where(allowed, row_dot(keys, query_turned[head]), masked_value)
            weights = jnp.exp(scores - lse_ref[head : head + 1, :])
            weight_grad = row_dot(values, grad_turned[head])
            score_grad = (weights * (weight_grad - row_dots[head])).astype(jnp.bfloat16)
            score_ref[:, lanes] = score_grad
            weight_ref[:, lanes] = weights.astype(jnp.bfloat16)
            dqt_ref[part, :] += row_dot(kt_ref[part, rows], score_grad)
        dkey_ref[rows, :] += row_dot(score_ref[...], query_stack)
        dvalue_ref[rows, :] += row_dot(weight_ref[...], grad_stack)
        return carry

    lax.fori_loop(low_ref[step], step + 1, body, 0)
    dq_ref[...] = (dqt_ref[...] * score_scale).T.astype(jnp.bfloat16)

    @pl.when(step == blocks - 1)
    def _():
        dk_ref[...] = dkey_ref[...].astype(jnp.bfloat16)
        dv_ref[...] = dvalue_ref[...].astype(jnp.bfloat16)


def attend_back(query, key, value, grad, attended, lse, start_rows, low_blocks, head_count, size):
    length, width = query.shape
    blocks = length // size
    stat_rows = lse.shape[0]
    block_spec = spec((size, width), lambda i, low: (i, 0))
    whole_spec = spec((length, width), lambda i, low: (0, 0))
    return pl.pallas_call(
        functools.partial(attend_back_kernel, head_count),
        grid_spec=pltpu.PrefetchScalarGridSpec(
            num_scalar_prefetch=1,
            grid=(blocks,),
            in_specs=[
                block_spec,
                whole_spec,
                whole_spec,
                block_spec,
                block_spec,
                spec((stat_rows, size), lambda i, low: (0, i)),
                spec((8, size), lambda i, low: (0, i)),
            ],
            out_specs=[block_spec, whole_spec, whole_spec],
            scratch_shapes=[
                pltpu.VMEM((width, length), jnp.bfloat16),
                pltpu.VMEM((length, width), jnp.float32),
                pltpu.VMEM((length, width), jnp.float32),
                pltpu.VMEM((width, size), jnp.float32),
                pltpu.VMEM((size, head_count * size), jnp.bfloat16),
                pltpu.VMEM((size, head_count * size), jnp.bfloat16),
            ],
        ),
        out_shape=[jax.ShapeDtypeStruct((length, width), jnp.bfloat16)] * 3,
        compiler_params=kernel_params(),
        cost_estimate=pl.CostEstimate(
            flops=5 * length * length * width,
            bytes_accessed=16 * length * width,
            transcendentals=length * length * head_count // 3,
        ),
        name="attend_back",
    )(low_blocks, query, key, value, grad, attended, lse, start_rows)


def to_columns(block, rows):
    parts = [block[group].T for group in range(block.shape[0])]
    return parts[0] if len(parts) == 1 else jnp.concatenate(parts, axis=0)


def near_kernel(
    spacing, dist_scale, q_ref, keys_ref, square_ref, values_ref, near_ref, target_ref, e_ref, s_ref
):
    rows, near_count = near_ref.shape
    lane = lax.broadcasted_iota(jnp.int32, (rows, near_count), 1)
    offset = near_ref[...] - spacing * lane
    target = to_columns(target_ref, rows)[:, 0:1]
    picked = jnp.zeros((rows, near_count), jnp.float32)
    words = jnp.full((rows, near_count), -1.0, jnp.float32)
    queries = q_ref[...]
    for plane in range(spacing):
        lanes = slice(plane * near_count, (plane + 1) * near_count)
        inner = row_dot(queries, keys_ref[:, lanes])
        chosen = offset == plane
        picked = jnp.where(chosen, 2.0 * inner - square_ref[plane : plane + 1, :], picked)
        words = jnp.where(chosen, values_ref[plane : plane + 1, :], words)
    scores = picked * dist_scale
    matched = words == target
    peak = jnp.max(scores, axis=1, keepdims=True)
    raised = jnp.exp(scores - peak)
    total = jnp.sum(raised, axis=1, keepdims=True)
    hits = jnp.sum(jnp.where(matched, raised, 0.0), axis=1, keepdims=True)
    e_ref[...] = jnp.where(matched, raised, -raised)
    stat_lane = lax.broadcasted_iota(jnp.int32, (rows, 128), 1)
    stats = jnp.where(stat_lane == 0, peak, jnp.where(stat_lane == 1, total, hits))
    groups, stat_rows, piece = s_ref.shape
    for group in range(groups):
        s_ref[group] = stats[group * piece : (group + 1) * piece, :].T[:stat_rows, :]


def near_scores(queries, keys_turned, square, values, near, target_rows, rows, spacing):
    slot_rows, width = queries.shape
    near_count = near.shape[1]
    groups = target_rows.shape[0] * rows // slot_rows
    piece = target_rows.shape[2]
    keys = keys_turned.shape[1]
    return pl.pallas_call(
        functools.partial(near_kernel, spacing, width ** (-0.5)),
        grid=(slot_rows // rows,),
        in_specs=[
            spec((rows, width), lambda i: (i, 0)),
            spec((width, keys), lambda i: (0, 0)),
            spec((spacing, near_count), lambda i: (0, 0)),
            spec((spacing, near_count), lambda i: (0, 0)),
            spec((rows, near_count), lambda i: (i, 0)),
            spec((groups, 8, piece), lambda i: (i, 0, 0)),
        ],
        out_specs=[
            spec((rows, near_count), lambda i: (i, 0)),
            spec((groups, 8, piece), lambda i: (i, 0, 0)),
        ],
        out_shape=[
            jax.ShapeDtypeStruct((slot_rows, near_count), jnp.float32),
            jax.ShapeDtypeStruct(target_rows.shape, jnp.float32),
        ],
        compiler_params=kernel_params(),
        cost_estimate=pl.CostEstimate(
            flops=2 * slot_rows * width * keys,
            bytes_accessed=slot_rows * (2 * width + 8 * near_count) + 2 * keys * width,
            transcendentals=slot_rows * near_count,
        ),
        name="near_scores",
    )(queries, keys_turned, square, values, near, target_rows)


def near_back_kernel(spacing, factor, e_ref, near_ref, coeff_ref, keys_ref, out_ref, dense_ref):
    rows, near_count = near_ref.shape
    lane = lax.broadcasted_iota(jnp.int32, (rows, near_count), 1)
    offset = near_ref[...] - spacing * lane
    columns = to_columns(coeff_ref, rows)
    coefficient, probability = columns[:, 0:1], columns[:, 1:2]
    marked = e_ref[...]
    matched = jnp.where(marked > 0.0, 1.0, 0.0)
    grads = coefficient * (matched - probability) * jnp.abs(marked) * factor
    for plane in range(spacing):
        lanes = slice(plane * near_count, (plane + 1) * near_count)
        dense_ref[:, lanes] = jnp.where(offset == plane, grads, 0.0).astype(jnp.bfloat16)
    out_ref[...] = row_dot(dense_ref[...], keys_ref[...]).astype(out_ref.dtype)


def near_back(marked, near, coeff_rows, keys_planes, rows, spacing):
    slot_rows, near_count = near.shape
    keys, width = keys_planes.shape
    groups = coeff_rows.shape[0] * rows // slot_rows
    piece = coeff_rows.shape[2]
    return pl.pallas_call(
        functools.partial(near_back_kernel, spacing, 2.0 * width ** (-0.5)),
        grid=(slot_rows // rows,),
        in_specs=[
            spec((rows, near_count), lambda i: (i, 0)),
            spec((rows, near_count), lambda i: (i, 0)),
            spec((groups, 8, piece), lambda i: (i, 0, 0)),
            spec((keys, width), lambda i: (0, 0)),
        ],
        out_specs=spec((rows, width), lambda i: (i, 0)),
        out_shape=jax.ShapeDtypeStruct((slot_rows, width), jnp.bfloat16),
        scratch_shapes=[pltpu.VMEM((rows, keys), jnp.bfloat16)],
        compiler_params=kernel_params(),
        cost_estimate=pl.CostEstimate(
            flops=2 * slot_rows * width * keys,
            bytes_accessed=slot_rows * (2 * width + 8 * near_count) + 2 * keys * width,
            transcendentals=0,
        ),
        name="near_back",
    )(marked, near, coeff_rows, keys_planes)


def pack_kernel(rows_ref, map_ref, out_ref):
    capacity = out_ref.shape[1]
    slot = lax.broadcasted_iota(jnp.int32, (capacity, rows_ref.shape[0]), 0)
    chosen = jnp.where(map_ref[0] == slot, 1.0, 0.0).astype(jnp.bfloat16)
    out_ref[0] = row_dot(chosen, rows_ref[...]).astype(out_ref.dtype)


def pack_rows(rows, slot_map, capacity):
    owners, tokens = slot_map.shape
    width = rows.shape[1]
    return pl.pallas_call(
        pack_kernel,
        grid=(owners,),
        in_specs=[
            spec((tokens, width), lambda o: (0, 0)),
            spec((1, 1, tokens), lambda o: (o, 0, 0)),
        ],
        out_specs=spec((1, capacity, width), lambda o: (o, 0, 0)),
        out_shape=jax.ShapeDtypeStruct((owners, capacity, width), rows.dtype),
        compiler_params=kernel_params(),
        cost_estimate=pl.CostEstimate(
            flops=2 * owners * capacity * tokens * width,
            bytes_accessed=2 * owners * capacity * width,
            transcendentals=0,
        ),
        name="pack_rows",
    )(rows, slot_map.reshape(owners, 1, tokens))


def unpack_kernel(back_ref, column_ref, out_ref):
    owner = pl.program_id(0)
    tokens, capacity = out_ref.shape[0], back_ref.shape[1]
    slot = lax.broadcasted_iota(jnp.int32, (tokens, capacity), 1)
    chosen = jnp.where(column_ref[0] == slot, 1.0, 0.0).astype(jnp.bfloat16)
    part = row_dot(chosen, back_ref[0])

    @pl.when(owner == 0)
    def _():
        out_ref[...] = part

    @pl.when(owner > 0)
    def _():
        out_ref[...] += part


def unpack_rows(returned, slot_map):
    owners, capacity, width = returned.shape
    tokens = slot_map.shape[1]
    return pl.pallas_call(
        unpack_kernel,
        grid=(owners,),
        in_specs=[
            spec((1, capacity, width), lambda o: (o, 0, 0)),
            spec((1, tokens, 1), lambda o: (o, 0, 0)),
        ],
        out_specs=spec((tokens, width), lambda o: (0, 0)),
        out_shape=jax.ShapeDtypeStruct((tokens, width), jnp.float32),
        compiler_params=kernel_params(),
        cost_estimate=pl.CostEstimate(
            flops=2 * owners * capacity * tokens * width,
            bytes_accessed=2 * owners * capacity * width,
            transcendentals=0,
        ),
        name="unpack_rows",
    )(returned, slot_map.reshape(owners, tokens, 1))


def mix_kernel(stats_ref, map_ref, prob_ref, loss_ref, send_ref, peak_ref, total_ref, hits_ref):
    owners, stat_rows, capacity = stats_ref.shape
    tokens = map_ref.shape[1]
    slot = lax.broadcasted_iota(jnp.int32, (capacity, tokens), 0)
    for owner in range(owners):
        chosen = map_ref[owner : owner + 1, :] == slot
        columns = stats_ref[owner].T
        for place, target in enumerate((peak_ref, total_ref, hits_ref)):
            target[owner : owner + 1, :] = jnp.sum(
                jnp.where(chosen, columns[:, place : place + 1], 0.0), axis=0, keepdims=True
            )
    member = map_ref[...] >= 0
    peaks = jnp.where(member, peak_ref[...], -3e38)
    best = jnp.max(peaks, axis=0, keepdims=True)
    rescale = jnp.where(member, jnp.exp(peaks - best), 0.0)
    knn_total = jnp.sum(total_ref[...] * rescale, axis=0, keepdims=True)
    knn_prob = jnp.sum(hits_ref[...] * rescale, axis=0, keepdims=True) / knn_total
    mixture = mix_weight * knn_prob + (1.0 - mix_weight) * prob_ref[...]
    loss_ref[...] = -jnp.log(mixture)
    peak_ref[...] = (-mix_weight / (mixture * knn_total)) * rescale
    for owner in range(owners):
        chosen = map_ref[owner : owner + 1, :] == slot
        coefficient = jnp.sum(
            jnp.where(chosen, peak_ref[owner : owner + 1, :], 0.0), axis=1, keepdims=True
        )
        probability = jnp.sum(jnp.where(chosen, knn_prob, 0.0), axis=1, keepdims=True)
        lane = lax.broadcasted_iota(jnp.int32, (capacity, 128), 1)
        both = jnp.where(lane == 0, coefficient, probability)
        send_ref[owner] = both.T[:stat_rows, :]


def mix_losses(stats, slot_map, model_prob):
    owners, stat_rows, capacity = stats.shape
    tokens = slot_map.shape[1]
    vmem = pl.BlockSpec(memory_space=pltpu.VMEM)
    return pl.pallas_call(
        mix_kernel,
        in_specs=[vmem] * 3,
        out_specs=[vmem] * 2,
        out_shape=[
            jax.ShapeDtypeStruct((1, tokens), jnp.float32),
            jax.ShapeDtypeStruct(stats.shape, jnp.float32),
        ],
        scratch_shapes=[pltpu.VMEM((owners, tokens), jnp.float32)] * 3,
        compiler_params=pltpu.CompilerParams(vmem_limit_bytes=vmem_limit),
        name="mix_losses",
    )(stats, slot_map, model_prob)


def row_chunk(total, choices):
    for choice in choices:
        if total % choice == 0:
            return choice
    return total


def slot_picker(slot_map, capacity):
    return slot_map[:, None, :] == jnp.arange(capacity, dtype=jnp.int32)[None, :, None]


def pack_any(rows, slot_map, capacity):
    if capacity % 16 == 0:
        return pack_rows(rows, slot_map, capacity)
    chosen = slot_picker(slot_map, capacity).astype(jnp.bfloat16)
    return row_dot(chosen, rows).astype(rows.dtype)


def unpack_any(returned, slot_map):
    capacity = returned.shape[1]
    if capacity % 16 == 0:
        return unpack_rows(returned, slot_map)
    chosen = slot_picker(slot_map, capacity).astype(jnp.bfloat16)
    return jnp.einsum("ost,osw->tw", chosen, returned, preferred_element_type=jnp.float32)


def mix_any(stats, slot_map, model_prob):
    owners, stat_rows, capacity = stats.shape
    if capacity % 16 == 0:
        return mix_losses(stats, slot_map, model_prob)
    chosen = slot_picker(slot_map, capacity)
    peak, total, hits = [
        jnp.sum(jnp.where(chosen, stats[:, row, :, None], 0.0), axis=1) for row in range(3)
    ]
    member = slot_map >= 0
    peaks = jnp.where(member, peak, -3e38)
    best = jnp.max(peaks, axis=0, keepdims=True)
    rescale = jnp.where(member, jnp.exp(peaks - best), 0.0)
    knn_total = jnp.sum(total * rescale, axis=0, keepdims=True)
    knn_prob = jnp.sum(hits * rescale, axis=0, keepdims=True) / knn_total
    mixture = mix_weight * knn_prob + (1.0 - mix_weight) * model_prob
    coefficient = (-mix_weight / (mixture * knn_total)) * rescale
    sent = [
        jnp.sum(jnp.where(chosen, part[:, None, :], 0.0), axis=2)
        for part in (coefficient, jnp.broadcast_to(knn_prob, coefficient.shape))
    ]
    sent = jnp.stack(sent + [sent[1]] * (stat_rows - 2), axis=1)
    return -jnp.log(mixture), sent


def local(
    tokens,
    cotangent,
    segment_ids,
    first_gain,
    first_shift,
    second_gain,
    second_shift,
    final_gain,
    final_shift,
    project_weight,
    output_weight,
    upward_weight,
    downward_weight,
    store_keys,
    store_values,
    owners,
    neighbours,
    targets,
    model_prob,
):
    head_count = HEADS
    group_seqs, block_len, width = tokens.shape
    seq_len = segment_ids.shape[1]
    ctx_count = lax.axis_size("ctx")
    shard_count = lax.axis_size("batch") * ctx_count
    capacity = neighbours.shape[3]
    near_count = neighbours.shape[4]
    top_count = owners.shape[2]
    key_count = store_keys.shape[0]
    spacing = key_count // near_count
    slot_rows = shard_count * capacity
    everyone = ("batch", "ctx")
    own_heads = head_count // ctx_count
    own_width = width // ctx_count
    attend_size = row_chunk(seq_len, (256, 128))

    tokens_full = lax.all_gather(tokens[0], "ctx", axis=0, tiled=True)
    vectors = jnp.stack(
        [first_gain, first_shift, second_gain, second_shift, final_gain, final_shift]
    )
    vectors = lax.all_gather(vectors, "ctx", axis=1, tiled=True).astype(jnp.float32)
    gain_list = [vectors[row] for row in range(6)]
    own_rows = project_weight.shape[0]
    proj_own = lax.all_to_all(
        project_weight.reshape(own_rows, 3, ctx_count, own_width).transpose(2, 0, 1, 3),
        "ctx",
        split_axis=0,
        concat_axis=0,
        tiled=True,
    ).reshape(width, 3 * own_width)

    def gather_weight(weight):
        half = weight.shape[0] // lax.axis_size("rep")
        mine = lax.dynamic_slice_in_dim(weight, lax.axis_index("rep") * half, half, 0)
        return lax.all_gather(mine, ("ctx", "rep"), axis=0, tiled=True)

    out_full = gather_weight(output_weight)
    up_full = gather_weight(upward_weight)
    down_full = gather_weight(downward_weight)

    member = jnp.any(
        owners[0][:, :, None] == jnp.arange(shard_count, dtype=jnp.int32)[None, None, :], axis=1
    )
    place = jnp.arange(block_len, dtype=jnp.int32)
    earlier = (place[:, None] <= place[None, :]).astype(jnp.bfloat16)
    running = left_dot(member.astype(jnp.bfloat16), earlier).astype(jnp.int32)
    slot_map = jnp.where(member.T, running - 1, -1)
    send_targets = jnp.sum(
        jnp.where(slot_picker(slot_map, capacity), targets.reshape(1, 1, -1), 0), axis=2
    )
    got_targets = lax.all_to_all(
        send_targets.astype(jnp.int32), everyone, split_axis=0, concat_axis=0, tiled=True
    ).astype(jnp.float32)
    planes = store_keys.reshape(near_count, spacing, width).transpose(1, 0, 2)
    planes = planes.reshape(key_count, width)
    planes_turned = planes.T
    key_square = jnp.sum(jnp.square(store_keys.astype(jnp.float32)), axis=1)
    key_square = key_square.reshape(near_count, spacing).T
    value_planes = store_values.astype(jnp.float32).reshape(near_count, spacing).T
    near_table = neighbours.reshape(slot_rows, near_count)
    if capacity % 16 == 0:
        near_rows = row_chunk(slot_rows, (2 * capacity,))
        stat_shape = (shard_count, 8, capacity)
    else:
        near_rows = row_chunk(slot_rows, (576, 512, 384, 256, 128))
        stat_shape = (slot_rows // near_rows, 8, near_rows)
    target_rows = jnp.broadcast_to(got_targets.reshape(stat_shape[0], 1, stat_shape[2]), stat_shape)

    segments = segment_ids[0]
    start_rows = jnp.sum(
        (segments[None, :] < segments[:, None]).astype(jnp.int32), axis=1
    )
    low_blocks = start_rows[::attend_size] // attend_size
    start_rows = jnp.broadcast_to(start_rows[None, :], (8, seq_len))
    normed_full = norm_rows(
        tokens_full.astype(jnp.float32), gain_list[0], gain_list[1]
    ).astype(jnp.bfloat16)
    projected = row_dot(normed_full, proj_own).astype(jnp.bfloat16)
    query_own = projected[:, :own_width]
    key_own = projected[:, own_width : 2 * own_width]
    value_own = projected[:, 2 * own_width :]
    attended_own, log_total = attend(
        query_own, key_own, value_own, start_rows, low_blocks, own_heads, attend_size
    )
    attended = lax.all_to_all(attended_own, "ctx", split_axis=0, concat_axis=1, tiled=True)
    inputs = tokens[0].astype(jnp.float32)
    hidden = inputs + row_dot(attended, out_full)
    normed_two = norm_rows(hidden, gain_list[2], gain_list[3]).astype(jnp.bfloat16)
    upper_rows = row_dot(normed_two, up_full)
    active = jax.nn.gelu(upper_rows).astype(jnp.bfloat16)
    summed = hidden + row_dot(active, down_full)
    final_rows = norm_rows(summed, gain_list[4], gain_list[5]).astype(jnp.bfloat16)

    got_queries = lax.all_to_all(
        pack_any(final_rows, slot_map, capacity),
        everyone,
        split_axis=0,
        concat_axis=0,
        tiled=True,
    ).reshape(slot_rows, width)
    marked, stats = near_scores(
        got_queries,
        planes_turned,
        key_square,
        value_planes,
        near_table,
        target_rows,
        near_rows,
        spacing,
    )

    def to_senders(rows):
        if rows.shape[0] == shard_count:
            return rows
        return rows.transpose(1, 0, 2).reshape(8, shard_count, capacity).transpose(1, 0, 2)

    def to_blocks(rows):
        if rows.shape == stat_shape:
            return rows
        return (
            rows.transpose(1, 0, 2)
            .reshape(8, stat_shape[0], stat_shape[2])
            .transpose(1, 0, 2)
        )

    replies = lax.all_to_all(
        to_senders(stats), everyone, split_axis=0, concat_axis=0, tiled=True
    )
    token_loss, send_coeff = mix_any(replies, slot_map, model_prob)
    got_coeff = lax.all_to_all(send_coeff, everyone, split_axis=0, concat_axis=0, tiled=True)
    partial_grad = near_back(
        marked, near_table, to_blocks(got_coeff), planes, near_rows, spacing
    ).reshape(shard_count, capacity, width)
    returned = lax.all_to_all(partial_grad, everyone, split_axis=0, concat_axis=0, tiled=True)
    query_grad = unpack_any(returned, slot_map)

    out_grad = cotangent[0].astype(jnp.float32) + query_grad
    final_vjp = jax.vjp(norm_rows, summed, gain_list[4], gain_list[5])[1]
    summed_grad, final_gain_grad, final_shift_grad = final_vjp(out_grad)
    branch_grad = summed_grad.astype(jnp.bfloat16)
    downward_grad = left_dot(active, branch_grad)
    active_grad = right_dot(branch_grad, down_full)
    gelu_vjp = jax.vjp(jax.nn.gelu, upper_rows)[1]
    upper_grad = gelu_vjp(active_grad)[0].astype(jnp.bfloat16)
    upward_grad = left_dot(normed_two, upper_grad)
    second_vjp = jax.vjp(norm_rows, hidden, gain_list[2], gain_list[3])[1]
    hidden_part, second_gain_grad, second_shift_grad = second_vjp(right_dot(upper_grad, up_full))
    hidden_grad = summed_grad + hidden_part
    attn_grad = hidden_grad.astype(jnp.bfloat16)
    output_grad = left_dot(attended, attn_grad)
    attended_grad = right_dot(attn_grad, out_full).astype(jnp.bfloat16)
    grad_own = lax.all_to_all(attended_grad, "ctx", split_axis=1, concat_axis=0, tiled=True)
    proj_grad = jnp.concatenate(
        attend_back(
            query_own,
            key_own,
            value_own,
            grad_own,
            attended_own,
            log_total,
            start_rows,
            low_blocks,
            own_heads,
            attend_size,
        ),
        axis=1,
    )
    normed_terms = right_dot(proj_grad, proj_own)
    first_vjp = jax.vjp(
        lambda gain, shift: norm_rows(tokens_full.astype(jnp.float32), gain, shift),
        gain_list[0],
        gain_list[1],
    )[1]
    first_gain_grad, first_shift_grad = first_vjp(normed_terms)
    normed_grad = lax.psum_scatter(
        normed_terms.astype(jnp.bfloat16), "ctx", scatter_dimension=0, tiled=True
    ).astype(jnp.float32)
    input_vjp = jax.vjp(lambda rows: norm_rows(rows, gain_list[0], gain_list[1]), inputs)[1]
    input_grad = hidden_grad + input_vjp(normed_grad)[0]

    def scatter_grad(grad):
        return lax.psum_scatter(
            grad.astype(jnp.bfloat16), ("ctx", "rep"), scatter_dimension=0, tiled=True
        )

    project_part = lax.all_to_all(
        left_dot(normed_full, proj_grad).astype(jnp.bfloat16),
        "ctx",
        split_axis=0,
        concat_axis=0,
        tiled=True,
    )
    project_part = (
        project_part.reshape(ctx_count, own_rows, 3, own_width)
        .transpose(1, 2, 0, 3)
        .reshape(own_rows, 3 * width)
    )
    pieces = (
        lax.psum_scatter(project_part, "rep", scatter_dimension=0, tiled=True),
        scatter_grad(output_grad),
        scatter_grad(upward_grad),
        scatter_grad(downward_grad),
    )
    weight_grads = [
        lax.all_gather(lax.psum(piece, "batch"), "rep", axis=0, tiled=True).astype(jnp.float32)
        for piece in pieces
    ]
    vector_grads = lax.psum(
        jnp.stack(
            [
                first_gain_grad,
                first_shift_grad,
                second_gain_grad,
                second_shift_grad,
                final_gain_grad,
                final_shift_grad,
            ]
        ),
        ("rep", "batch", "ctx"),
    )
    own_vector = first_gain.shape[0]
    vector_grads = lax.dynamic_slice_in_dim(
        vector_grads, lax.axis_index("ctx") * own_vector, own_vector, 1
    )
    return (
        final_rows.reshape(group_seqs, block_len, width),
        token_loss.reshape(group_seqs, block_len),
        query_grad.reshape(group_seqs, block_len, width),
        input_grad.reshape(group_seqs, block_len, width),
        *weight_grads,
        *[vector_grads[row] for row in range(6)],
    )


def solution(mesh):
    placed = (
        P(("rep", "batch"), "ctx", None),
        P(("rep", "batch"), "ctx", None),
        P(("rep", "batch"), None),
        P("ctx"),
        P("ctx"),
        P("ctx"),
        P("ctx"),
        P("ctx"),
        P("ctx"),
        P("ctx", None),
        P("ctx", None),
        P("ctx", None),
        P("ctx", None),
        P(("batch", "ctx"), None),
        P(("batch", "ctx")),
        P(("rep", "batch"), "ctx", None),
        P("rep", ("batch", "ctx"), None, None, None),
        P(("rep", "batch"), "ctx"),
        P(("rep", "batch"), "ctx"),
    )
    return jax.shard_map(
        local,
        mesh=mesh,
        in_specs=placed,
        out_specs=(
            P(("rep", "batch"), "ctx", None),
            P(("rep", "batch"), "ctx"),
            P(("rep", "batch"), "ctx", None),
            P(("rep", "batch"), "ctx", None),
            P("ctx", None),
            P("ctx", None),
            P("ctx", None),
            P("ctx", None),
            P("ctx"),
            P("ctx"),
            P("ctx"),
            P("ctx"),
            P("ctx"),
            P("ctx"),
        ),
        check_vma=False,
    )
```

```python
import functools

import jax
import jax.numpy as jnp
from jax import lax
from jax.experimental import pallas as pl
from jax.experimental.pallas import tpu as pltpu
from jax.sharding import PartitionSpec as P

HEADS = 16


norm_eps = 1e-05
mix_weight = 0.25
masked_value = -1e30
vmem_limit = 60 * 1024 * 1024
small_cost = pl.CostEstimate(flops=1000, bytes_accessed=1000, transcendentals=0)


def norm_rows(values, scale_gain, shift_term):
    average = jnp.mean(values, axis=-1, keepdims=True)
    centred = values - average
    spread = jnp.mean(centred * centred, axis=-1, keepdims=True)
    return centred * lax.rsqrt(spread + norm_eps) * scale_gain + shift_term


def row_dot(left_side, right_side):
    return jnp.dot(left_side, right_side, preferred_element_type=jnp.float32)


def left_dot(left_side, right_side):
    return lax.dot_general(
        left_side, right_side, (((0,), (0,)), ((), ())), preferred_element_type=jnp.float32
    )


def right_dot(left_side, right_side):
    return lax.dot_general(
        left_side, right_side, (((1,), (1,)), ((), ())), preferred_element_type=jnp.float32
    )


def spec(shape, index_map):
    return pl.BlockSpec(shape, index_map)


def kernel_params(dims=1):
    return pltpu.CompilerParams(
        vmem_limit_bytes=vmem_limit, dimension_semantics=("arbitrary",) * dims
    )


def later(kernel, place, count):
    return lambda *refs: kernel(*refs[:place], *refs[place + count :])


def later_specs(after):
    return [pl.BlockSpec(memory_space=pl.ANY)] * len(after)


def run_after(arrays, after):
    def kernel(*refs):
        pass

    return pl.pallas_call(
        kernel,
        in_specs=later_specs((*arrays, *after)),
        out_specs=later_specs(arrays),
        out_shape=[jax.ShapeDtypeStruct(rows.shape, rows.dtype) for rows in arrays],
        input_output_aliases={place: place for place in range(len(arrays))},
        cost_estimate=small_cost,
        name="run_after",
    )(*arrays, *after)


def place_kernel(count, start_ref, *refs):
    for place in range(count):

        @pl.when(pl.program_id(0) == place)
        def _():
            refs[count][...] = refs[place][...]


def place_rows(pieces, places):
    count = len(pieces)
    rows, width = pieces[0].shape
    return pl.pallas_call(
        functools.partial(place_kernel, count),
        grid_spec=pltpu.PrefetchScalarGridSpec(
            num_scalar_prefetch=1,
            grid=(count,),
            in_specs=[spec((rows, width), lambda i, places: (0, 0))] * count,
            out_specs=spec((rows, width), lambda i, places: (places[i], 0)),
        ),
        out_shape=jax.ShapeDtypeStruct((count * rows, width), pieces[0].dtype),
        compiler_params=kernel_params(),
        cost_estimate=small_cost,
        name="place_rows",
    )(places, *pieces)


def head_rows(head, size):
    return slice(head * size, (head + 1) * size)


def masked_heads(block, head_count, axis):
    size = block.shape[axis] // head_count
    index = lax.broadcasted_iota(jnp.int32, block.shape, axis) // size
    zero = jnp.zeros((), block.dtype)
    return [jnp.where(index == head, block, zero) for head in range(head_count)]


def block_mask(key_block, query_block, size, start_row):
    key_pos = key_block * size + lax.broadcasted_iota(jnp.int32, (size, size), 0)
    query_pos = query_block * size + lax.broadcasted_iota(jnp.int32, (size, size), 1)
    return (key_pos <= query_pos) & (key_pos >= start_row)


def attend_kernel(
    head_count, low_ref, q_ref, k_ref, v_ref, start_ref, o_ref, lse_ref, vt_ref, acc_ref
):
    step = pl.program_id(0)
    size, width = q_ref.shape
    head_size = width // head_count
    blocks = k_ref.shape[0] // size

    @pl.when(step == 0)
    def _():
        for block in range(blocks):
            rows = slice(block * size, (block + 1) * size)
            vt_ref[:, rows] = v_ref[rows, :].astype(jnp.float32).T.astype(jnp.bfloat16)

    scaled = q_ref[...].astype(jnp.float32) * (head_size ** (-0.5))
    turned = jnp.concatenate(
        [part.astype(jnp.bfloat16) for part in masked_heads(scaled.T, head_count, 0)], axis=1
    )
    start_row = start_ref[0:1, :]
    acc_ref[...] = jnp.zeros_like(acc_ref)
    first = (
        jnp.full((1, head_count * size), masked_value, jnp.float32),
        jnp.zeros((1, head_count * size), jnp.float32),
    )

    def body(masked, block, state):
        peak, total = state
        rows = pl.ds(pl.multiple_of(block * size, size), size)
        scores = row_dot(k_ref[rows, :], turned)
        if masked:
            allowed = block_mask(block, step, size, start_row)
            scores = jnp.concatenate(
                [
                    jnp.where(allowed, scores[:, head * size : (head + 1) * size], masked_value)
                    for head in range(head_count)
                ],
                axis=1,
            )
        new_peak = jnp.maximum(peak, jnp.max(scores, axis=0, keepdims=True))
        fade = jnp.exp(peak - new_peak)
        weights = jnp.exp(scores - new_peak)
        total = total * fade + jnp.sum(weights, axis=0, keepdims=True)
        weights = weights.astype(jnp.bfloat16)
        for head in range(head_count):
            part = head_rows(head, head_size)
            lanes = slice(head * size, (head + 1) * size)
            acc_ref[part, :] = acc_ref[part, :] * fade[:, lanes] + row_dot(
                vt_ref[part, rows], weights[:, lanes]
            )
        return new_peak, total

    low = low_ref[step]
    inner = low_ref[blocks + step]
    state = lax.fori_loop(low, inner, functools.partial(body, True), first)
    state = lax.fori_loop(inner, step, functools.partial(body, False), state)
    peak, total = body(True, step, state)
    for head in range(head_count):
        part = head_rows(head, head_size)
        lanes = slice(head * size, (head + 1) * size)
        acc_ref[part, :] = acc_ref[part, :] / total[:, lanes]
        lse_ref[head : head + 1, :] = peak[:, lanes] + jnp.log(total[:, lanes])
    o_ref[...] = acc_ref[...].T.astype(jnp.bfloat16)


def with_inner(low_blocks, start_rows, size):
    last = start_rows[0, size - 1 :: size]
    inner = jnp.minimum(-(-last // size), jnp.arange(low_blocks.shape[0], dtype=jnp.int32))
    return jnp.concatenate([low_blocks, inner])


def attend(query, key, value, start_rows, low_blocks, head_count, size, after=()):
    length, width = query.shape
    blocks = length // size
    stat_rows = -(-head_count // 8) * 8
    return pl.pallas_call(
        later(functools.partial(attend_kernel, head_count), 5, len(after)),
        grid_spec=pltpu.PrefetchScalarGridSpec(
            num_scalar_prefetch=1,
            grid=(blocks,),
            in_specs=[
                spec((size, width), lambda i, low: (i, 0)),
                spec((length, width), lambda i, low: (0, 0)),
                spec((length, width), lambda i, low: (0, 0)),
                spec((8, size), lambda i, low: (0, i)),
                *later_specs(after),
            ],
            out_specs=[
                spec((size, width), lambda i, low: (i, 0)),
                spec((stat_rows, size), lambda i, low: (0, i)),
            ],
            scratch_shapes=[
                pltpu.VMEM((width, length), jnp.bfloat16),
                pltpu.VMEM((width, size), jnp.float32),
            ],
        ),
        out_shape=[
            jax.ShapeDtypeStruct((length, width), jnp.bfloat16),
            jax.ShapeDtypeStruct((stat_rows, length), jnp.float32),
        ],
        compiler_params=kernel_params(),
        cost_estimate=pl.CostEstimate(
            flops=20_000_000_000, bytes_accessed=1000, transcendentals=0
        ),
        name="attend",
    )(with_inner(low_blocks, start_rows, size), query, key, value, start_rows, *after)


def attend_back_kernel(
    head_count,
    low_ref,
    q_ref,
    k_ref,
    v_ref,
    grad_ref,
    o_ref,
    lse_ref,
    start_ref,
    dq_ref,
    dk_ref,
    dv_ref,
    kt_ref,
    dkey_ref,
    dvalue_ref,
    dqt_ref,
    score_ref,
    weight_ref,
):
    step = pl.program_id(0)
    size, width = q_ref.shape
    head_size = width // head_count
    score_scale = head_size ** (-0.5)
    blocks = k_ref.shape[0] // size

    @pl.when(step == 0)
    def _():
        dkey_ref[...] = jnp.zeros_like(dkey_ref)
        dvalue_ref[...] = jnp.zeros_like(dvalue_ref)
        for block in range(blocks):
            rows = slice(block * size, (block + 1) * size)
            kt_ref[:, rows] = k_ref[rows, :].astype(jnp.float32).T.astype(jnp.bfloat16)

    scaled = q_ref[...].astype(jnp.float32) * score_scale
    grads = grad_ref[...].astype(jnp.float32)
    dots = (grads * o_ref[...].astype(jnp.float32)).T
    query_turned = [p.astype(jnp.bfloat16) for p in masked_heads(scaled.T, head_count, 0)]
    grad_turned = [p.astype(jnp.bfloat16) for p in masked_heads(grads.T, head_count, 0)]
    query_stack = jnp.concatenate(
        [p.astype(jnp.bfloat16) for p in masked_heads(scaled, head_count, 1)], axis=0
    )
    grad_stack = jnp.concatenate(
        [p.astype(jnp.bfloat16) for p in masked_heads(grads, head_count, 1)], axis=0
    )
    row_dots = [
        jnp.sum(dots[head_rows(head, head_size), :], axis=0, keepdims=True)
        for head in range(head_count)
    ]
    start_row = start_ref[0:1, :]
    dqt_ref[...] = jnp.zeros_like(dqt_ref)

    query_wide = jnp.concatenate(query_turned, axis=1)
    grad_wide = jnp.concatenate(grad_turned, axis=1)
    row_wide = jnp.concatenate(row_dots, axis=1)
    lse_wide = jnp.concatenate([lse_ref[head : head + 1, :] for head in range(head_count)], axis=1)

    def body(masked, block, carry):
        rows = pl.ds(pl.multiple_of(block * size, size), size)
        scores = row_dot(k_ref[rows, :], query_wide)
        if masked:
            allowed = block_mask(block, step, size, start_row)
            scores = jnp.concatenate(
                [
                    jnp.where(allowed, scores[:, head * size : (head + 1) * size], masked_value)
                    for head in range(head_count)
                ],
                axis=1,
            )
        weights = jnp.exp(scores - lse_wide)
        weight_grad = row_dot(v_ref[rows, :], grad_wide)
        score_grad = (weights * (weight_grad - row_wide)).astype(jnp.bfloat16)
        weights = weights.astype(jnp.bfloat16)
        for head in range(head_count):
            part = head_rows(head, head_size)
            lanes = slice(head * size, (head + 1) * size)
            dqt_ref[part, :] += row_dot(kt_ref[part, rows], score_grad[:, lanes])
        dkey_ref[rows, :] += row_dot(score_grad, query_stack)
        dvalue_ref[rows, :] += row_dot(weights, grad_stack)
        return carry

    low = low_ref[step]
    inner = low_ref[blocks + step]
    lax.fori_loop(low, inner, functools.partial(body, True), 0)
    lax.fori_loop(inner, step, functools.partial(body, False), 0)
    body(True, step, 0)
    dq_ref[...] = (dqt_ref[...] * score_scale).T.astype(jnp.bfloat16)

    @pl.when(step == blocks - 1)
    def _():
        dk_ref[...] = dkey_ref[...].astype(jnp.bfloat16)
        dv_ref[...] = dvalue_ref[...].astype(jnp.bfloat16)


def attend_back(
    query, key, value, grad, attended, lse, start_rows, low_blocks, head_count, size, after=()
):
    length, width = query.shape
    blocks = length // size
    stat_rows = lse.shape[0]
    block_spec = spec((size, width), lambda i, low: (i, 0))
    whole_spec = spec((length, width), lambda i, low: (0, 0))
    return pl.pallas_call(
        later(functools.partial(attend_back_kernel, head_count), 8, len(after)),
        grid_spec=pltpu.PrefetchScalarGridSpec(
            num_scalar_prefetch=1,
            grid=(blocks,),
            in_specs=[
                block_spec,
                whole_spec,
                whole_spec,
                block_spec,
                block_spec,
                spec((stat_rows, size), lambda i, low: (0, i)),
                spec((8, size), lambda i, low: (0, i)),
                *later_specs(after),
            ],
            out_specs=[block_spec, whole_spec, whole_spec],
            scratch_shapes=[
                pltpu.VMEM((width, length), jnp.bfloat16),
                pltpu.VMEM((length, width), jnp.float32),
                pltpu.VMEM((length, width), jnp.float32),
                pltpu.VMEM((width, size), jnp.float32),
                pltpu.VMEM((size, head_count * size), jnp.bfloat16),
                pltpu.VMEM((size, head_count * size), jnp.bfloat16),
            ],
        ),
        out_shape=[jax.ShapeDtypeStruct((length, width), jnp.bfloat16)] * 3,
        compiler_params=kernel_params(),
        cost_estimate=small_cost,
        name="attend_back",
    )(with_inner(low_blocks, start_rows, size), query, key, value, grad, attended, lse, start_rows, *after)


def project_kernel(count, own_width, order_ref, *refs):
    block_refs, weight_refs, vector_ref = refs[:count], refs[count : 2 * count], refs[2 * count]
    weight_ref, plain_ref, normed_ref, q_ref, k_ref, v_ref = refs[2 * count + 1 :]
    piece = weight_refs[0].shape[0]

    @pl.when(pl.program_id(0) == 0)
    def _():
        for place in range(count):
            rows = pl.ds(pl.multiple_of(order_ref[place] * piece, piece), piece)
            weight_ref[rows, :] = weight_refs[place][:, : 3 * own_width]

    for place in range(count):

        @pl.when(pl.program_id(0) == place)
        def _():
            rows = norm_rows(block_refs[place][...].astype(jnp.float32), 1.0, 0.0)
            plain_ref[...] = rows.astype(jnp.bfloat16)
            normed = (rows * vector_ref[0:1, :] + vector_ref[1:2, :]).astype(jnp.bfloat16)
            normed_ref[...] = normed
            projected = row_dot(normed, weight_ref[...]).astype(jnp.bfloat16)
            q_ref[...] = projected[:, :own_width]
            k_ref[...] = projected[:, own_width : 2 * own_width]
            v_ref[...] = projected[:, 2 * own_width :]


def project_rows(blocks, weights, order, vectors):
    count = len(blocks)
    size, width = blocks[0].shape
    weight_rows = weights[0].shape[0]
    own_width = width // count
    whole = lambda shape: spec(shape, lambda i, order: (0, 0))
    placed = lambda columns: spec((size, columns), lambda i, order: (order[i], 0))
    return pl.pallas_call(
        functools.partial(project_kernel, count, own_width),
        grid_spec=pltpu.PrefetchScalarGridSpec(
            num_scalar_prefetch=1,
            grid=(count,),
            in_specs=[
                *[whole((size, width))] * count,
                *[whole(weights[0].shape)] * count,
                whole(vectors.shape),
            ],
            out_specs=[whole((width, 3 * own_width))]
            + [placed(width)] * 2
            + [placed(own_width)] * 3,
        ),
        out_shape=[jax.ShapeDtypeStruct((width, 3 * own_width), jnp.bfloat16)]
        + [jax.ShapeDtypeStruct((count * size, width), jnp.bfloat16)] * 2
        + [jax.ShapeDtypeStruct((count * size, own_width), jnp.bfloat16)] * 3,
        compiler_params=kernel_params(),
        cost_estimate=pl.CostEstimate(
            flops=13_000_000_000, bytes_accessed=1000, transcendentals=0
        ),
        name="project_rows",
    )(order, *blocks, *weights, vectors)


def to_columns(block, rows):
    parts = [block[group].T for group in range(block.shape[0])]
    return parts[0] if len(parts) == 1 else jnp.concatenate(parts, axis=0)


def near_kernel(spacing, dist_scale, parts, *refs):
    order_ref, query_ref, keys_ref, square_ref, values_ref = refs[:5]
    near_refs, target_refs = refs[5 : 5 + parts], refs[5 + parts : 5 + 2 * parts]
    e_ref, s_ref = refs[5 + 2 * parts :]
    piece, near_count = near_refs[0].shape[1:]
    rows = parts * piece
    lane = lax.broadcasted_iota(jnp.int32, (rows, near_count), 1)
    near = jnp.concatenate([ref[0] for ref in near_refs], axis=0)
    offset = near - spacing * lane
    target = jnp.concatenate([ref[0].T for ref in target_refs], axis=0)[:, 0:1]
    picked = jnp.zeros((rows, near_count), jnp.float32)
    words = jnp.full((rows, near_count), -1.0, jnp.float32)
    queries = query_ref[...]
    for plane in range(spacing):
        lanes = slice(plane * near_count, (plane + 1) * near_count)
        inner = row_dot(queries, keys_ref[:, lanes])
        chosen = offset == plane
        picked = jnp.where(chosen, 2.0 * inner - square_ref[plane : plane + 1, :], picked)
        words = jnp.where(chosen, values_ref[plane : plane + 1, :], words)
    scores = picked * dist_scale
    matched = words == target
    peak = jnp.max(scores, axis=1, keepdims=True)
    raised = jnp.exp(scores - peak)
    total = jnp.sum(raised, axis=1, keepdims=True)
    hits = jnp.sum(jnp.where(matched, raised, 0.0), axis=1, keepdims=True)
    e_ref[...] = jnp.where(matched, raised, -raised)
    stat_lane = lax.broadcasted_iota(jnp.int32, (rows, 128), 1)
    stats = jnp.where(stat_lane == 0, peak, jnp.where(stat_lane == 1, total, hits))
    for part in range(parts):
        s_ref[part] = stats[part * piece : (part + 1) * piece, :].T[: s_ref.shape[1], :]


def picked_specs(shape, parts):
    return [
        spec((1,) + shape, functools.partial(lambda part, i, order: (order[i * parts + part], 0, 0), part))
        for part in range(parts)
    ]


def near_scores(queries, keys_turned, square, values, near, target_rows, order, parts, spacing):
    stat_rows, piece = target_rows.shape[1:]
    near_count = near.shape[2]
    slot_rows = queries.shape[0]
    width, keys = keys_turned.shape
    rows = parts * piece
    return pl.pallas_call(
        functools.partial(near_kernel, spacing, width ** (-0.5), parts),
        grid_spec=pltpu.PrefetchScalarGridSpec(
            num_scalar_prefetch=1,
            grid=(slot_rows // rows,),
            in_specs=[
                spec((rows, width), lambda i, order: (i, 0)),
                spec((width, keys), lambda i, order: (0, 0)),
                spec((spacing, near_count), lambda i, order: (0, 0)),
                spec((spacing, near_count), lambda i, order: (0, 0)),
            ]
            + picked_specs((piece, near_count), parts)
            + picked_specs((stat_rows, piece), parts),
            out_specs=[
                spec((rows, near_count), lambda i, order: (i, 0)),
                spec((parts, stat_rows, piece), lambda i, order: (i, 0, 0)),
            ],
        ),
        out_shape=[
            jax.ShapeDtypeStruct((slot_rows, near_count), jnp.float32),
            jax.ShapeDtypeStruct((slot_rows // piece, stat_rows, piece), jnp.float32),
        ],
        compiler_params=kernel_params(),
        cost_estimate=small_cost,
        name="near_scores",
    )(order, queries, keys_turned, square, values, *[near] * parts, *[target_rows] * parts)


def near_back_kernel(spacing, factor, parts, *refs):
    order_ref, e_ref = refs[:2]
    near_refs, coeff_refs = refs[2 : 2 + parts], refs[2 + parts : 2 + 2 * parts]
    keys_ref, out_ref, dense_ref = refs[2 + 2 * parts :]
    piece, near_count = near_refs[0].shape[1:]
    lane = lax.broadcasted_iota(jnp.int32, (piece, near_count), 1)
    for part in range(parts):
        rows = slice(part * piece, (part + 1) * piece)
        offset = near_refs[part][0] - spacing * lane
        columns = coeff_refs[part][0].T
        coefficient, probability = columns[:, 0:1], columns[:, 1:2]
        marked = e_ref[rows, :]
        matched = jnp.where(marked > 0.0, 1.0, 0.0)
        grads = coefficient * (matched - probability) * jnp.abs(marked) * factor
        for plane in range(spacing):
            lanes = slice(plane * near_count, (plane + 1) * near_count)
            dense_ref[rows, lanes] = jnp.where(offset == plane, grads, 0.0).astype(jnp.bfloat16)
    out_ref[...] = row_dot(dense_ref[...], keys_ref[...]).astype(out_ref.dtype)


def near_back(marked, near, coeff_rows, keys_planes, order, parts, spacing, after=()):
    stat_rows, piece = coeff_rows.shape[1:]
    slot_rows, near_count = marked.shape
    keys, width = keys_planes.shape
    rows = parts * piece
    return pl.pallas_call(
        later(
            functools.partial(near_back_kernel, spacing, 2.0 * width ** (-0.5), parts),
            3 + 2 * parts,
            len(after),
        ),
        grid_spec=pltpu.PrefetchScalarGridSpec(
            num_scalar_prefetch=1,
            grid=(slot_rows // rows,),
            in_specs=[spec((rows, near_count), lambda i, order: (i, 0))]
            + picked_specs((piece, near_count), parts)
            + picked_specs((stat_rows, piece), parts)
            + [spec((keys, width), lambda i, order: (0, 0))]
            + later_specs(after),
            out_specs=spec((rows, width), lambda i, order: (i, 0)),
            scratch_shapes=[pltpu.VMEM((rows, keys), jnp.bfloat16)],
        ),
        out_shape=jax.ShapeDtypeStruct((slot_rows, width), jnp.bfloat16),
        compiler_params=kernel_params(),
        cost_estimate=small_cost,
        name="near_back",
    )(order, marked, *[near] * parts, *[coeff_rows] * parts, keys_planes, *after)


def pack_kernel(options, pick_ref, *refs):
    row_refs, (map_ref, out_ref, chosen_ref) = refs[:options], refs[options:]
    owners, capacity = out_ref.shape[:2]
    tokens = map_ref.shape[1]

    @pl.when(pl.program_id(0) == 0)
    def _():
        slot = lax.broadcasted_iota(jnp.int32, (capacity, tokens), 0)
        for owner in range(owners):
            chosen = jnp.where(map_ref[owner : owner + 1, :] == slot, 1.0, 0.0)
            chosen_ref[owner * capacity : (owner + 1) * capacity, :] = chosen.astype(jnp.bfloat16)

    rows = row_refs[0][...]
    for place in range(1, options):
        rows = jnp.where(pick_ref[0] == place, row_refs[place][...], rows)
    packed = row_dot(chosen_ref[...], rows).astype(out_ref.dtype)
    out_ref[...] = packed.reshape(out_ref.shape)


def pack_rows(options, pick, slot_map, capacity, after=()):
    owners, tokens = slot_map.shape
    width = options[0].shape[1]
    columns = row_chunk(width, (256,))
    return pl.pallas_call(
        later(functools.partial(pack_kernel, len(options)), 2 + len(options), len(after)),
        grid_spec=pltpu.PrefetchScalarGridSpec(
            num_scalar_prefetch=1,
            grid=(width // columns,),
            in_specs=[
                *[spec((tokens, columns), lambda i, pick: (0, i))] * len(options),
                spec((owners, tokens), lambda i, pick: (0, 0)),
                *later_specs(after),
            ],
            out_specs=spec((owners, capacity, columns), lambda i, pick: (0, 0, i)),
            scratch_shapes=[pltpu.VMEM((owners * capacity, tokens), jnp.bfloat16)],
        ),
        out_shape=jax.ShapeDtypeStruct((owners, capacity, width), options[0].dtype),
        compiler_params=kernel_params(),
        cost_estimate=small_cost,
        name="pack_rows",
    )(pick, *options, slot_map, *after)


def unpack_kernel(back_ref, column_ref, out_ref, chosen_ref):
    owners, capacity, columns = back_ref.shape
    tokens = out_ref.shape[0]

    @pl.when(pl.program_id(0) == 0)
    def _():
        slot = lax.broadcasted_iota(jnp.int32, (capacity, tokens), 0)
        for owner in range(owners):
            chosen = jnp.where(column_ref[owner : owner + 1, :] == slot, 1.0, 0.0)
            chosen_ref[owner * capacity : (owner + 1) * capacity, :] = chosen.astype(jnp.bfloat16)

    back = back_ref[...].reshape(owners * capacity, columns)
    out_ref[...] = left_dot(chosen_ref[...], back).astype(out_ref.dtype)


def unpack_rows(returned, slot_map, kind, after=()):
    owners, capacity, width = returned.shape
    tokens = slot_map.shape[1]
    columns = row_chunk(width, (256,))
    return pl.pallas_call(
        later(unpack_kernel, 2, len(after)),
        grid=(width // columns,),
        in_specs=[
            spec((owners, capacity, columns), lambda i: (0, 0, i)),
            spec((owners, tokens), lambda i: (0, 0)),
            *later_specs(after),
        ],
        out_specs=spec((tokens, columns), lambda i: (0, i)),
        out_shape=jax.ShapeDtypeStruct((tokens, width), kind),
        scratch_shapes=[pltpu.VMEM((owners * capacity, tokens), jnp.bfloat16)],
        compiler_params=kernel_params(),
        cost_estimate=small_cost,
        name="unpack_rows",
    )(returned, slot_map, *after)


def mix_kernel(stats_ref, map_ref, prob_ref, loss_ref, send_ref, peak_ref, total_ref, hits_ref):
    owners, stat_rows, capacity = stats_ref.shape
    tokens = map_ref.shape[1]
    slot = lax.broadcasted_iota(jnp.int32, (capacity, tokens), 0)
    for owner in range(owners):
        chosen = map_ref[owner : owner + 1, :] == slot
        columns = stats_ref[owner].T
        for place, target in enumerate((peak_ref, total_ref, hits_ref)):
            target[owner : owner + 1, :] = jnp.sum(
                jnp.where(chosen, columns[:, place : place + 1], 0.0), axis=0, keepdims=True
            )
    member = map_ref[...] >= 0
    peaks = jnp.where(member, peak_ref[...], -3e38)
    best = jnp.max(peaks, axis=0, keepdims=True)
    rescale = jnp.where(member, jnp.exp(peaks - best), 0.0)
    knn_total = jnp.sum(total_ref[...] * rescale, axis=0, keepdims=True)
    knn_prob = jnp.sum(hits_ref[...] * rescale, axis=0, keepdims=True) / knn_total
    mixture = mix_weight * knn_prob + (1.0 - mix_weight) * prob_ref[...]
    loss_ref[...] = -jnp.log(mixture)
    peak_ref[...] = (-mix_weight / (mixture * knn_total)) * rescale
    for owner in range(owners):
        chosen = map_ref[owner : owner + 1, :] == slot
        coefficient = jnp.sum(
            jnp.where(chosen, peak_ref[owner : owner + 1, :], 0.0), axis=1, keepdims=True
        )
        probability = jnp.sum(jnp.where(chosen, knn_prob, 0.0), axis=1, keepdims=True)
        lane = lax.broadcasted_iota(jnp.int32, (capacity, 128), 1)
        both = jnp.where(lane == 0, coefficient, probability)
        send_ref[owner] = both.T[:stat_rows, :]


def mix_losses(stats, slot_map, model_prob):
    owners, stat_rows, capacity = stats.shape
    tokens = slot_map.shape[1]
    vmem = pl.BlockSpec(memory_space=pltpu.VMEM)
    return pl.pallas_call(
        mix_kernel,
        in_specs=[vmem] * 3,
        out_specs=[vmem] * 2,
        out_shape=[
            jax.ShapeDtypeStruct((1, tokens), jnp.float32),
            jax.ShapeDtypeStruct(stats.shape, jnp.float32),
        ],
        scratch_shapes=[pltpu.VMEM((owners, tokens), jnp.float32)] * 3,
        compiler_params=pltpu.CompilerParams(vmem_limit_bytes=vmem_limit),
        name="mix_losses",
    )(stats, slot_map, model_prob)


def row_chunk(total, choices):
    for choice in choices:
        if total % choice == 0:
            return choice
    return total


def slot_picker(slot_map, capacity):
    return slot_map[:, None, :] == jnp.arange(capacity, dtype=jnp.int32)[None, :, None]


def layer_table(count):
    return [
        sorted(range(count), key=lambda other: (abs(other - layer), (other ^ layer) != 1, other))
        for layer in range(count)
    ]


def own_choice(options):
    layer = lax.axis_index("batch")
    kept = options[0]
    for place in range(1, len(options)):
        if all(options[place] is not other for other in options[:place]):
            same = [i for i, other in enumerate(options) if other is options[place]]
            here = functools.reduce(jnp.logical_or, [layer == i for i in same])
            kept = jnp.where(here, options[place], kept)
    return kept


def layer_step(step, ups, downs):
    options, picks = [], []
    for layer, line in enumerate(layer_table(lax.axis_size("batch"))):
        there = line[step]
        block = ups[layer - there] if there < layer else downs[there - layer]
        places = [place for place, other in enumerate(options) if other is block]
        if not places:
            options.append(block)
        picks.append(places[0] if places else len(options) - 1)
    return options, jnp.array(picks, jnp.int32)[lax.axis_index("batch")][None]


def layer_hop(hop, blocks, above, below):
    count = lax.axis_size("batch")
    reach = count - hop
    table = layer_table(count)

    def bound(layer, to):
        return blocks[table[layer].index(to) if 0 <= to < count else hop_step]

    hop_step = reach
    up = own_choice([bound(layer, layer + reach) for layer in range(count)])
    down = own_choice([bound(layer, layer - reach) for layer in range(count)])
    if hop > 1:
        up = (up.astype(jnp.float32) + above).astype(up.dtype)
        down = (down.astype(jnp.float32) + below).astype(down.dtype)
    return (
        lax.ppermute(up, "batch", [(i, i + 1) for i in range(hop)]),
        lax.ppermute(down, "batch", [(i, i - 1) for i in range(reach, count)]),
    )


def across(rows, step):
    return lax.ppermute(rows, "ctx", [(i, i ^ step) for i in range(lax.axis_size("ctx"))])


def in_ctx_order(parts):
    count = len(parts)
    own = lax.axis_index("ctx")
    stacked = jnp.stack(parts)
    return stacked[jnp.arange(count, dtype=jnp.int32) ^ own]


def ctx_gather(rows):
    return in_ctx_order([rows] + [across(rows, step) for step in range(1, lax.axis_size("ctx"))])


def swap_cores(rows):
    return lax.ppermute(rows, "rep", [(0, 1), (1, 0)])


def reduce_cores(grad):
    count = lax.axis_size("ctx")
    parts = grad.astype(jnp.bfloat16).reshape(count, 2, grad.shape[0] // (2 * count), grad.shape[1])
    core = lax.axis_index("rep")
    keep = lax.dynamic_index_in_dim(parts, core, 1, keepdims=False)
    send = lax.dynamic_index_in_dim(parts, 1 - core, 1, keepdims=False)
    return (keep.astype(jnp.float32) + swap_cores(send)).astype(jnp.bfloat16)


def ctx_trade(blocks):
    return [part if step == 0 else across(part, step) for step, part in enumerate(blocks)]


def exchange(blocks, axis):
    return lax.all_to_all(blocks, axis, split_axis=0, concat_axis=0, tiled=True)


def block_sum(blocks):
    total = blocks[0].astype(jnp.float32)
    for place in range(1, len(blocks)):
        total = total + blocks[place].astype(jnp.float32)
    return total


def ctx_reduce(halves):
    return lax.psum_scatter(halves, "ctx", scatter_dimension=0)


def layer_total(blocks):
    return block_sum(exchange(blocks, "batch")).astype(jnp.bfloat16)


def layer_blocks(rows):
    return rows.reshape(lax.axis_size("batch"), -1, rows.shape[1])


def both_halves(half):
    other = swap_cores(half)
    first = lax.axis_index("rep") == 0
    both = jnp.stack([jnp.where(first, half, other), jnp.where(first, other, half)])
    return both.reshape(-1, half.shape[-1]).astype(jnp.float32)


def shard_gather(rows):
    return both_halves(lax.all_gather(rows, "batch"))


def layer_gather(rows):
    count, layer = lax.axis_size("batch"), lax.axis_index("batch")
    parts = [rows] + [
        lax.ppermute(rows, "batch", [(i, (i + hops) % count) for i in range(count)])
        for hops in range(1, count)
    ]
    return both_halves(jnp.stack(parts)[(layer - jnp.arange(count, dtype=jnp.int32)) % count])


def mix_any(stats, slot_map, model_prob):
    owners, stat_rows, capacity = stats.shape
    if capacity % 16 == 0:
        return mix_losses(stats, slot_map, model_prob)
    chosen = slot_picker(slot_map, capacity)
    peak, total, hits = [
        jnp.sum(jnp.where(chosen, stats[:, row, :, None], 0.0), axis=1) for row in range(3)
    ]
    member = slot_map >= 0
    peaks = jnp.where(member, peak, -3e38)
    best = jnp.max(peaks, axis=0, keepdims=True)
    rescale = jnp.where(member, jnp.exp(peaks - best), 0.0)
    knn_total = jnp.sum(total * rescale, axis=0, keepdims=True)
    knn_prob = jnp.sum(hits * rescale, axis=0, keepdims=True) / knn_total
    mixture = mix_weight * knn_prob + (1.0 - mix_weight) * model_prob
    coefficient = (-mix_weight / (mixture * knn_total)) * rescale
    sent = [
        jnp.sum(jnp.where(chosen, part[:, None, :], 0.0), axis=2)
        for part in (coefficient, jnp.broadcast_to(knn_prob, coefficient.shape))
    ]
    sent = jnp.stack(sent + [sent[1]] * (stat_rows - 2), axis=1)
    return -jnp.log(mixture), sent


def local(
    tokens,
    cotangent,
    segment_ids,
    first_gain,
    first_shift,
    second_gain,
    second_shift,
    final_gain,
    final_shift,
    project_weight,
    output_weight,
    upward_weight,
    downward_weight,
    store_keys,
    store_values,
    owners,
    neighbours,
    targets,
    model_prob,
):
    head_count = HEADS
    group_seqs, block_len, width = tokens.shape
    seq_len = segment_ids.shape[1]
    ctx_count = lax.axis_size("ctx")
    shard_count = lax.axis_size("batch") * ctx_count
    capacity = neighbours.shape[3]
    near_count = neighbours.shape[4]
    top_count = owners.shape[2]
    key_count = store_keys.shape[0]
    spacing = key_count // near_count
    slot_rows = shard_count * capacity
    everyone = ("batch", "ctx")
    own_heads = head_count // ctx_count
    own_width = width // ctx_count
    attend_size = row_chunk(seq_len, (256, 128))

    arrived = [tokens[0]] + [across(tokens[0], step) for step in range(1, ctx_count)]
    own_rows = project_weight.shape[0]
    own_ctx = lax.axis_index("ctx")
    vectors = jnp.stack(
        [first_gain, first_shift, second_gain, second_shift, final_gain, final_shift], axis=1
    )
    vectors = jnp.pad(vectors, ((0, 0), (0, 128 - vectors.shape[1])))
    proj_pieces = [
        jnp.concatenate(
            [
                lax.dynamic_slice_in_dim(
                    project_weight, part * width + (own_ctx ^ step) * own_width, own_width, 1
                )
                for part in range(3)
            ]
            + [vectors],
            axis=1,
        )
        for step in range(ctx_count)
    ]
    proj_pieces = ctx_trade(proj_pieces)
    vectors = in_ctx_order([piece[:, 3 * own_width :] for piece in proj_pieces])
    vectors = vectors.reshape(width, -1)[:, :6].T.astype(jnp.float32)
    gain_list = [vectors[row] for row in range(6)]

    member = jnp.any(
        owners[0][:, :, None] == jnp.arange(shard_count, dtype=jnp.int32)[None, None, :], axis=1
    )
    place = jnp.arange(block_len, dtype=jnp.int32)
    earlier = (place[:, None] <= place[None, :]).astype(jnp.bfloat16)
    running = left_dot(member.astype(jnp.bfloat16), earlier).astype(jnp.int32)
    slot_map = jnp.where(member.T, running - 1, -1)
    send_targets = jnp.sum(
        jnp.where(slot_picker(slot_map, capacity), targets.reshape(1, 1, -1), 0), axis=2
    )
    got_targets = exchange(send_targets.astype(jnp.int32), everyone).astype(jnp.float32)
    planes = store_keys.reshape(near_count, spacing, width).transpose(1, 0, 2)
    planes = planes.reshape(key_count, width)
    planes_turned = planes.T
    key_square = jnp.sum(jnp.square(store_keys.astype(jnp.float32)), axis=1)
    key_square = key_square.reshape(near_count, spacing).T
    value_planes = store_values.astype(jnp.float32).reshape(near_count, spacing).T
    by_layer = capacity % 16 == 0
    if by_layer:
        piece, parts = capacity, 2 if ctx_count % 2 == 0 else 1
        layer_count = lax.axis_size("batch")
        maps = exchange(slot_map.reshape(layer_count, ctx_count, block_len), "batch")
        table = jnp.array(layer_table(layer_count), jnp.int32)[lax.axis_index("batch")]
        maps = maps[table]
        orders = table[:, None] * ctx_count + jnp.arange(ctx_count, dtype=jnp.int32)[None, :]
    else:
        piece, parts = row_chunk(slot_rows, (576, 512, 384, 256, 128)), 1
        orders = jnp.arange(slot_rows // piece, dtype=jnp.int32)[None, :]
        chosen_slots = slot_picker(slot_map, capacity).astype(jnp.bfloat16)
    near_table = neighbours.reshape(slot_rows // piece, piece, near_count)
    stat_shape = (slot_rows // piece, 8, piece)
    target_rows = jnp.broadcast_to(got_targets.reshape(stat_shape[0], 1, piece), stat_shape)

    early = proj_pieces[1:]
    core = lax.axis_index("rep")

    def own_half(weight):
        half = weight.shape[0] // 2
        mine = lax.dynamic_slice_in_dim(weight, core * half, half, 0)
        return run_after([mine], [*arrived[1:], *early])[0]

    def gather_weight(weight):
        return lax.all_gather(own_half(weight), ("ctx", "rep"), axis=0, tiled=True)

    out_full = gather_weight(output_weight)
    down_full = gather_weight(downward_weight)
    up_half = own_half(upward_weight)
    up_pieces = [across(up_half, step) for step in range(1, ctx_count)]
    sources = own_ctx ^ jnp.arange(ctx_count, dtype=jnp.int32)

    segments = segment_ids[0]
    start_rows = jnp.sum((segments[None, :] < segments[:, None]).astype(jnp.int32), axis=1)
    low_blocks = start_rows[::attend_size] // attend_size
    start_rows = jnp.broadcast_to(start_rows[None, :], (8, seq_len))
    proj_own, plain_full, normed_full, query_own, key_own, value_own = project_rows(
        arrived, proj_pieces, sources, vectors
    )
    attended_own, log_total = attend(
        query_own, key_own, value_own, start_rows, low_blocks, own_heads, attend_size
    )
    attended = lax.all_to_all(attended_own, "ctx", split_axis=0, concat_axis=1, tiled=True)
    attended = run_after([attended], [target_rows, maps] if by_layer else [target_rows])[0]
    up_pieces = [up_half, *run_after(up_pieces, [attended])]
    up_full = place_rows(
        up_pieces + [swap_cores(piece) for piece in up_pieces],
        jnp.concatenate([2 * sources + core, 2 * sources + 1 - core]),
    )
    inputs = tokens[0].astype(jnp.float32)
    hidden = inputs + row_dot(attended, out_full)
    normed_two = norm_rows(hidden, gain_list[2], gain_list[3]).astype(jnp.bfloat16)
    upper_rows = row_dot(normed_two, up_full)
    active = jax.nn.gelu(upper_rows).astype(jnp.bfloat16)
    summed = hidden + row_dot(active, down_full)
    final_rows = norm_rows(summed, gain_list[4], gain_list[5]).astype(jnp.bfloat16)

    if by_layer:
        ups, downs, packed, queries = [final_rows], [final_rows], [], []
        for step in range(layer_count):
            hop = step + 1
            if hop < layer_count:
                up, down = ups[-1], downs[-1]
                if hop == 2:
                    up, down = run_after([up, down], packed)
                    ups[-1], downs[-1] = up, down
                elif hop > 2:
                    up, down = run_after([up, down], [queries[hop - 3]])
                    ups[-1], downs[-1] = up, down
                ups.append(
                    lax.ppermute(up, "batch", [(i, i + 1) for i in range(step, layer_count - 1)])
                )
                downs.append(
                    lax.ppermute(down, "batch", [(i, i - 1) for i in range(1, layer_count - step)])
                )
            options, pick = layer_step(step, ups, downs)
            between = (planes, planes_turned, key_square) if step == 1 else ()
            packed.append(pack_rows(options, pick, maps[step], capacity, between))
            queries.append(exchange(packed[step], "ctx").reshape(-1, width))
    else:
        packed = jnp.einsum(
            "ost,tw->osw", chosen_slots, final_rows, preferred_element_type=jnp.float32
        )
        queries = [exchange(packed.astype(jnp.bfloat16), everyone).reshape(slot_rows, width)]
    marked, stats = zip(
        *[
            near_scores(
                rows,
                planes_turned,
                key_square,
                value_planes,
                near_table,
                target_rows,
                orders[step],
                parts,
                spacing,
            )
            for step, rows in enumerate(queries)
        ]
    )
    if by_layer:
        inverse = jnp.argmin(
            jnp.abs(table[None, :] - jnp.arange(layer_count, dtype=jnp.int32)[:, None]), axis=1
        )
        stats = jnp.stack(stats)[inverse].reshape(stat_shape)
    else:
        stats = stats[0].transpose(1, 0, 2).reshape(8, shard_count, capacity).transpose(1, 0, 2)
    token_loss, send_coeff = mix_any(exchange(stats, everyone), slot_map, model_prob)
    got_coeff = exchange(send_coeff, everyone)
    if not by_layer:
        got_coeff = got_coeff.transpose(1, 0, 2).reshape(8, -1, piece).transpose(1, 0, 2)
    if by_layer:
        returned, above, below = {}, None, None
        for step in reversed(range(layer_count)):
            hop = layer_count - 1 - step
            partial_grad = near_back(
                marked[step],
                near_table,
                got_coeff,
                planes,
                orders[step],
                parts,
                spacing,
                [returned[step + 2]] if hop >= 2 else [],
            )
            back = exchange(partial_grad.reshape(ctx_count, capacity, width), "ctx")
            if hop > 0:
                above, below = layer_hop(hop, returned, above, below)
            returned[step] = unpack_rows(
                back,
                maps[step],
                jnp.bfloat16 if step > 0 else jnp.float32,
                [above, below] if hop > 0 else [],
            )
        query_grad = returned[0] + above.astype(jnp.float32) + below.astype(jnp.float32)
    else:
        partial_grad = near_back(
            marked[0], near_table, got_coeff, planes, orders[0], parts, spacing
        )
        back = exchange(partial_grad.reshape(shard_count, capacity, width), everyone)
        query_grad = jnp.einsum(
            "ost,osw->tw", chosen_slots, back, preferred_element_type=jnp.float32
        )

    out_grad = cotangent[0].astype(jnp.float32) + query_grad
    final_vjp = jax.vjp(norm_rows, summed, gain_list[4], gain_list[5])[1]
    summed_grad, final_gain_grad, final_shift_grad = final_vjp(out_grad)
    branch_grad = summed_grad.astype(jnp.bfloat16)
    downward_grad = left_dot(active, branch_grad)
    active_grad = right_dot(branch_grad, down_full)
    gelu_vjp = jax.vjp(jax.nn.gelu, upper_rows)[1]
    upper_grad = gelu_vjp(active_grad)[0].astype(jnp.bfloat16)
    downward_half = reduce_cores(downward_grad)
    upper_grad = run_after([upper_grad], [downward_half])[0]
    second_vjp = jax.vjp(norm_rows, hidden, gain_list[2], gain_list[3])[1]
    hidden_part, second_gain_grad, second_shift_grad = second_vjp(right_dot(upper_grad, up_full))
    hidden_grad = summed_grad + hidden_part
    attn_grad = hidden_grad.astype(jnp.bfloat16)
    attended_grad = right_dot(attn_grad, out_full).astype(jnp.bfloat16)
    downward_half = ctx_reduce(downward_half)
    second_half = reduce_cores(
        jnp.concatenate(
            [
                left_dot(normed_two, upper_grad).astype(jnp.bfloat16),
                left_dot(attended, attn_grad).astype(jnp.bfloat16),
            ],
            axis=1,
        )
    )
    attended_grad = run_after([attended_grad], [downward_half])[0]
    grad_own = lax.all_to_all(attended_grad, "ctx", split_axis=1, concat_axis=0, tiled=True)
    second_half = run_after([second_half], [grad_own])[0]
    downward_half = run_after([downward_half], [second_half])[0]
    downward_total = layer_total(layer_blocks(downward_half))
    proj_grad = jnp.concatenate(
        run_after(
            attend_back(
                query_own,
                key_own,
                value_own,
                grad_own,
                attended_own,
                log_total,
                start_rows,
                low_blocks,
                own_heads,
                attend_size,
                (second_half, downward_half),
            ),
            [downward_total],
        ),
        axis=1,
    )
    plain_part = left_dot(plain_full, proj_grad)
    column_sums = jnp.sum(proj_grad.astype(jnp.float32), axis=0)
    proj_full = proj_own.astype(jnp.float32)
    first_gain_grad = jnp.sum(plain_part * proj_full, axis=1)
    first_shift_grad = jnp.sum(column_sums[None, :] * proj_full, axis=1)
    project_part = plain_part * gain_list[0][:, None] + column_sums[None, :] * gain_list[1][:, None]

    vector_part = jnp.stack(
        [
            first_gain_grad,
            first_shift_grad,
            second_gain_grad,
            second_shift_grad,
            final_gain_grad,
            final_shift_grad,
        ],
        axis=1,
    )
    vector_part = jnp.pad(vector_part, ((0, 0), (0, 128 - vector_part.shape[1])))
    project_part = jnp.concatenate([project_part, vector_part], axis=1)
    project_part = reduce_cores(project_part)
    normed_terms = right_dot(proj_grad, run_after([proj_own], [project_part])[0])
    term_blocks = normed_terms.astype(jnp.bfloat16).reshape(ctx_count, block_len, width)
    term_parts = ctx_trade(
        [
            lax.dynamic_index_in_dim(term_blocks, own_ctx ^ step, 0, keepdims=False)
            for step in range(ctx_count)
        ]
    )
    project_part = exchange(project_part, "ctx")
    second_part = run_after([ctx_reduce(second_half)], [project_part])[0]
    second_total = layer_total(layer_blocks(second_part))
    vector_part = block_sum(project_part[:, :, 3 * own_width :]).astype(jnp.bfloat16)
    project_part = (
        project_part[:, :, : 3 * own_width]
        .reshape(ctx_count, own_rows // 2, 3, own_width)
        .transpose(1, 2, 0, 3)
        .reshape(own_rows // 2, 3 * width)
    )
    small_rows = jnp.concatenate([project_part, vector_part], axis=1)
    term_parts = [term_parts[0], *run_after(term_parts[1:], [second_total])]
    small_rows = run_after([small_rows], [second_total])[0]
    small_total = layer_total(layer_blocks(small_rows))
    small_total = run_after([small_total], term_parts[1:])[0]
    input_vjp = jax.vjp(lambda rows: norm_rows(rows, gain_list[0], gain_list[1]), inputs)[1]
    input_grad = hidden_grad + input_vjp(block_sum(term_parts))[0]
    small_grads = layer_gather(small_total)
    second_grads = shard_gather(second_total)
    weight_grads = [
        small_grads[:, : 3 * width],
        second_grads[:, second_grads.shape[1] - width :],
        second_grads[:, : second_grads.shape[1] - width],
        both_halves(
            run_after([lax.all_gather(downward_total, "batch")], [small_total])[0]
        ),
    ]
    vector_grads = small_grads[:, 3 * width : 3 * width + 6].T
    return (
        final_rows.reshape(group_seqs, block_len, width),
        token_loss.reshape(group_seqs, block_len),
        query_grad.reshape(group_seqs, block_len, width),
        input_grad.reshape(group_seqs, block_len, width),
        *weight_grads,
        *[vector_grads[row] for row in range(6)],
    )


def solution(mesh):
    placed = (
        P(("rep", "batch"), "ctx", None),
        P(("rep", "batch"), "ctx", None),
        P(("rep", "batch"), None),
        P("ctx"),
        P("ctx"),
        P("ctx"),
        P("ctx"),
        P("ctx"),
        P("ctx"),
        P("ctx", None),
        P("ctx", None),
        P("ctx", None),
        P("ctx", None),
        P(("batch", "ctx"), None),
        P(("batch", "ctx")),
        P(("rep", "batch"), "ctx", None),
        P("rep", ("batch", "ctx"), None, None, None),
        P(("rep", "batch"), "ctx"),
        P(("rep", "batch"), "ctx"),
    )
    return jax.shard_map(
        local,
        mesh=mesh,
        in_specs=placed,
        out_specs=(
            P(("rep", "batch"), "ctx", None),
            P(("rep", "batch"), "ctx"),
            P(("rep", "batch"), "ctx", None),
            P(("rep", "batch"), "ctx", None),
            P("ctx", None),
            P("ctx", None),
            P("ctx", None),
            P("ctx", None),
            P("ctx"),
            P("ctx"),
            P("ctx"),
            P("ctx"),
            P("ctx"),
            P("ctx"),
        ),
        check_vma=False,
    )
```

```python
import functools

import jax
import jax.numpy as jnp
from jax import lax
from jax.experimental import pallas as pl
from jax.experimental.pallas import tpu as pltpu
from jax.sharding import PartitionSpec as P

HEADS = 16


norm_eps = 1e-05
mix_weight = 0.25
masked_value = -1e30
vmem_limit = 60 * 1024 * 1024
small_cost = pl.CostEstimate(flops=1000, bytes_accessed=1000, transcendentals=0)


def norm_rows(values, scale_gain, shift_term):
    average = jnp.mean(values, axis=-1, keepdims=True)
    centred = values - average
    spread = jnp.mean(centred * centred, axis=-1, keepdims=True)
    return centred * lax.rsqrt(spread + norm_eps) * scale_gain + shift_term


def row_dot(left_side, right_side):
    return jnp.dot(left_side, right_side, preferred_element_type=jnp.float32)


def left_dot(left_side, right_side):
    return lax.dot_general(
        left_side, right_side, (((0,), (0,)), ((), ())), preferred_element_type=jnp.float32
    )


def right_dot(left_side, right_side):
    return lax.dot_general(
        left_side, right_side, (((1,), (1,)), ((), ())), preferred_element_type=jnp.float32
    )


def spec(shape, index_map):
    return pl.BlockSpec(shape, index_map)


def kernel_params(dims=1):
    return pltpu.CompilerParams(
        vmem_limit_bytes=vmem_limit, dimension_semantics=("arbitrary",) * dims
    )


def later(kernel, place, count):
    return lambda *refs: kernel(*refs[:place], *refs[place + count :])


def later_specs(after):
    return [pl.BlockSpec(memory_space=pl.ANY)] * len(after)


def run_after(arrays, after):
    def kernel(*refs):
        pass

    return pl.pallas_call(
        kernel,
        in_specs=later_specs((*arrays, *after)),
        out_specs=later_specs(arrays),
        out_shape=[jax.ShapeDtypeStruct(rows.shape, rows.dtype) for rows in arrays],
        input_output_aliases={place: place for place in range(len(arrays))},
        cost_estimate=small_cost,
        name="run_after",
    )(*arrays, *after)


def place_kernel(count, start_ref, *refs):
    for place in range(count):

        @pl.when(pl.program_id(0) == place)
        def _():
            refs[count][...] = refs[place][...]


def place_rows(pieces, places):
    count = len(pieces)
    rows, width = pieces[0].shape
    return pl.pallas_call(
        functools.partial(place_kernel, count),
        grid_spec=pltpu.PrefetchScalarGridSpec(
            num_scalar_prefetch=1,
            grid=(count,),
            in_specs=[spec((rows, width), lambda i, places: (0, 0))] * count,
            out_specs=spec((rows, width), lambda i, places: (places[i], 0)),
        ),
        out_shape=jax.ShapeDtypeStruct((count * rows, width), pieces[0].dtype),
        compiler_params=kernel_params(),
        cost_estimate=small_cost,
        name="place_rows",
    )(places, *pieces)


def head_rows(head, size):
    return slice(head * size, (head + 1) * size)


def masked_heads(block, head_count, axis):
    size = block.shape[axis] // head_count
    index = lax.broadcasted_iota(jnp.int32, block.shape, axis) // size
    zero = jnp.zeros((), block.dtype)
    return [jnp.where(index == head, block, zero) for head in range(head_count)]


def block_mask(key_block, query_block, size, start_row):
    key_pos = key_block * size + lax.broadcasted_iota(jnp.int32, (size, size), 0)
    query_pos = query_block * size + lax.broadcasted_iota(jnp.int32, (size, size), 1)
    return (key_pos <= query_pos) & (key_pos >= start_row)


def attend_kernel(
    head_count, low_ref, q_ref, k_ref, v_ref, start_ref, o_ref, lse_ref, vt_ref, acc_ref
):
    step = pl.program_id(0)
    size, width = q_ref.shape
    head_size = width // head_count
    blocks = k_ref.shape[0] // size

    @pl.when(step == 0)
    def _():
        for block in range(blocks):
            rows = slice(block * size, (block + 1) * size)
            vt_ref[:, rows] = v_ref[rows, :].astype(jnp.float32).T.astype(jnp.bfloat16)

    scaled = q_ref[...].astype(jnp.float32) * (head_size ** (-0.5))
    turned = jnp.concatenate(
        [part.astype(jnp.bfloat16) for part in masked_heads(scaled.T, head_count, 0)], axis=1
    )
    start_row = start_ref[0:1, :]
    acc_ref[...] = jnp.zeros_like(acc_ref)
    first = (
        jnp.full((1, head_count * size), masked_value, jnp.float32),
        jnp.zeros((1, head_count * size), jnp.float32),
    )

    def body(masked, block, state):
        peak, total = state
        rows = pl.ds(pl.multiple_of(block * size, size), size)
        scores = row_dot(k_ref[rows, :], turned)
        if masked:
            allowed = block_mask(block, step, size, start_row)
            scores = jnp.concatenate(
                [
                    jnp.where(allowed, scores[:, head * size : (head + 1) * size], masked_value)
                    for head in range(head_count)
                ],
                axis=1,
            )
        new_peak = jnp.maximum(peak, jnp.max(scores, axis=0, keepdims=True))
        fade = jnp.exp(peak - new_peak)
        weights = jnp.exp(scores - new_peak)
        total = total * fade + jnp.sum(weights, axis=0, keepdims=True)
        weights = weights.astype(jnp.bfloat16)
        for head in range(head_count):
            part = head_rows(head, head_size)
            lanes = slice(head * size, (head + 1) * size)
            acc_ref[part, :] = acc_ref[part, :] * fade[:, lanes] + row_dot(
                vt_ref[part, rows], weights[:, lanes]
            )
        return new_peak, total

    low = low_ref[step]
    inner = low_ref[blocks + step]
    state = lax.fori_loop(low, inner, functools.partial(body, True), first)
    state = lax.fori_loop(inner, step, functools.partial(body, False), state)
    peak, total = body(True, step, state)
    for head in range(head_count):
        part = head_rows(head, head_size)
        lanes = slice(head * size, (head + 1) * size)
        acc_ref[part, :] = acc_ref[part, :] / total[:, lanes]
        lse_ref[head : head + 1, :] = peak[:, lanes] + jnp.log(total[:, lanes])
    o_ref[...] = acc_ref[...].T.astype(jnp.bfloat16)


def with_inner(low_blocks, start_rows, size):
    last = start_rows[0, size - 1 :: size]
    inner = jnp.minimum(-(-last // size), jnp.arange(low_blocks.shape[0], dtype=jnp.int32))
    return jnp.concatenate([low_blocks, inner])


def attend(query, key, value, start_rows, low_blocks, head_count, size, after=()):
    length, width = query.shape
    blocks = length // size
    stat_rows = -(-head_count // 8) * 8
    return pl.pallas_call(
        later(functools.partial(attend_kernel, head_count), 5, len(after)),
        grid_spec=pltpu.PrefetchScalarGridSpec(
            num_scalar_prefetch=1,
            grid=(blocks,),
            in_specs=[
                spec((size, width), lambda i, low: (i, 0)),
                spec((length, width), lambda i, low: (0, 0)),
                spec((length, width), lambda i, low: (0, 0)),
                spec((8, size), lambda i, low: (0, i)),
                *later_specs(after),
            ],
            out_specs=[
                spec((size, width), lambda i, low: (i, 0)),
                spec((stat_rows, size), lambda i, low: (0, i)),
            ],
            scratch_shapes=[
                pltpu.VMEM((width, length), jnp.bfloat16),
                pltpu.VMEM((width, size), jnp.float32),
            ],
        ),
        out_shape=[
            jax.ShapeDtypeStruct((length, width), jnp.bfloat16),
            jax.ShapeDtypeStruct((stat_rows, length), jnp.float32),
        ],
        compiler_params=kernel_params(),
        cost_estimate=pl.CostEstimate(
            flops=20_000_000_000, bytes_accessed=1000, transcendentals=0
        ),
        name="attend",
    )(with_inner(low_blocks, start_rows, size), query, key, value, start_rows, *after)


def attend_back_kernel(
    head_count,
    low_ref,
    q_ref,
    k_ref,
    v_ref,
    grad_ref,
    o_ref,
    lse_ref,
    start_ref,
    dq_ref,
    dk_ref,
    dv_ref,
    kt_ref,
    dkey_ref,
    dvalue_ref,
    dqt_ref,
    score_ref,
    weight_ref,
):
    step = pl.program_id(0)
    size, width = q_ref.shape
    head_size = width // head_count
    score_scale = head_size ** (-0.5)
    blocks = k_ref.shape[0] // size

    @pl.when(step == 0)
    def _():
        dkey_ref[...] = jnp.zeros_like(dkey_ref)
        dvalue_ref[...] = jnp.zeros_like(dvalue_ref)
        for block in range(blocks):
            rows = slice(block * size, (block + 1) * size)
            kt_ref[:, rows] = k_ref[rows, :].astype(jnp.float32).T.astype(jnp.bfloat16)

    scaled = q_ref[...].astype(jnp.float32) * score_scale
    grads = grad_ref[...].astype(jnp.float32)
    dots = (grads * o_ref[...].astype(jnp.float32)).T
    query_turned = [p.astype(jnp.bfloat16) for p in masked_heads(scaled.T, head_count, 0)]
    grad_turned = [p.astype(jnp.bfloat16) for p in masked_heads(grads.T, head_count, 0)]
    query_stack = jnp.concatenate(
        [p.astype(jnp.bfloat16) for p in masked_heads(scaled, head_count, 1)], axis=0
    )
    grad_stack = jnp.concatenate(
        [p.astype(jnp.bfloat16) for p in masked_heads(grads, head_count, 1)], axis=0
    )
    row_dots = [
        jnp.sum(dots[head_rows(head, head_size), :], axis=0, keepdims=True)
        for head in range(head_count)
    ]
    start_row = start_ref[0:1, :]
    dqt_ref[...] = jnp.zeros_like(dqt_ref)

    query_wide = jnp.concatenate(query_turned, axis=1)
    grad_wide = jnp.concatenate(grad_turned, axis=1)
    row_wide = jnp.concatenate(row_dots, axis=1)
    lse_wide = jnp.concatenate([lse_ref[head : head + 1, :] for head in range(head_count)], axis=1)

    def body(masked, block, carry):
        rows = pl.ds(pl.multiple_of(block * size, size), size)
        scores = row_dot(k_ref[rows, :], query_wide)
        if masked:
            allowed = block_mask(block, step, size, start_row)
            scores = jnp.concatenate(
                [
                    jnp.where(allowed, scores[:, head * size : (head + 1) * size], masked_value)
                    for head in range(head_count)
                ],
                axis=1,
            )
        weights = jnp.exp(scores - lse_wide)
        weight_grad = row_dot(v_ref[rows, :], grad_wide)
        score_grad = (weights * (weight_grad - row_wide)).astype(jnp.bfloat16)
        weights = weights.astype(jnp.bfloat16)
        for head in range(head_count):
            part = head_rows(head, head_size)
            lanes = slice(head * size, (head + 1) * size)
            dqt_ref[part, :] += row_dot(kt_ref[part, rows], score_grad[:, lanes])
        dkey_ref[rows, :] += row_dot(score_grad, query_stack)
        dvalue_ref[rows, :] += row_dot(weights, grad_stack)
        return carry

    low = low_ref[step]
    inner = low_ref[blocks + step]
    lax.fori_loop(low, inner, functools.partial(body, True), 0)
    lax.fori_loop(inner, step, functools.partial(body, False), 0)
    body(True, step, 0)
    dq_ref[...] = (dqt_ref[...] * score_scale).T.astype(jnp.bfloat16)

    @pl.when(step == blocks - 1)
    def _():
        dk_ref[...] = dkey_ref[...].astype(jnp.bfloat16)
        dv_ref[...] = dvalue_ref[...].astype(jnp.bfloat16)


def attend_back(
    query, key, value, grad, attended, lse, start_rows, low_blocks, head_count, size, after=()
):
    length, width = query.shape
    blocks = length // size
    stat_rows = lse.shape[0]
    block_spec = spec((size, width), lambda i, low: (i, 0))
    whole_spec = spec((length, width), lambda i, low: (0, 0))
    return pl.pallas_call(
        later(functools.partial(attend_back_kernel, head_count), 8, len(after)),
        grid_spec=pltpu.PrefetchScalarGridSpec(
            num_scalar_prefetch=1,
            grid=(blocks,),
            in_specs=[
                block_spec,
                whole_spec,
                whole_spec,
                block_spec,
                block_spec,
                spec((stat_rows, size), lambda i, low: (0, i)),
                spec((8, size), lambda i, low: (0, i)),
                *later_specs(after),
            ],
            out_specs=[block_spec, whole_spec, whole_spec],
            scratch_shapes=[
                pltpu.VMEM((width, length), jnp.bfloat16),
                pltpu.VMEM((length, width), jnp.float32),
                pltpu.VMEM((length, width), jnp.float32),
                pltpu.VMEM((width, size), jnp.float32),
                pltpu.VMEM((size, head_count * size), jnp.bfloat16),
                pltpu.VMEM((size, head_count * size), jnp.bfloat16),
            ],
        ),
        out_shape=[jax.ShapeDtypeStruct((length, width), jnp.bfloat16)] * 3,
        compiler_params=kernel_params(),
        cost_estimate=small_cost,
        name="attend_back",
    )(with_inner(low_blocks, start_rows, size), query, key, value, grad, attended, lse, start_rows, *after)


def project_kernel(count, own_width, order_ref, *refs):
    block_refs, weight_refs, vector_ref = refs[:count], refs[count : 2 * count], refs[2 * count]
    weight_ref, plain_ref, normed_ref, q_ref, k_ref, v_ref = refs[2 * count + 1 :]
    piece = weight_refs[0].shape[0]

    @pl.when(pl.program_id(0) == 0)
    def _():
        for place in range(count):
            rows = pl.ds(pl.multiple_of(order_ref[place] * piece, piece), piece)
            weight_ref[rows, :] = weight_refs[place][:, : 3 * own_width]

    for place in range(count):

        @pl.when(pl.program_id(0) == place)
        def _():
            rows = norm_rows(block_refs[place][...].astype(jnp.float32), 1.0, 0.0)
            plain_ref[...] = rows.astype(jnp.bfloat16)
            normed = (rows * vector_ref[0:1, :] + vector_ref[1:2, :]).astype(jnp.bfloat16)
            normed_ref[...] = normed
            projected = row_dot(normed, weight_ref[...]).astype(jnp.bfloat16)
            q_ref[...] = projected[:, :own_width]
            k_ref[...] = projected[:, own_width : 2 * own_width]
            v_ref[...] = projected[:, 2 * own_width :]


def project_rows(blocks, weights, order, vectors):
    count = len(blocks)
    size, width = blocks[0].shape
    weight_rows = weights[0].shape[0]
    own_width = width // count
    whole = lambda shape: spec(shape, lambda i, order: (0, 0))
    placed = lambda columns: spec((size, columns), lambda i, order: (order[i], 0))
    return pl.pallas_call(
        functools.partial(project_kernel, count, own_width),
        grid_spec=pltpu.PrefetchScalarGridSpec(
            num_scalar_prefetch=1,
            grid=(count,),
            in_specs=[
                *[whole((size, width))] * count,
                *[whole(weights[0].shape)] * count,
                whole(vectors.shape),
            ],
            out_specs=[whole((width, 3 * own_width))]
            + [placed(width)] * 2
            + [placed(own_width)] * 3,
        ),
        out_shape=[jax.ShapeDtypeStruct((width, 3 * own_width), jnp.bfloat16)]
        + [jax.ShapeDtypeStruct((count * size, width), jnp.bfloat16)] * 2
        + [jax.ShapeDtypeStruct((count * size, own_width), jnp.bfloat16)] * 3,
        compiler_params=kernel_params(),
        cost_estimate=pl.CostEstimate(
            flops=13_000_000_000, bytes_accessed=1000, transcendentals=0
        ),
        name="project_rows",
    )(order, *blocks, *weights, vectors)


def planes_kernel(spacing, keys_ref, planes_ref, turned_ref, square_ref, wide_ref):
    near_count = keys_ref.shape[0] // spacing

    @pl.when(pl.program_id(0) == 0)
    def _():
        square_ref[...] = jnp.zeros_like(square_ref)

    wide_ref[...] = keys_ref[...].astype(jnp.float32)
    for plane in range(spacing):
        rows = slice(plane * near_count, (plane + 1) * near_count)
        keys = wide_ref[pl.ds(plane, near_count, stride=spacing), :]
        planes_ref[rows, :] = keys.astype(jnp.bfloat16)
        turned = keys.T
        turned_ref[:, rows] = turned.astype(jnp.bfloat16)
        square_ref[plane : plane + 1, :] += jnp.sum(turned * turned, axis=0, keepdims=True)


def key_planes(keys, spacing):
    count, width = keys.shape
    columns = row_chunk(width, (128,))
    near_count = count // spacing
    return pl.pallas_call(
        functools.partial(planes_kernel, spacing),
        grid=(width // columns,),
        in_specs=[spec((count, columns), lambda i: (0, i))],
        out_specs=[
            spec((count, columns), lambda i: (0, i)),
            spec((columns, count), lambda i: (i, 0)),
            spec((spacing, near_count), lambda i: (0, 0)),
        ],
        out_shape=[
            jax.ShapeDtypeStruct((count, width), jnp.bfloat16),
            jax.ShapeDtypeStruct((width, count), jnp.bfloat16),
            jax.ShapeDtypeStruct((spacing, near_count), jnp.float32),
        ],
        scratch_shapes=[pltpu.VMEM((count, columns), jnp.float32)],
        compiler_params=kernel_params(),
        cost_estimate=small_cost,
        name="key_planes",
    )(keys)


def near_kernel(spacing, dist_scale, parts, *refs):
    order_ref, query_ref, keys_ref, square_ref, values_ref = refs[:5]
    near_refs, target_refs = refs[5 : 5 + parts], refs[5 + parts : 5 + 2 * parts]
    e_ref, s_ref = refs[5 + 2 * parts :]
    piece, near_count = near_refs[0].shape[1:]
    rows = parts * piece
    lane = lax.broadcasted_iota(jnp.int32, (rows, near_count), 1)
    near = jnp.concatenate([ref[0] for ref in near_refs], axis=0)
    offset = near - spacing * lane
    target = jnp.concatenate([ref[0].T for ref in target_refs], axis=0)[:, 0:1]
    picked = jnp.zeros((rows, near_count), jnp.float32)
    words = jnp.full((rows, near_count), -1.0, jnp.float32)
    queries = query_ref[...]
    for plane in range(spacing):
        lanes = slice(plane * near_count, (plane + 1) * near_count)
        inner = row_dot(queries, keys_ref[:, lanes])
        chosen = offset == plane
        picked = jnp.where(chosen, 2.0 * inner - square_ref[plane : plane + 1, :], picked)
        words = jnp.where(chosen, values_ref[plane : plane + 1, :], words)
    scores = picked * dist_scale
    matched = words == target
    peak = jnp.max(scores, axis=1, keepdims=True)
    raised = jnp.exp(scores - peak)
    total = jnp.sum(raised, axis=1, keepdims=True)
    hits = jnp.sum(jnp.where(matched, raised, 0.0), axis=1, keepdims=True)
    e_ref[...] = jnp.where(matched, raised, -raised)
    stat_lane = lax.broadcasted_iota(jnp.int32, (rows, 128), 1)
    stats = jnp.where(stat_lane == 0, peak, jnp.where(stat_lane == 1, total, hits))
    for part in range(parts):
        s_ref[part] = stats[part * piece : (part + 1) * piece, :].T[: s_ref.shape[1], :]


def picked_specs(shape, parts):
    return [
        spec((1,) + shape, functools.partial(lambda part, i, order: (order[i * parts + part], 0, 0), part))
        for part in range(parts)
    ]


def near_scores(queries, keys_turned, square, values, near, target_rows, order, parts, spacing):
    stat_rows, piece = target_rows.shape[1:]
    near_count = near.shape[2]
    slot_rows = queries.shape[0]
    width, keys = keys_turned.shape
    rows = parts * piece
    return pl.pallas_call(
        functools.partial(near_kernel, spacing, width ** (-0.5), parts),
        grid_spec=pltpu.PrefetchScalarGridSpec(
            num_scalar_prefetch=1,
            grid=(slot_rows // rows,),
            in_specs=[
                spec((rows, width), lambda i, order: (i, 0)),
                spec((width, keys), lambda i, order: (0, 0)),
                spec((spacing, near_count), lambda i, order: (0, 0)),
                spec((spacing, near_count), lambda i, order: (0, 0)),
            ]
            + picked_specs((piece, near_count), parts)
            + picked_specs((stat_rows, piece), parts),
            out_specs=[
                spec((rows, near_count), lambda i, order: (i, 0)),
                spec((parts, stat_rows, piece), lambda i, order: (i, 0, 0)),
            ],
        ),
        out_shape=[
            jax.ShapeDtypeStruct((slot_rows, near_count), jnp.float32),
            jax.ShapeDtypeStruct((slot_rows // piece, stat_rows, piece), jnp.float32),
        ],
        compiler_params=kernel_params(),
        cost_estimate=small_cost,
        name="near_scores",
    )(order, queries, keys_turned, square, values, *[near] * parts, *[target_rows] * parts)


def near_back_kernel(spacing, factor, parts, *refs):
    order_ref, e_ref = refs[:2]
    near_refs, coeff_refs = refs[2 : 2 + parts], refs[2 + parts : 2 + 2 * parts]
    keys_ref, out_ref, dense_ref = refs[2 + 2 * parts :]
    piece, near_count = near_refs[0].shape[1:]
    lane = lax.broadcasted_iota(jnp.int32, (piece, near_count), 1)
    for part in range(parts):
        rows = slice(part * piece, (part + 1) * piece)
        offset = near_refs[part][0] - spacing * lane
        columns = coeff_refs[part][0].T
        coefficient, probability = columns[:, 0:1], columns[:, 1:2]
        marked = e_ref[rows, :]
        matched = jnp.where(marked > 0.0, 1.0, 0.0)
        grads = coefficient * (matched - probability) * jnp.abs(marked) * factor
        for plane in range(spacing):
            lanes = slice(plane * near_count, (plane + 1) * near_count)
            dense_ref[rows, lanes] = jnp.where(offset == plane, grads, 0.0).astype(jnp.bfloat16)
    out_ref[...] = row_dot(dense_ref[...], keys_ref[...]).astype(out_ref.dtype)


def near_back(marked, near, coeff_rows, keys_planes, order, parts, spacing, after=()):
    stat_rows, piece = coeff_rows.shape[1:]
    slot_rows, near_count = marked.shape
    keys, width = keys_planes.shape
    rows = parts * piece
    return pl.pallas_call(
        later(
            functools.partial(near_back_kernel, spacing, 2.0 * width ** (-0.5), parts),
            3 + 2 * parts,
            len(after),
        ),
        grid_spec=pltpu.PrefetchScalarGridSpec(
            num_scalar_prefetch=1,
            grid=(slot_rows // rows,),
            in_specs=[spec((rows, near_count), lambda i, order: (i, 0))]
            + picked_specs((piece, near_count), parts)
            + picked_specs((stat_rows, piece), parts)
            + [spec((keys, width), lambda i, order: (0, 0))]
            + later_specs(after),
            out_specs=spec((rows, width), lambda i, order: (i, 0)),
            scratch_shapes=[pltpu.VMEM((rows, keys), jnp.bfloat16)],
        ),
        out_shape=jax.ShapeDtypeStruct((slot_rows, width), jnp.bfloat16),
        compiler_params=kernel_params(),
        cost_estimate=small_cost,
        name="near_back",
    )(order, marked, *[near] * parts, *[coeff_rows] * parts, keys_planes, *after)


def pack_kernel(options, pick_ref, *refs):
    row_refs, (map_ref, out_ref, chosen_ref) = refs[:options], refs[options:]
    owners, capacity = out_ref.shape[:2]
    tokens = map_ref.shape[1]

    @pl.when(pl.program_id(0) == 0)
    def _():
        slot = lax.broadcasted_iota(jnp.int32, (capacity, tokens), 0)
        for owner in range(owners):
            chosen = jnp.where(map_ref[owner : owner + 1, :] == slot, 1.0, 0.0)
            chosen_ref[owner * capacity : (owner + 1) * capacity, :] = chosen.astype(jnp.bfloat16)

    rows = row_refs[0][...]
    for place in range(1, options):
        rows = jnp.where(pick_ref[0] == place, row_refs[place][...], rows)
    packed = row_dot(chosen_ref[...], rows).astype(out_ref.dtype)
    out_ref[...] = packed.reshape(out_ref.shape)


def pack_rows(options, pick, slot_map, capacity, after=()):
    owners, tokens = slot_map.shape
    width = options[0].shape[1]
    columns = row_chunk(width, (256,))
    return pl.pallas_call(
        later(functools.partial(pack_kernel, len(options)), 2 + len(options), len(after)),
        grid_spec=pltpu.PrefetchScalarGridSpec(
            num_scalar_prefetch=1,
            grid=(width // columns,),
            in_specs=[
                *[spec((tokens, columns), lambda i, pick: (0, i))] * len(options),
                spec((owners, tokens), lambda i, pick: (0, 0)),
                *later_specs(after),
            ],
            out_specs=spec((owners, capacity, columns), lambda i, pick: (0, 0, i)),
            scratch_shapes=[pltpu.VMEM((owners * capacity, tokens), jnp.bfloat16)],
        ),
        out_shape=jax.ShapeDtypeStruct((owners, capacity, width), options[0].dtype),
        compiler_params=kernel_params(),
        cost_estimate=pl.CostEstimate(
            flops=30_000_000_000, bytes_accessed=1000, transcendentals=0
        ),
        name="pack_rows",
    )(pick, *options, slot_map, *after)


def unpack_kernel(back_ref, column_ref, out_ref, chosen_ref):
    owners, capacity, columns = back_ref.shape
    tokens = out_ref.shape[0]

    @pl.when(pl.program_id(0) == 0)
    def _():
        slot = lax.broadcasted_iota(jnp.int32, (capacity, tokens), 0)
        for owner in range(owners):
            chosen = jnp.where(column_ref[owner : owner + 1, :] == slot, 1.0, 0.0)
            chosen_ref[owner * capacity : (owner + 1) * capacity, :] = chosen.astype(jnp.bfloat16)

    back = back_ref[...].reshape(owners * capacity, columns)
    out_ref[...] = left_dot(chosen_ref[...], back).astype(out_ref.dtype)


def unpack_rows(returned, slot_map, kind, after=()):
    owners, capacity, width = returned.shape
    tokens = slot_map.shape[1]
    columns = row_chunk(width, (256,))
    return pl.pallas_call(
        later(unpack_kernel, 2, len(after)),
        grid=(width // columns,),
        in_specs=[
            spec((owners, capacity, columns), lambda i: (0, 0, i)),
            spec((owners, tokens), lambda i: (0, 0)),
            *later_specs(after),
        ],
        out_specs=spec((tokens, columns), lambda i: (0, i)),
        out_shape=jax.ShapeDtypeStruct((tokens, width), kind),
        scratch_shapes=[pltpu.VMEM((owners * capacity, tokens), jnp.bfloat16)],
        compiler_params=kernel_params(),
        cost_estimate=small_cost,
        name="unpack_rows",
    )(returned, slot_map, *after)


def mix_kernel(stats_ref, map_ref, prob_ref, loss_ref, send_ref, peak_ref, total_ref, hits_ref):
    owners, stat_rows, capacity = stats_ref.shape
    tokens = map_ref.shape[1]
    slot = lax.broadcasted_iota(jnp.int32, (capacity, tokens), 0)
    for owner in range(owners):
        chosen = map_ref[owner : owner + 1, :] == slot
        columns = stats_ref[owner].T
        for place, target in enumerate((peak_ref, total_ref, hits_ref)):
            target[owner : owner + 1, :] = jnp.sum(
                jnp.where(chosen, columns[:, place : place + 1], 0.0), axis=0, keepdims=True
            )
    member = map_ref[...] >= 0
    peaks = jnp.where(member, peak_ref[...], -3e38)
    best = jnp.max(peaks, axis=0, keepdims=True)
    rescale = jnp.where(member, jnp.exp(peaks - best), 0.0)
    knn_total = jnp.sum(total_ref[...] * rescale, axis=0, keepdims=True)
    knn_prob = jnp.sum(hits_ref[...] * rescale, axis=0, keepdims=True) / knn_total
    mixture = mix_weight * knn_prob + (1.0 - mix_weight) * prob_ref[...]
    loss_ref[...] = -jnp.log(mixture)
    peak_ref[...] = (-mix_weight / (mixture * knn_total)) * rescale
    for owner in range(owners):
        chosen = map_ref[owner : owner + 1, :] == slot
        coefficient = jnp.sum(
            jnp.where(chosen, peak_ref[owner : owner + 1, :], 0.0), axis=1, keepdims=True
        )
        probability = jnp.sum(jnp.where(chosen, knn_prob, 0.0), axis=1, keepdims=True)
        lane = lax.broadcasted_iota(jnp.int32, (capacity, 128), 1)
        both = jnp.where(lane == 0, coefficient, probability)
        send_ref[owner] = both.T[:stat_rows, :]


def mix_losses(stats, slot_map, model_prob):
    owners, stat_rows, capacity = stats.shape
    tokens = slot_map.shape[1]
    vmem = pl.BlockSpec(memory_space=pltpu.VMEM)
    return pl.pallas_call(
        mix_kernel,
        in_specs=[vmem] * 3,
        out_specs=[vmem] * 2,
        out_shape=[
            jax.ShapeDtypeStruct((1, tokens), jnp.float32),
            jax.ShapeDtypeStruct(stats.shape, jnp.float32),
        ],
        scratch_shapes=[pltpu.VMEM((owners, tokens), jnp.float32)] * 3,
        compiler_params=pltpu.CompilerParams(vmem_limit_bytes=vmem_limit),
        name="mix_losses",
    )(stats, slot_map, model_prob)


def row_chunk(total, choices):
    for choice in choices:
        if total % choice == 0:
            return choice
    return total


def slot_picker(slot_map, capacity):
    return slot_map[:, None, :] == jnp.arange(capacity, dtype=jnp.int32)[None, :, None]


def layer_table(count):
    return [
        sorted(range(count), key=lambda other: (abs(other - layer), (other ^ layer) != 1, other))
        for layer in range(count)
    ]


def own_choice(options):
    layer = lax.axis_index("batch")
    kept = options[0]
    for place in range(1, len(options)):
        if all(options[place] is not other for other in options[:place]):
            same = [i for i, other in enumerate(options) if other is options[place]]
            here = functools.reduce(jnp.logical_or, [layer == i for i in same])
            kept = jnp.where(here, options[place], kept)
    return kept


def layer_step(step, ups, downs):
    options, picks = [], []
    for layer, line in enumerate(layer_table(lax.axis_size("batch"))):
        there = line[step]
        block = ups[layer - there] if there < layer else downs[there - layer]
        places = [place for place, other in enumerate(options) if other is block]
        if not places:
            options.append(block)
        picks.append(places[0] if places else len(options) - 1)
    return options, jnp.array(picks, jnp.int32)[lax.axis_index("batch")][None]


def layer_hop(hop, blocks, above, below):
    count = lax.axis_size("batch")
    reach = count - hop
    table = layer_table(count)

    def bound(layer, to):
        return blocks[table[layer].index(to) if 0 <= to < count else hop_step]

    hop_step = reach
    up = own_choice([bound(layer, layer + reach) for layer in range(count)])
    down = own_choice([bound(layer, layer - reach) for layer in range(count)])
    if hop > 1:
        up = (up.astype(jnp.float32) + above).astype(up.dtype)
        down = (down.astype(jnp.float32) + below).astype(down.dtype)
    return (
        lax.ppermute(up, "batch", [(i, i + 1) for i in range(hop)]),
        lax.ppermute(down, "batch", [(i, i - 1) for i in range(reach, count)]),
    )


def across(rows, step):
    return lax.ppermute(rows, "ctx", [(i, i ^ step) for i in range(lax.axis_size("ctx"))])


def in_ctx_order(parts):
    count = len(parts)
    own = lax.axis_index("ctx")
    stacked = jnp.stack(parts)
    return stacked[jnp.arange(count, dtype=jnp.int32) ^ own]


def ctx_gather(rows):
    return in_ctx_order([rows] + [across(rows, step) for step in range(1, lax.axis_size("ctx"))])


def swap_cores(rows):
    return lax.ppermute(rows, "rep", [(0, 1), (1, 0)])


def reduce_cores(grad):
    count = lax.axis_size("ctx")
    parts = grad.astype(jnp.bfloat16).reshape(count, 2, grad.shape[0] // (2 * count), grad.shape[1])
    core = lax.axis_index("rep")
    keep = lax.dynamic_index_in_dim(parts, core, 1, keepdims=False)
    send = lax.dynamic_index_in_dim(parts, 1 - core, 1, keepdims=False)
    return (keep.astype(jnp.float32) + swap_cores(send)).astype(jnp.bfloat16)


def ctx_trade(blocks):
    return [part if step == 0 else across(part, step) for step, part in enumerate(blocks)]


def exchange(blocks, axis):
    return lax.all_to_all(blocks, axis, split_axis=0, concat_axis=0, tiled=True)


def block_sum(blocks):
    total = blocks[0].astype(jnp.float32)
    for place in range(1, len(blocks)):
        total = total + blocks[place].astype(jnp.float32)
    return total


def ctx_reduce(halves):
    return lax.psum_scatter(halves, "ctx", scatter_dimension=0)


def layer_total(blocks):
    return block_sum(exchange(blocks, "batch")).astype(jnp.bfloat16)


def layer_blocks(rows):
    return rows.reshape(lax.axis_size("batch"), -1, rows.shape[1])


def both_halves(half):
    other = swap_cores(half)
    first = lax.axis_index("rep") == 0
    both = jnp.stack([jnp.where(first, half, other), jnp.where(first, other, half)])
    return both.reshape(-1, half.shape[-1]).astype(jnp.float32)


def layer_gather(rows):
    count = lax.axis_size("batch")
    return [rows] + [
        lax.ppermute(rows, "batch", [(i, (i + hops) % count) for i in range(count)])
        for hops in range(1, count)
    ]


def whole_shard(parts):
    count, layer = len(parts), lax.axis_index("batch")
    return both_halves(jnp.stack(parts)[(layer - jnp.arange(count, dtype=jnp.int32)) % count])


def mix_any(stats, slot_map, model_prob):
    owners, stat_rows, capacity = stats.shape
    if capacity % 16 == 0:
        return mix_losses(stats, slot_map, model_prob)
    chosen = slot_picker(slot_map, capacity)
    peak, total, hits = [
        jnp.sum(jnp.where(chosen, stats[:, row, :, None], 0.0), axis=1) for row in range(3)
    ]
    member = slot_map >= 0
    peaks = jnp.where(member, peak, -3e38)
    best = jnp.max(peaks, axis=0, keepdims=True)
    rescale = jnp.where(member, jnp.exp(peaks - best), 0.0)
    knn_total = jnp.sum(total * rescale, axis=0, keepdims=True)
    knn_prob = jnp.sum(hits * rescale, axis=0, keepdims=True) / knn_total
    mixture = mix_weight * knn_prob + (1.0 - mix_weight) * model_prob
    coefficient = (-mix_weight / (mixture * knn_total)) * rescale
    sent = [
        jnp.sum(jnp.where(chosen, part[:, None, :], 0.0), axis=2)
        for part in (coefficient, jnp.broadcast_to(knn_prob, coefficient.shape))
    ]
    sent = jnp.stack(sent + [sent[1]] * (stat_rows - 2), axis=1)
    return -jnp.log(mixture), sent


def local(
    tokens,
    cotangent,
    segment_ids,
    first_gain,
    first_shift,
    second_gain,
    second_shift,
    final_gain,
    final_shift,
    project_weight,
    output_weight,
    upward_weight,
    downward_weight,
    store_keys,
    store_values,
    owners,
    neighbours,
    targets,
    model_prob,
):
    head_count = HEADS
    group_seqs, block_len, width = tokens.shape
    seq_len = segment_ids.shape[1]
    ctx_count = lax.axis_size("ctx")
    shard_count = lax.axis_size("batch") * ctx_count
    capacity = neighbours.shape[3]
    near_count = neighbours.shape[4]
    top_count = owners.shape[2]
    key_count = store_keys.shape[0]
    spacing = key_count // near_count
    slot_rows = shard_count * capacity
    everyone = ("batch", "ctx")
    own_heads = head_count // ctx_count
    own_width = width // ctx_count
    attend_size = row_chunk(seq_len, (256, 128))

    arrived = [tokens[0]] + [across(tokens[0], step) for step in range(1, ctx_count)]
    own_rows = project_weight.shape[0]
    own_ctx = lax.axis_index("ctx")
    vectors = jnp.stack(
        [first_gain, first_shift, second_gain, second_shift, final_gain, final_shift], axis=1
    )
    vectors = jnp.pad(vectors, ((0, 0), (0, 128 - vectors.shape[1])))
    proj_pieces = [
        jnp.concatenate(
            [
                lax.dynamic_slice_in_dim(
                    project_weight, part * width + (own_ctx ^ step) * own_width, own_width, 1
                )
                for part in range(3)
            ]
            + [vectors],
            axis=1,
        )
        for step in range(ctx_count)
    ]
    proj_pieces = ctx_trade(proj_pieces)
    vectors = in_ctx_order([piece[:, 3 * own_width :] for piece in proj_pieces])
    vectors = vectors.reshape(width, -1)[:, :6].T.astype(jnp.float32)
    gain_list = [vectors[row] for row in range(6)]

    member = jnp.any(
        owners[0][:, :, None] == jnp.arange(shard_count, dtype=jnp.int32)[None, None, :], axis=1
    )
    place = jnp.arange(block_len, dtype=jnp.int32)
    earlier = (place[:, None] <= place[None, :]).astype(jnp.bfloat16)
    running = left_dot(member.astype(jnp.bfloat16), earlier).astype(jnp.int32)
    slot_map = jnp.where(member.T, running - 1, -1)
    send_targets = jnp.sum(
        jnp.where(slot_picker(slot_map, capacity), targets.reshape(1, 1, -1), 0), axis=2
    )
    got_targets = exchange(send_targets.astype(jnp.int32), everyone).astype(jnp.float32)
    planes, planes_turned, key_square = key_planes(store_keys, spacing)
    value_planes = store_values.astype(jnp.float32).reshape(near_count, spacing).T
    by_layer = capacity % 16 == 0
    if by_layer:
        piece, parts = capacity, 2 if ctx_count % 2 == 0 else 1
        layer_count = lax.axis_size("batch")
        maps = exchange(slot_map.reshape(layer_count, ctx_count, block_len), "batch")
        table = jnp.array(layer_table(layer_count), jnp.int32)[lax.axis_index("batch")]
        maps = maps[table]
        orders = table[:, None] * ctx_count + jnp.arange(ctx_count, dtype=jnp.int32)[None, :]
    else:
        piece, parts = row_chunk(slot_rows, (576, 512, 384, 256, 128)), 1
        orders = jnp.arange(slot_rows // piece, dtype=jnp.int32)[None, :]
        chosen_slots = slot_picker(slot_map, capacity).astype(jnp.bfloat16)
    near_table = neighbours.reshape(slot_rows // piece, piece, near_count)
    stat_shape = (slot_rows // piece, 8, piece)
    target_rows = jnp.broadcast_to(got_targets.reshape(stat_shape[0], 1, piece), stat_shape)

    early = proj_pieces[1:]
    core = lax.axis_index("rep")

    def own_half(weight):
        half = weight.shape[0] // 2
        mine = lax.dynamic_slice_in_dim(weight, core * half, half, 0)
        return run_after([mine], [*arrived[1:], *early])[0]

    def gather_weight(weight):
        return lax.all_gather(own_half(weight), ("ctx", "rep"), axis=0, tiled=True)

    out_full = gather_weight(output_weight)
    down_full = gather_weight(downward_weight)
    up_half = own_half(upward_weight)
    up_pieces = [across(up_half, step) for step in range(1, ctx_count)]
    sources = own_ctx ^ jnp.arange(ctx_count, dtype=jnp.int32)

    segments = segment_ids[0]
    start_rows = jnp.sum((segments[None, :] < segments[:, None]).astype(jnp.int32), axis=1)
    low_blocks = start_rows[::attend_size] // attend_size
    start_rows = jnp.broadcast_to(start_rows[None, :], (8, seq_len))
    proj_own, plain_full, normed_full, query_own, key_own, value_own = project_rows(
        arrived, proj_pieces, sources, vectors
    )
    attended_own, log_total = attend(
        query_own, key_own, value_own, start_rows, low_blocks, own_heads, attend_size
    )
    attended = lax.all_to_all(attended_own, "ctx", split_axis=0, concat_axis=1, tiled=True)
    attended = run_after([attended], [target_rows, maps] if by_layer else [target_rows])[0]
    up_pieces = [up_half, *run_after(up_pieces, [attended])]
    up_full = place_rows(
        up_pieces + [swap_cores(piece) for piece in up_pieces],
        jnp.concatenate([2 * sources + core, 2 * sources + 1 - core]),
    )
    inputs = tokens[0].astype(jnp.float32)
    hidden = inputs + row_dot(attended, out_full)
    normed_two = norm_rows(hidden, gain_list[2], gain_list[3]).astype(jnp.bfloat16)
    upper_rows = row_dot(normed_two, up_full)
    active = jax.nn.gelu(upper_rows).astype(jnp.bfloat16)
    summed = hidden + row_dot(active, down_full)
    final_rows = norm_rows(summed, gain_list[4], gain_list[5]).astype(jnp.bfloat16)

    if by_layer:
        ups, downs, packed, queries = [final_rows], [final_rows], [], []
        for step in range(layer_count):
            hop = step + 1
            if hop < layer_count:
                up, down = ups[-1], downs[-1]
                if hop == 2:
                    up, down = run_after([up, down], packed)
                    ups[-1], downs[-1] = up, down
                elif hop > 2:
                    up, down = run_after([up, down], [queries[hop - 3]])
                    ups[-1], downs[-1] = up, down
                ups.append(
                    lax.ppermute(up, "batch", [(i, i + 1) for i in range(step, layer_count - 1)])
                )
                downs.append(
                    lax.ppermute(down, "batch", [(i, i - 1) for i in range(1, layer_count - step)])
                )
            options, pick = layer_step(step, ups, downs)
            between = (planes, planes_turned, key_square) if step == 1 else ()
            packed.append(pack_rows(options, pick, maps[step], capacity, between))
            queries.append(exchange(packed[step], "ctx").reshape(-1, width))
    else:
        packed = jnp.einsum(
            "ost,tw->osw", chosen_slots, final_rows, preferred_element_type=jnp.float32
        )
        queries = [exchange(packed.astype(jnp.bfloat16), everyone).reshape(slot_rows, width)]
    marked, stats = zip(
        *[
            near_scores(
                rows,
                planes_turned,
                key_square,
                value_planes,
                near_table,
                target_rows,
                orders[step],
                parts,
                spacing,
            )
            for step, rows in enumerate(queries)
        ]
    )
    if by_layer:
        inverse = jnp.argmin(
            jnp.abs(table[None, :] - jnp.arange(layer_count, dtype=jnp.int32)[:, None]), axis=1
        )
        stats = jnp.stack(stats)[inverse].reshape(stat_shape)
    else:
        stats = stats[0].transpose(1, 0, 2).reshape(8, shard_count, capacity).transpose(1, 0, 2)
    token_loss, send_coeff = mix_any(exchange(stats, everyone), slot_map, model_prob)
    got_coeff = exchange(send_coeff, everyone)
    if not by_layer:
        got_coeff = got_coeff.transpose(1, 0, 2).reshape(8, -1, piece).transpose(1, 0, 2)
    if by_layer:
        returned, above, below = {}, None, None
        for step in reversed(range(layer_count)):
            hop = layer_count - 1 - step
            partial_grad = near_back(
                marked[step],
                near_table,
                got_coeff,
                planes,
                orders[step],
                parts,
                spacing,
                [returned[step + 2]] if hop >= 2 else [],
            )
            back = exchange(partial_grad.reshape(ctx_count, capacity, width), "ctx")
            if hop > 0:
                above, below = layer_hop(hop, returned, above, below)
            returned[step] = unpack_rows(
                back,
                maps[step],
                jnp.bfloat16 if step > 0 else jnp.float32,
                [above, below] if 0 < hop < layer_count - 1 else [],
            )
        query_grad = returned[0] + above.astype(jnp.float32) + below.astype(jnp.float32)
    else:
        partial_grad = near_back(
            marked[0], near_table, got_coeff, planes, orders[0], parts, spacing
        )
        back = exchange(partial_grad.reshape(shard_count, capacity, width), everyone)
        query_grad = jnp.einsum(
            "ost,osw->tw", chosen_slots, back, preferred_element_type=jnp.float32
        )

    out_grad = cotangent[0].astype(jnp.float32) + query_grad
    final_vjp = jax.vjp(norm_rows, summed, gain_list[4], gain_list[5])[1]
    summed_grad, final_gain_grad, final_shift_grad = final_vjp(out_grad)
    branch_grad = summed_grad.astype(jnp.bfloat16)
    downward_grad = left_dot(active, branch_grad)
    active_grad = right_dot(branch_grad, down_full)
    gelu_vjp = jax.vjp(jax.nn.gelu, upper_rows)[1]
    upper_grad = gelu_vjp(active_grad)[0].astype(jnp.bfloat16)
    downward_half = reduce_cores(downward_grad)
    upper_grad = run_after([upper_grad], [downward_half])[0]
    second_vjp = jax.vjp(norm_rows, hidden, gain_list[2], gain_list[3])[1]
    hidden_part, second_gain_grad, second_shift_grad = second_vjp(right_dot(upper_grad, up_full))
    hidden_grad = summed_grad + hidden_part
    attn_grad = hidden_grad.astype(jnp.bfloat16)
    attended_grad = right_dot(attn_grad, out_full).astype(jnp.bfloat16)
    downward_half = ctx_reduce(downward_half)
    second_half = reduce_cores(
        jnp.concatenate(
            [
                left_dot(normed_two, upper_grad).astype(jnp.bfloat16),
                left_dot(attended, attn_grad).astype(jnp.bfloat16),
            ],
            axis=1,
        )
    )
    attended_grad = run_after([attended_grad], [downward_half])[0]
    grad_own = lax.all_to_all(attended_grad, "ctx", split_axis=1, concat_axis=0, tiled=True)
    second_half = run_after([second_half], [grad_own])[0]
    downward_half = run_after([downward_half], [second_half])[0]
    downward_total = layer_total(layer_blocks(downward_half))
    second_start = second_half
    second_half = ctx_reduce(second_half)
    proj_grad = jnp.concatenate(
        run_after(
            attend_back(
                query_own,
                key_own,
                value_own,
                grad_own,
                attended_own,
                log_total,
                start_rows,
                low_blocks,
                own_heads,
                attend_size,
                (second_start, downward_half),
            ),
            [downward_total],
        ),
        axis=1,
    )
    normed_terms = right_dot(proj_grad, proj_own).astype(jnp.bfloat16)
    normed_grad = lax.psum_scatter(normed_terms, "ctx", scatter_dimension=0, tiled=True)

    second_half = run_after([second_half], [normed_terms])[0]
    second_total = layer_total(layer_blocks(second_half))
    second_parts = layer_gather(second_total)
    plain_part = left_dot(plain_full, proj_grad)
    column_sums = jnp.sum(proj_grad.astype(jnp.float32), axis=0)
    proj_full = proj_own.astype(jnp.float32)
    first_gain_grad = jnp.sum(plain_part * proj_full, axis=1)
    first_shift_grad = jnp.sum(column_sums[None, :] * proj_full, axis=1)
    project_part = plain_part * gain_list[0][:, None] + column_sums[None, :] * gain_list[1][:, None]

    vector_part = jnp.stack(
        [
            first_gain_grad,
            first_shift_grad,
            second_gain_grad,
            second_shift_grad,
            final_gain_grad,
            final_shift_grad,
        ],
        axis=1,
    )
    vector_part = jnp.pad(vector_part, ((0, 0), (0, 128 - vector_part.shape[1])))
    project_part = jnp.concatenate([project_part, vector_part], axis=1).astype(jnp.bfloat16)
    project_part = reduce_cores(run_after([project_part], [second_total])[0])
    downward_parts = layer_gather(run_after([downward_total], [project_part])[0])
    project_part = in_ctx_order(
        ctx_trade(
            [
                lax.dynamic_index_in_dim(project_part, own_ctx ^ step, 0, keepdims=False)
                for step in range(ctx_count)
            ]
        )
    )
    vector_part = block_sum(project_part[:, :, 3 * own_width :]).astype(jnp.bfloat16)
    project_part = (
        project_part[:, :, : 3 * own_width]
        .reshape(ctx_count, own_rows // 2, 3, own_width)
        .transpose(1, 2, 0, 3)
        .reshape(own_rows // 2, 3 * width)
    )
    small_rows = jnp.concatenate([project_part, vector_part], axis=1)
    small_rows = run_after([small_rows], second_parts[1:])[0]
    small_total = layer_total(layer_blocks(small_rows))
    input_vjp = jax.vjp(lambda rows: norm_rows(rows, gain_list[0], gain_list[1]), inputs)[1]
    normed_grad = run_after([normed_grad], [small_total])[0]
    input_grad = hidden_grad + input_vjp(normed_grad.astype(jnp.float32))[0]
    small_grads = whole_shard(layer_gather(small_total))
    second_grads = whole_shard(second_parts)
    weight_grads = [
        small_grads[:, : 3 * width],
        second_grads[:, second_grads.shape[1] - width :],
        second_grads[:, : second_grads.shape[1] - width],
        whole_shard(downward_parts),
    ]
    vector_grads = small_grads[:, 3 * width : 3 * width + 6].T
    return (
        final_rows.reshape(group_seqs, block_len, width),
        token_loss.reshape(group_seqs, block_len),
        query_grad.reshape(group_seqs, block_len, width),
        input_grad.reshape(group_seqs, block_len, width),
        *weight_grads,
        *[vector_grads[row] for row in range(6)],
    )


def solution(mesh):
    placed = (
        P(("rep", "batch"), "ctx", None),
        P(("rep", "batch"), "ctx", None),
        P(("rep", "batch"), None),
        P("ctx"),
        P("ctx"),
        P("ctx"),
        P("ctx"),
        P("ctx"),
        P("ctx"),
        P("ctx", None),
        P("ctx", None),
        P("ctx", None),
        P("ctx", None),
        P(("batch", "ctx"), None),
        P(("batch", "ctx")),
        P(("rep", "batch"), "ctx", None),
        P("rep", ("batch", "ctx"), None, None, None),
        P(("rep", "batch"), "ctx"),
        P(("rep", "batch"), "ctx"),
    )
    return jax.shard_map(
        local,
        mesh=mesh,
        in_specs=placed,
        out_specs=(
            P(("rep", "batch"), "ctx", None),
            P(("rep", "batch"), "ctx"),
            P(("rep", "batch"), "ctx", None),
            P(("rep", "batch"), "ctx", None),
            P("ctx", None),
            P("ctx", None),
            P("ctx", None),
            P("ctx", None),
            P("ctx"),
            P("ctx"),
            P("ctx"),
            P("ctx"),
            P("ctx"),
            P("ctx"),
        ),
        check_vma=False,
    )
```

```python
import functools

import jax
import jax.numpy as jnp
from jax import lax
from jax.experimental import pallas as pl
from jax.experimental.pallas import tpu as pltpu
from jax.sharding import PartitionSpec as P

HEADS = 16


norm_eps = 1e-05
mix_weight = 0.25
masked_value = -1e30
vmem_limit = 60 * 1024 * 1024
small_cost = pl.CostEstimate(flops=1000, bytes_accessed=1000, transcendentals=0)


def norm_rows(values, scale_gain, shift_term):
    average = jnp.mean(values, axis=-1, keepdims=True)
    centred = values - average
    spread = jnp.mean(centred * centred, axis=-1, keepdims=True)
    return centred * lax.rsqrt(spread + norm_eps) * scale_gain + shift_term


def row_dot(left_side, right_side):
    return jnp.dot(left_side, right_side, preferred_element_type=jnp.float32)


def left_dot(left_side, right_side):
    return lax.dot_general(
        left_side, right_side, (((0,), (0,)), ((), ())), preferred_element_type=jnp.float32
    )


def right_dot(left_side, right_side):
    return lax.dot_general(
        left_side, right_side, (((1,), (1,)), ((), ())), preferred_element_type=jnp.float32
    )


def spec(shape, index_map):
    return pl.BlockSpec(shape, index_map)


def kernel_params(dims=1):
    return pltpu.CompilerParams(
        vmem_limit_bytes=vmem_limit, dimension_semantics=("arbitrary",) * dims
    )


def later(kernel, place, count):
    return lambda *refs: kernel(*refs[:place], *refs[place + count :])


def later_specs(after):
    return [pl.BlockSpec(memory_space=pl.ANY)] * len(after)


def run_after(arrays, after):
    def kernel(*refs):
        pass

    return pl.pallas_call(
        kernel,
        in_specs=later_specs((*arrays, *after)),
        out_specs=later_specs(arrays),
        out_shape=[jax.ShapeDtypeStruct(rows.shape, rows.dtype) for rows in arrays],
        input_output_aliases={place: place for place in range(len(arrays))},
        cost_estimate=small_cost,
        name="run_after",
    )(*arrays, *after)


def place_kernel(count, start_ref, *refs):
    for place in range(count):

        @pl.when(pl.program_id(0) == place)
        def _():
            refs[count][...] = refs[place][...]


def place_rows(pieces, places):
    count = len(pieces)
    rows, width = pieces[0].shape
    return pl.pallas_call(
        functools.partial(place_kernel, count),
        grid_spec=pltpu.PrefetchScalarGridSpec(
            num_scalar_prefetch=1,
            grid=(count,),
            in_specs=[spec((rows, width), lambda i, places: (0, 0))] * count,
            out_specs=spec((rows, width), lambda i, places: (places[i], 0)),
        ),
        out_shape=jax.ShapeDtypeStruct((count * rows, width), pieces[0].dtype),
        compiler_params=kernel_params(),
        cost_estimate=small_cost,
        name="place_rows",
    )(places, *pieces)


def head_rows(head, size):
    return slice(head * size, (head + 1) * size)


def masked_heads(block, head_count, axis):
    size = block.shape[axis] // head_count
    index = lax.broadcasted_iota(jnp.int32, block.shape, axis) // size
    zero = jnp.zeros((), block.dtype)
    return [jnp.where(index == head, block, zero) for head in range(head_count)]


def block_mask(key_block, query_block, size, start_row):
    key_pos = key_block * size + lax.broadcasted_iota(jnp.int32, (size, size), 0)
    query_pos = query_block * size + lax.broadcasted_iota(jnp.int32, (size, size), 1)
    return (key_pos <= query_pos) & (key_pos >= start_row)


def attend_kernel(
    head_count, low_ref, q_ref, k_ref, v_ref, start_ref, o_ref, lse_ref, vt_ref, acc_ref
):
    step = pl.program_id(0)
    size, width = q_ref.shape
    head_size = width // head_count
    blocks = k_ref.shape[0] // size

    @pl.when(step == 0)
    def _():
        for block in range(blocks):
            rows = slice(block * size, (block + 1) * size)
            vt_ref[:, rows] = v_ref[rows, :].astype(jnp.float32).T.astype(jnp.bfloat16)

    scaled = q_ref[...].astype(jnp.float32) * (head_size ** (-0.5))
    turned = jnp.concatenate(
        [part.astype(jnp.bfloat16) for part in masked_heads(scaled.T, head_count, 0)], axis=1
    )
    start_row = start_ref[0:1, :]
    acc_ref[...] = jnp.zeros_like(acc_ref)
    first = (
        jnp.full((1, head_count * size), masked_value, jnp.float32),
        jnp.zeros((1, head_count * size), jnp.float32),
    )

    def body(masked, block, state):
        peak, total = state
        rows = pl.ds(pl.multiple_of(block * size, size), size)
        scores = row_dot(k_ref[rows, :], turned)
        if masked:
            allowed = block_mask(block, step, size, start_row)
            scores = jnp.concatenate(
                [
                    jnp.where(allowed, scores[:, head * size : (head + 1) * size], masked_value)
                    for head in range(head_count)
                ],
                axis=1,
            )
        new_peak = jnp.maximum(peak, jnp.max(scores, axis=0, keepdims=True))
        fade = jnp.exp(peak - new_peak)
        weights = jnp.exp(scores - new_peak)
        total = total * fade + jnp.sum(weights, axis=0, keepdims=True)
        weights = weights.astype(jnp.bfloat16)
        for head in range(head_count):
            part = head_rows(head, head_size)
            lanes = slice(head * size, (head + 1) * size)
            acc_ref[part, :] = acc_ref[part, :] * fade[:, lanes] + row_dot(
                vt_ref[part, rows], weights[:, lanes]
            )
        return new_peak, total

    low = low_ref[step]
    inner = low_ref[blocks + step]
    state = lax.fori_loop(low, inner, functools.partial(body, True), first)
    state = lax.fori_loop(inner, step, functools.partial(body, False), state)
    peak, total = body(True, step, state)
    for head in range(head_count):
        part = head_rows(head, head_size)
        lanes = slice(head * size, (head + 1) * size)
        acc_ref[part, :] = acc_ref[part, :] / total[:, lanes]
        lse_ref[head : head + 1, :] = peak[:, lanes] + jnp.log(total[:, lanes])
    o_ref[...] = acc_ref[...].T.astype(jnp.bfloat16)


def with_inner(low_blocks, start_rows, size):
    last = start_rows[0, size - 1 :: size]
    inner = jnp.minimum(-(-last // size), jnp.arange(low_blocks.shape[0], dtype=jnp.int32))
    return jnp.concatenate([low_blocks, inner])


def attend(query, key, value, start_rows, low_blocks, head_count, size, after=()):
    length, width = query.shape
    blocks = length // size
    stat_rows = -(-head_count // 8) * 8
    return pl.pallas_call(
        later(functools.partial(attend_kernel, head_count), 5, len(after)),
        grid_spec=pltpu.PrefetchScalarGridSpec(
            num_scalar_prefetch=1,
            grid=(blocks,),
            in_specs=[
                spec((size, width), lambda i, low: (i, 0)),
                spec((length, width), lambda i, low: (0, 0)),
                spec((length, width), lambda i, low: (0, 0)),
                spec((8, size), lambda i, low: (0, i)),
                *later_specs(after),
            ],
            out_specs=[
                spec((size, width), lambda i, low: (i, 0)),
                spec((stat_rows, size), lambda i, low: (0, i)),
            ],
            scratch_shapes=[
                pltpu.VMEM((width, length), jnp.bfloat16),
                pltpu.VMEM((width, size), jnp.float32),
            ],
        ),
        out_shape=[
            jax.ShapeDtypeStruct((length, width), jnp.bfloat16),
            jax.ShapeDtypeStruct((stat_rows, length), jnp.float32),
        ],
        compiler_params=kernel_params(),
        cost_estimate=pl.CostEstimate(
            flops=20_000_000_000, bytes_accessed=1000, transcendentals=0
        ),
        name="attend",
    )(with_inner(low_blocks, start_rows, size), query, key, value, start_rows, *after)


def attend_back_kernel(
    head_count,
    low_ref,
    q_ref,
    k_ref,
    v_ref,
    grad_ref,
    o_ref,
    lse_ref,
    start_ref,
    dq_ref,
    dk_ref,
    dv_ref,
    kt_ref,
    dkey_ref,
    dvalue_ref,
    dqt_ref,
    score_ref,
    weight_ref,
):
    step = pl.program_id(0)
    size, width = q_ref.shape
    head_size = width // head_count
    score_scale = head_size ** (-0.5)
    blocks = k_ref.shape[0] // size

    @pl.when(step == 0)
    def _():
        dkey_ref[...] = jnp.zeros_like(dkey_ref)
        dvalue_ref[...] = jnp.zeros_like(dvalue_ref)
        for block in range(blocks):
            rows = slice(block * size, (block + 1) * size)
            kt_ref[:, rows] = k_ref[rows, :].astype(jnp.float32).T.astype(jnp.bfloat16)

    scaled = q_ref[...].astype(jnp.float32) * score_scale
    grads = grad_ref[...].astype(jnp.float32)
    dots = (grads * o_ref[...].astype(jnp.float32)).T
    query_turned = [p.astype(jnp.bfloat16) for p in masked_heads(scaled.T, head_count, 0)]
    grad_turned = [p.astype(jnp.bfloat16) for p in masked_heads(grads.T, head_count, 0)]
    query_stack = jnp.concatenate(
        [p.astype(jnp.bfloat16) for p in masked_heads(scaled, head_count, 1)], axis=0
    )
    grad_stack = jnp.concatenate(
        [p.astype(jnp.bfloat16) for p in masked_heads(grads, head_count, 1)], axis=0
    )
    row_dots = [
        jnp.sum(dots[head_rows(head, head_size), :], axis=0, keepdims=True)
        for head in range(head_count)
    ]
    start_row = start_ref[0:1, :]
    dqt_ref[...] = jnp.zeros_like(dqt_ref)

    query_wide = jnp.concatenate(query_turned, axis=1)
    grad_wide = jnp.concatenate(grad_turned, axis=1)
    row_wide = jnp.concatenate(row_dots, axis=1)
    lse_wide = jnp.concatenate([lse_ref[head : head + 1, :] for head in range(head_count)], axis=1)

    def body(masked, block, carry):
        rows = pl.ds(pl.multiple_of(block * size, size), size)
        scores = row_dot(k_ref[rows, :], query_wide)
        if masked:
            allowed = block_mask(block, step, size, start_row)
            scores = jnp.concatenate(
                [
                    jnp.where(allowed, scores[:, head * size : (head + 1) * size], masked_value)
                    for head in range(head_count)
                ],
                axis=1,
            )
        weights = jnp.exp(scores - lse_wide)
        weight_grad = row_dot(v_ref[rows, :], grad_wide)
        score_grad = (weights * (weight_grad - row_wide)).astype(jnp.bfloat16)
        weights = weights.astype(jnp.bfloat16)
        for head in range(head_count):
            part = head_rows(head, head_size)
            lanes = slice(head * size, (head + 1) * size)
            dqt_ref[part, :] += row_dot(kt_ref[part, rows], score_grad[:, lanes])
        dkey_ref[rows, :] += row_dot(score_grad, query_stack)
        dvalue_ref[rows, :] += row_dot(weights, grad_stack)
        return carry

    low = low_ref[step]
    inner = low_ref[blocks + step]
    lax.fori_loop(low, inner, functools.partial(body, True), 0)
    lax.fori_loop(inner, step, functools.partial(body, False), 0)
    body(True, step, 0)
    dq_ref[...] = (dqt_ref[...] * score_scale).T.astype(jnp.bfloat16)

    @pl.when(step == blocks - 1)
    def _():
        dk_ref[...] = dkey_ref[...].astype(jnp.bfloat16)
        dv_ref[...] = dvalue_ref[...].astype(jnp.bfloat16)


def attend_back(
    query, key, value, grad, attended, lse, start_rows, low_blocks, head_count, size, after=()
):
    length, width = query.shape
    blocks = length // size
    stat_rows = lse.shape[0]
    block_spec = spec((size, width), lambda i, low: (i, 0))
    whole_spec = spec((length, width), lambda i, low: (0, 0))
    return pl.pallas_call(
        later(functools.partial(attend_back_kernel, head_count), 8, len(after)),
        grid_spec=pltpu.PrefetchScalarGridSpec(
            num_scalar_prefetch=1,
            grid=(blocks,),
            in_specs=[
                block_spec,
                whole_spec,
                whole_spec,
                block_spec,
                block_spec,
                spec((stat_rows, size), lambda i, low: (0, i)),
                spec((8, size), lambda i, low: (0, i)),
                *later_specs(after),
            ],
            out_specs=[block_spec, whole_spec, whole_spec],
            scratch_shapes=[
                pltpu.VMEM((width, length), jnp.bfloat16),
                pltpu.VMEM((length, width), jnp.float32),
                pltpu.VMEM((length, width), jnp.float32),
                pltpu.VMEM((width, size), jnp.float32),
                pltpu.VMEM((size, head_count * size), jnp.bfloat16),
                pltpu.VMEM((size, head_count * size), jnp.bfloat16),
            ],
        ),
        out_shape=[jax.ShapeDtypeStruct((length, width), jnp.bfloat16)] * 3,
        compiler_params=kernel_params(),
        cost_estimate=small_cost,
        name="attend_back",
    )(with_inner(low_blocks, start_rows, size), query, key, value, grad, attended, lse, start_rows, *after)


def project_kernel(count, own_width, order_ref, *refs):
    block_refs, weight_refs, vector_ref = refs[:count], refs[count : 2 * count], refs[2 * count]
    weight_ref, plain_ref, normed_ref, q_ref, k_ref, v_ref = refs[2 * count + 1 :]
    piece = weight_refs[0].shape[0]

    @pl.when(pl.program_id(0) == 0)
    def _():
        for place in range(count):
            rows = pl.ds(pl.multiple_of(order_ref[place] * piece, piece), piece)
            weight_ref[rows, :] = weight_refs[place][:, : 3 * own_width]

    for place in range(count):

        @pl.when(pl.program_id(0) == place)
        def _():
            rows = norm_rows(block_refs[place][...].astype(jnp.float32), 1.0, 0.0)
            plain_ref[...] = rows.astype(jnp.bfloat16)
            normed = (rows * vector_ref[0:1, :] + vector_ref[1:2, :]).astype(jnp.bfloat16)
            normed_ref[...] = normed
            projected = row_dot(normed, weight_ref[...]).astype(jnp.bfloat16)
            q_ref[...] = projected[:, :own_width]
            k_ref[...] = projected[:, own_width : 2 * own_width]
            v_ref[...] = projected[:, 2 * own_width :]


def project_rows(blocks, weights, order, vectors):
    count = len(blocks)
    size, width = blocks[0].shape
    weight_rows = weights[0].shape[0]
    own_width = width // count
    whole = lambda shape: spec(shape, lambda i, order: (0, 0))
    placed = lambda columns: spec((size, columns), lambda i, order: (order[i], 0))
    return pl.pallas_call(
        functools.partial(project_kernel, count, own_width),
        grid_spec=pltpu.PrefetchScalarGridSpec(
            num_scalar_prefetch=1,
            grid=(count,),
            in_specs=[
                *[whole((size, width))] * count,
                *[whole(weights[0].shape)] * count,
                whole(vectors.shape),
            ],
            out_specs=[whole((width, 3 * own_width))]
            + [placed(width)] * 2
            + [placed(own_width)] * 3,
        ),
        out_shape=[jax.ShapeDtypeStruct((width, 3 * own_width), jnp.bfloat16)]
        + [jax.ShapeDtypeStruct((count * size, width), jnp.bfloat16)] * 2
        + [jax.ShapeDtypeStruct((count * size, own_width), jnp.bfloat16)] * 3,
        compiler_params=kernel_params(),
        cost_estimate=pl.CostEstimate(
            flops=13_000_000_000, bytes_accessed=1000, transcendentals=0
        ),
        name="project_rows",
    )(order, *blocks, *weights, vectors)


def planes_kernel(spacing, keys_ref, planes_ref, turned_ref, square_ref, wide_ref):
    near_count = keys_ref.shape[0] // spacing

    @pl.when(pl.program_id(0) == 0)
    def _():
        square_ref[...] = jnp.zeros_like(square_ref)

    wide_ref[...] = keys_ref[...].astype(jnp.float32)
    for plane in range(spacing):
        rows = slice(plane * near_count, (plane + 1) * near_count)
        keys = wide_ref[pl.ds(plane, near_count, stride=spacing), :]
        planes_ref[rows, :] = keys.astype(jnp.bfloat16)
        turned = keys.T
        turned_ref[:, rows] = turned.astype(jnp.bfloat16)
        square_ref[plane : plane + 1, :] += jnp.sum(turned * turned, axis=0, keepdims=True)


def key_planes(keys, spacing, after=()):
    count, width = keys.shape
    columns = row_chunk(width, (128,))
    near_count = count // spacing
    return pl.pallas_call(
        later(functools.partial(planes_kernel, spacing), 1, len(after)),
        grid=(width // columns,),
        in_specs=[spec((count, columns), lambda i: (0, i)), *later_specs(after)],
        out_specs=[
            spec((count, columns), lambda i: (0, i)),
            spec((columns, count), lambda i: (i, 0)),
            spec((spacing, near_count), lambda i: (0, 0)),
        ],
        out_shape=[
            jax.ShapeDtypeStruct((count, width), jnp.bfloat16),
            jax.ShapeDtypeStruct((width, count), jnp.bfloat16),
            jax.ShapeDtypeStruct((spacing, near_count), jnp.float32),
        ],
        scratch_shapes=[pltpu.VMEM((count, columns), jnp.float32)],
        compiler_params=kernel_params(),
        cost_estimate=small_cost,
        name="key_planes",
    )(keys, *after)


def near_kernel(spacing, dist_scale, parts, *refs):
    order_ref, query_ref, keys_ref, square_ref, values_ref = refs[:5]
    near_refs, target_refs = refs[5 : 5 + parts], refs[5 + parts : 5 + 2 * parts]
    e_ref, s_ref = refs[5 + 2 * parts :]
    piece, near_count = near_refs[0].shape[1:]
    rows = parts * piece
    lane = lax.broadcasted_iota(jnp.int32, (rows, near_count), 1)
    near = jnp.concatenate([ref[0] for ref in near_refs], axis=0)
    offset = near - spacing * lane
    target = jnp.concatenate([ref[0].T for ref in target_refs], axis=0)[:, 0:1]
    picked = jnp.zeros((rows, near_count), jnp.float32)
    words = jnp.full((rows, near_count), -1.0, jnp.float32)
    queries = query_ref[...]
    for plane in range(spacing):
        lanes = slice(plane * near_count, (plane + 1) * near_count)
        inner = row_dot(queries, keys_ref[:, lanes])
        chosen = offset == plane
        picked = jnp.where(chosen, 2.0 * inner - square_ref[plane : plane + 1, :], picked)
        words = jnp.where(chosen, values_ref[plane : plane + 1, :], words)
    scores = picked * dist_scale
    matched = words == target
    peak = jnp.max(scores, axis=1, keepdims=True)
    raised = jnp.exp(scores - peak)
    total = jnp.sum(raised, axis=1, keepdims=True)
    hits = jnp.sum(jnp.where(matched, raised, 0.0), axis=1, keepdims=True)
    e_ref[...] = jnp.where(matched, raised, -raised)
    stat_lane = lax.broadcasted_iota(jnp.int32, (rows, 128), 1)
    stats = jnp.where(stat_lane == 0, peak, jnp.where(stat_lane == 1, total, hits))
    for part in range(parts):
        s_ref[part] = stats[part * piece : (part + 1) * piece, :].T[: s_ref.shape[1], :]


def picked_specs(shape, parts):
    return [
        spec((1,) + shape, functools.partial(lambda part, i, order: (order[i * parts + part], 0, 0), part))
        for part in range(parts)
    ]


def near_scores(queries, keys_turned, square, values, near, target_rows, order, parts, spacing):
    stat_rows, piece = target_rows.shape[1:]
    near_count = near.shape[2]
    slot_rows = queries.shape[0]
    width, keys = keys_turned.shape
    rows = parts * piece
    return pl.pallas_call(
        functools.partial(near_kernel, spacing, width ** (-0.5), parts),
        grid_spec=pltpu.PrefetchScalarGridSpec(
            num_scalar_prefetch=1,
            grid=(slot_rows // rows,),
            in_specs=[
                spec((rows, width), lambda i, order: (i, 0)),
                spec((width, keys), lambda i, order: (0, 0)),
                spec((spacing, near_count), lambda i, order: (0, 0)),
                spec((spacing, near_count), lambda i, order: (0, 0)),
            ]
            + picked_specs((piece, near_count), parts)
            + picked_specs((stat_rows, piece), parts),
            out_specs=[
                spec((rows, near_count), lambda i, order: (i, 0)),
                spec((parts, stat_rows, piece), lambda i, order: (i, 0, 0)),
            ],
        ),
        out_shape=[
            jax.ShapeDtypeStruct((slot_rows, near_count), jnp.float32),
            jax.ShapeDtypeStruct((slot_rows // piece, stat_rows, piece), jnp.float32),
        ],
        compiler_params=kernel_params(),
        cost_estimate=small_cost,
        name="near_scores",
    )(order, queries, keys_turned, square, values, *[near] * parts, *[target_rows] * parts)


def near_back_kernel(spacing, factor, parts, *refs):
    order_ref, e_ref = refs[:2]
    near_refs, coeff_refs = refs[2 : 2 + parts], refs[2 + parts : 2 + 2 * parts]
    keys_ref, out_ref, dense_ref = refs[2 + 2 * parts :]
    piece, near_count = near_refs[0].shape[1:]
    lane = lax.broadcasted_iota(jnp.int32, (piece, near_count), 1)
    for part in range(parts):
        rows = slice(part * piece, (part + 1) * piece)
        offset = near_refs[part][0] - spacing * lane
        columns = coeff_refs[part][0].T
        coefficient, probability = columns[:, 0:1], columns[:, 1:2]
        marked = e_ref[rows, :]
        matched = jnp.where(marked > 0.0, 1.0, 0.0)
        grads = coefficient * (matched - probability) * jnp.abs(marked) * factor
        for plane in range(spacing):
            lanes = slice(plane * near_count, (plane + 1) * near_count)
            dense_ref[rows, lanes] = jnp.where(offset == plane, grads, 0.0).astype(jnp.bfloat16)
    out_ref[...] = row_dot(dense_ref[...], keys_ref[...]).astype(out_ref.dtype)


def near_back(marked, near, coeff_rows, keys_planes, order, parts, spacing, after=()):
    stat_rows, piece = coeff_rows.shape[1:]
    slot_rows, near_count = marked.shape
    keys, width = keys_planes.shape
    rows = parts * piece
    return pl.pallas_call(
        later(
            functools.partial(near_back_kernel, spacing, 2.0 * width ** (-0.5), parts),
            3 + 2 * parts,
            len(after),
        ),
        grid_spec=pltpu.PrefetchScalarGridSpec(
            num_scalar_prefetch=1,
            grid=(slot_rows // rows,),
            in_specs=[spec((rows, near_count), lambda i, order: (i, 0))]
            + picked_specs((piece, near_count), parts)
            + picked_specs((stat_rows, piece), parts)
            + [spec((keys, width), lambda i, order: (0, 0))]
            + later_specs(after),
            out_specs=spec((rows, width), lambda i, order: (i, 0)),
            scratch_shapes=[pltpu.VMEM((rows, keys), jnp.bfloat16)],
        ),
        out_shape=jax.ShapeDtypeStruct((slot_rows, width), jnp.bfloat16),
        compiler_params=kernel_params(),
        cost_estimate=small_cost,
        name="near_back",
    )(order, marked, *[near] * parts, *[coeff_rows] * parts, keys_planes, *after)


def pack_kernel(options, pick_ref, *refs):
    row_refs, (map_ref, out_ref, chosen_ref) = refs[:options], refs[options:]
    owners, capacity = out_ref.shape[:2]
    tokens = map_ref.shape[1]

    @pl.when(pl.program_id(0) == 0)
    def _():
        slot = lax.broadcasted_iota(jnp.int32, (capacity, tokens), 0)
        for owner in range(owners):
            chosen = jnp.where(map_ref[owner : owner + 1, :] == slot, 1.0, 0.0)
            chosen_ref[owner * capacity : (owner + 1) * capacity, :] = chosen.astype(jnp.bfloat16)

    rows = row_refs[0][...]
    for place in range(1, options):
        rows = jnp.where(pick_ref[0] == place, row_refs[place][...], rows)
    packed = row_dot(chosen_ref[...], rows).astype(out_ref.dtype)
    out_ref[...] = packed.reshape(out_ref.shape)


def pack_rows(options, pick, slot_map, capacity, after=()):
    owners, tokens = slot_map.shape
    width = options[0].shape[1]
    columns = row_chunk(width, (256,))
    return pl.pallas_call(
        later(functools.partial(pack_kernel, len(options)), 2 + len(options), len(after)),
        grid_spec=pltpu.PrefetchScalarGridSpec(
            num_scalar_prefetch=1,
            grid=(width // columns,),
            in_specs=[
                *[spec((tokens, columns), lambda i, pick: (0, i))] * len(options),
                spec((owners, tokens), lambda i, pick: (0, 0)),
                *later_specs(after),
            ],
            out_specs=spec((owners, capacity, columns), lambda i, pick: (0, 0, i)),
            scratch_shapes=[pltpu.VMEM((owners * capacity, tokens), jnp.bfloat16)],
        ),
        out_shape=jax.ShapeDtypeStruct((owners, capacity, width), options[0].dtype),
        compiler_params=kernel_params(),
        cost_estimate=pl.CostEstimate(
            flops=30_000_000_000, bytes_accessed=1000, transcendentals=0
        ),
        name="pack_rows",
    )(pick, *options, slot_map, *after)


def unpack_kernel(back_ref, column_ref, out_ref, chosen_ref):
    owners, capacity, columns = back_ref.shape
    tokens = out_ref.shape[0]

    @pl.when(pl.program_id(0) == 0)
    def _():
        slot = lax.broadcasted_iota(jnp.int32, (capacity, tokens), 0)
        for owner in range(owners):
            chosen = jnp.where(column_ref[owner : owner + 1, :] == slot, 1.0, 0.0)
            chosen_ref[owner * capacity : (owner + 1) * capacity, :] = chosen.astype(jnp.bfloat16)

    back = back_ref[...].reshape(owners * capacity, columns)
    out_ref[...] = left_dot(chosen_ref[...], back).astype(out_ref.dtype)


def unpack_rows(returned, slot_map, kind, after=()):
    owners, capacity, width = returned.shape
    tokens = slot_map.shape[1]
    columns = row_chunk(width, (256,))
    return pl.pallas_call(
        later(unpack_kernel, 2, len(after)),
        grid=(width // columns,),
        in_specs=[
            spec((owners, capacity, columns), lambda i: (0, 0, i)),
            spec((owners, tokens), lambda i: (0, 0)),
            *later_specs(after),
        ],
        out_specs=spec((tokens, columns), lambda i: (0, i)),
        out_shape=jax.ShapeDtypeStruct((tokens, width), kind),
        scratch_shapes=[pltpu.VMEM((owners * capacity, tokens), jnp.bfloat16)],
        compiler_params=kernel_params(),
        cost_estimate=small_cost,
        name="unpack_rows",
    )(returned, slot_map, *after)


def mix_kernel(stats_ref, map_ref, prob_ref, loss_ref, send_ref, peak_ref, total_ref, hits_ref):
    owners, stat_rows, capacity = stats_ref.shape
    tokens = map_ref.shape[1]
    slot = lax.broadcasted_iota(jnp.int32, (capacity, tokens), 0)
    for owner in range(owners):
        chosen = map_ref[owner : owner + 1, :] == slot
        columns = stats_ref[owner].T
        for place, target in enumerate((peak_ref, total_ref, hits_ref)):
            target[owner : owner + 1, :] = jnp.sum(
                jnp.where(chosen, columns[:, place : place + 1], 0.0), axis=0, keepdims=True
            )
    member = map_ref[...] >= 0
    peaks = jnp.where(member, peak_ref[...], -3e38)
    best = jnp.max(peaks, axis=0, keepdims=True)
    rescale = jnp.where(member, jnp.exp(peaks - best), 0.0)
    knn_total = jnp.sum(total_ref[...] * rescale, axis=0, keepdims=True)
    knn_prob = jnp.sum(hits_ref[...] * rescale, axis=0, keepdims=True) / knn_total
    mixture = mix_weight * knn_prob + (1.0 - mix_weight) * prob_ref[...]
    loss_ref[...] = -jnp.log(mixture)
    peak_ref[...] = (-mix_weight / (mixture * knn_total)) * rescale
    for owner in range(owners):
        chosen = map_ref[owner : owner + 1, :] == slot
        coefficient = jnp.sum(
            jnp.where(chosen, peak_ref[owner : owner + 1, :], 0.0), axis=1, keepdims=True
        )
        probability = jnp.sum(jnp.where(chosen, knn_prob, 0.0), axis=1, keepdims=True)
        lane = lax.broadcasted_iota(jnp.int32, (capacity, 128), 1)
        both = jnp.where(lane == 0, coefficient, probability)
        send_ref[owner] = both.T[:stat_rows, :]


def mix_losses(stats, slot_map, model_prob):
    owners, stat_rows, capacity = stats.shape
    tokens = slot_map.shape[1]
    vmem = pl.BlockSpec(memory_space=pltpu.VMEM)
    return pl.pallas_call(
        mix_kernel,
        in_specs=[vmem] * 3,
        out_specs=[vmem] * 2,
        out_shape=[
            jax.ShapeDtypeStruct((1, tokens), jnp.float32),
            jax.ShapeDtypeStruct(stats.shape, jnp.float32),
        ],
        scratch_shapes=[pltpu.VMEM((owners, tokens), jnp.float32)] * 3,
        compiler_params=pltpu.CompilerParams(vmem_limit_bytes=vmem_limit),
        name="mix_losses",
    )(stats, slot_map, model_prob)


def row_chunk(total, choices):
    for choice in choices:
        if total % choice == 0:
            return choice
    return total


def slot_picker(slot_map, capacity):
    return slot_map[:, None, :] == jnp.arange(capacity, dtype=jnp.int32)[None, :, None]


def layer_table(count):
    return [
        sorted(range(count), key=lambda other: (abs(other - layer), (other ^ layer) != 1, other))
        for layer in range(count)
    ]


def own_choice(options):
    layer = lax.axis_index("batch")
    kept = options[0]
    for place in range(1, len(options)):
        if all(options[place] is not other for other in options[:place]):
            same = [i for i, other in enumerate(options) if other is options[place]]
            here = functools.reduce(jnp.logical_or, [layer == i for i in same])
            kept = jnp.where(here, options[place], kept)
    return kept


def layer_step(step, ups, downs):
    options, picks = [], []
    for layer, line in enumerate(layer_table(lax.axis_size("batch"))):
        there = line[step]
        block = ups[layer - there] if there < layer else downs[there - layer]
        places = [place for place, other in enumerate(options) if other is block]
        if not places:
            options.append(block)
        picks.append(places[0] if places else len(options) - 1)
    return options, jnp.array(picks, jnp.int32)[lax.axis_index("batch")][None]


def layer_hop(hop, blocks, above, below):
    count = lax.axis_size("batch")
    reach = count - hop
    table = layer_table(count)

    def bound(layer, to):
        return blocks[table[layer].index(to) if 0 <= to < count else hop_step]

    hop_step = reach
    up = own_choice([bound(layer, layer + reach) for layer in range(count)])
    down = own_choice([bound(layer, layer - reach) for layer in range(count)])
    if hop > 1:
        up = (up.astype(jnp.float32) + above).astype(up.dtype)
        down = (down.astype(jnp.float32) + below).astype(down.dtype)
    return (
        lax.ppermute(up, "batch", [(i, i + 1) for i in range(hop)]),
        lax.ppermute(down, "batch", [(i, i - 1) for i in range(reach, count)]),
    )


def across(rows, step):
    return lax.ppermute(rows, "ctx", [(i, i ^ step) for i in range(lax.axis_size("ctx"))])


def in_ctx_order(parts):
    count = len(parts)
    own = lax.axis_index("ctx")
    stacked = jnp.stack(parts)
    return stacked[jnp.arange(count, dtype=jnp.int32) ^ own]


def ctx_gather(rows):
    return in_ctx_order([rows] + [across(rows, step) for step in range(1, lax.axis_size("ctx"))])


def swap_cores(rows):
    return lax.ppermute(rows, "rep", [(0, 1), (1, 0)])


def reduce_cores(grad):
    count = lax.axis_size("ctx")
    parts = grad.astype(jnp.bfloat16).reshape(count, 2, grad.shape[0] // (2 * count), grad.shape[1])
    core = lax.axis_index("rep")
    keep = lax.dynamic_index_in_dim(parts, core, 1, keepdims=False)
    send = lax.dynamic_index_in_dim(parts, 1 - core, 1, keepdims=False)
    return (keep.astype(jnp.float32) + swap_cores(send)).astype(jnp.bfloat16)


def ctx_trade(blocks):
    return [part if step == 0 else across(part, step) for step, part in enumerate(blocks)]


def exchange(blocks, axis):
    return lax.all_to_all(blocks, axis, split_axis=0, concat_axis=0, tiled=True)


def block_sum(blocks):
    total = blocks[0].astype(jnp.float32)
    for place in range(1, len(blocks)):
        total = total + blocks[place].astype(jnp.float32)
    return total


def ctx_reduce(halves):
    return lax.psum_scatter(halves, "ctx", scatter_dimension=0)


def layer_total(blocks):
    return block_sum(exchange(blocks, "batch")).astype(jnp.bfloat16)


def layer_blocks(rows):
    return rows.reshape(lax.axis_size("batch"), -1, rows.shape[1])


def both_halves(half):
    other = swap_cores(half)
    first = lax.axis_index("rep") == 0
    both = jnp.stack([jnp.where(first, half, other), jnp.where(first, other, half)])
    return both.reshape(-1, half.shape[-1]).astype(jnp.float32)


def layer_gather(rows):
    count = lax.axis_size("batch")
    return [rows] + [
        lax.ppermute(rows, "batch", [(i, (i + hops) % count) for i in range(count)])
        for hops in range(1, count)
    ]


def whole_shard(parts):
    count, layer = len(parts), lax.axis_index("batch")
    return both_halves(jnp.stack(parts)[(layer - jnp.arange(count, dtype=jnp.int32)) % count])


def mix_any(stats, slot_map, model_prob):
    owners, stat_rows, capacity = stats.shape
    if capacity % 16 == 0:
        return mix_losses(stats, slot_map, model_prob)
    chosen = slot_picker(slot_map, capacity)
    peak, total, hits = [
        jnp.sum(jnp.where(chosen, stats[:, row, :, None], 0.0), axis=1) for row in range(3)
    ]
    member = slot_map >= 0
    peaks = jnp.where(member, peak, -3e38)
    best = jnp.max(peaks, axis=0, keepdims=True)
    rescale = jnp.where(member, jnp.exp(peaks - best), 0.0)
    knn_total = jnp.sum(total * rescale, axis=0, keepdims=True)
    knn_prob = jnp.sum(hits * rescale, axis=0, keepdims=True) / knn_total
    mixture = mix_weight * knn_prob + (1.0 - mix_weight) * model_prob
    coefficient = (-mix_weight / (mixture * knn_total)) * rescale
    sent = [
        jnp.sum(jnp.where(chosen, part[:, None, :], 0.0), axis=2)
        for part in (coefficient, jnp.broadcast_to(knn_prob, coefficient.shape))
    ]
    sent = jnp.stack(sent + [sent[1]] * (stat_rows - 2), axis=1)
    return -jnp.log(mixture), sent


def local(
    tokens,
    cotangent,
    segment_ids,
    first_gain,
    first_shift,
    second_gain,
    second_shift,
    final_gain,
    final_shift,
    project_weight,
    output_weight,
    upward_weight,
    downward_weight,
    store_keys,
    store_values,
    owners,
    neighbours,
    targets,
    model_prob,
):
    head_count = HEADS
    group_seqs, block_len, width = tokens.shape
    seq_len = segment_ids.shape[1]
    ctx_count = lax.axis_size("ctx")
    shard_count = lax.axis_size("batch") * ctx_count
    capacity = neighbours.shape[3]
    near_count = neighbours.shape[4]
    top_count = owners.shape[2]
    key_count = store_keys.shape[0]
    spacing = key_count // near_count
    slot_rows = shard_count * capacity
    everyone = ("batch", "ctx")
    own_heads = head_count // ctx_count
    own_width = width // ctx_count
    attend_size = row_chunk(seq_len, (256, 128))

    arrived = [tokens[0]] + [across(tokens[0], step) for step in range(1, ctx_count)]
    own_rows = project_weight.shape[0]
    own_ctx = lax.axis_index("ctx")
    vectors = jnp.stack(
        [first_gain, first_shift, second_gain, second_shift, final_gain, final_shift], axis=1
    )
    vectors = jnp.pad(vectors, ((0, 0), (0, 128 - vectors.shape[1])))
    proj_pieces = [
        jnp.concatenate(
            [
                lax.dynamic_slice_in_dim(
                    project_weight, part * width + (own_ctx ^ step) * own_width, own_width, 1
                )
                for part in range(3)
            ]
            + [vectors],
            axis=1,
        )
        for step in range(ctx_count)
    ]
    proj_pieces = ctx_trade(proj_pieces)
    vectors = in_ctx_order([piece[:, 3 * own_width :] for piece in proj_pieces])
    vectors = vectors.reshape(width, -1)[:, :6].T.astype(jnp.float32)
    gain_list = [vectors[row] for row in range(6)]

    member = jnp.any(
        owners[0][:, :, None] == jnp.arange(shard_count, dtype=jnp.int32)[None, None, :], axis=1
    )
    place = jnp.arange(block_len, dtype=jnp.int32)
    earlier = (place[:, None] <= place[None, :]).astype(jnp.bfloat16)
    running = left_dot(member.astype(jnp.bfloat16), earlier).astype(jnp.int32)
    slot_map = jnp.where(member.T, running - 1, -1)
    send_targets = jnp.sum(
        jnp.where(slot_picker(slot_map, capacity), targets.reshape(1, 1, -1), 0), axis=2
    )
    got_targets = exchange(send_targets.astype(jnp.int32), everyone).astype(jnp.float32)
    value_planes = store_values.astype(jnp.float32).reshape(near_count, spacing).T
    by_layer = capacity % 16 == 0
    if by_layer:
        piece, parts = capacity, 2 if ctx_count % 2 == 0 else 1
        layer_count = lax.axis_size("batch")
        maps = exchange(slot_map.reshape(layer_count, ctx_count, block_len), "batch")
        table = jnp.array(layer_table(layer_count), jnp.int32)[lax.axis_index("batch")]
        maps = maps[table]
        orders = table[:, None] * ctx_count + jnp.arange(ctx_count, dtype=jnp.int32)[None, :]
    else:
        piece, parts = row_chunk(slot_rows, (576, 512, 384, 256, 128)), 1
        orders = jnp.arange(slot_rows // piece, dtype=jnp.int32)[None, :]
        chosen_slots = slot_picker(slot_map, capacity).astype(jnp.bfloat16)
    near_table = neighbours.reshape(slot_rows // piece, piece, near_count)
    stat_shape = (slot_rows // piece, 8, piece)
    target_rows = jnp.broadcast_to(got_targets.reshape(stat_shape[0], 1, piece), stat_shape)

    early = proj_pieces[1:]
    core = lax.axis_index("rep")

    def own_half(weight):
        half = weight.shape[0] // 2
        mine = lax.dynamic_slice_in_dim(weight, core * half, half, 0)
        return run_after([mine], [*arrived[1:], *early])[0]

    def gather_weight(weight):
        return lax.all_gather(own_half(weight), ("ctx", "rep"), axis=0, tiled=True)

    out_full = gather_weight(output_weight)
    down_full = gather_weight(downward_weight)
    up_half = own_half(upward_weight)
    up_pieces = [across(up_half, step) for step in range(1, ctx_count)]
    sources = own_ctx ^ jnp.arange(ctx_count, dtype=jnp.int32)

    segments = segment_ids[0]
    start_rows = jnp.sum((segments[None, :] < segments[:, None]).astype(jnp.int32), axis=1)
    low_blocks = start_rows[::attend_size] // attend_size
    start_rows = jnp.broadcast_to(start_rows[None, :], (8, seq_len))
    proj_own, plain_full, normed_full, query_own, key_own, value_own = project_rows(
        arrived, proj_pieces, sources, vectors
    )
    attended_own, log_total = attend(
        query_own, key_own, value_own, start_rows, low_blocks, own_heads, attend_size
    )
    attended = lax.all_to_all(attended_own, "ctx", split_axis=0, concat_axis=1, tiled=True)
    attended = run_after([attended], [target_rows, maps] if by_layer else [target_rows])[0]
    up_pieces = [up_half, *run_after(up_pieces, [attended])]
    up_full = place_rows(
        up_pieces + [swap_cores(piece) for piece in up_pieces],
        jnp.concatenate([2 * sources + core, 2 * sources + 1 - core]),
    )
    inputs = tokens[0].astype(jnp.float32)
    hidden = inputs + row_dot(attended, out_full)
    normed_two = norm_rows(hidden, gain_list[2], gain_list[3]).astype(jnp.bfloat16)
    upper_rows = row_dot(normed_two, up_full)
    active = jax.nn.gelu(upper_rows).astype(jnp.bfloat16)
    summed = hidden + row_dot(active, down_full)
    final_rows = norm_rows(summed, gain_list[4], gain_list[5]).astype(jnp.bfloat16)

    if by_layer:
        ups, downs, packed, queries = [final_rows], [final_rows], [], []
        for step in range(layer_count):
            hop = step + 1
            if hop < layer_count:
                up, down = ups[-1], downs[-1]
                if hop == 2:
                    up, down = run_after([up, down], packed)
                    ups[-1], downs[-1] = up, down
                elif hop > 2:
                    up, down = run_after([up, down], [queries[hop - 3]])
                    ups[-1], downs[-1] = up, down
                ups.append(
                    lax.ppermute(up, "batch", [(i, i + 1) for i in range(step, layer_count - 1)])
                )
                downs.append(
                    lax.ppermute(down, "batch", [(i, i - 1) for i in range(1, layer_count - step)])
                )
            options, pick = layer_step(step, ups, downs)
            between = ()
            if step == 1:
                between = planes, planes_turned, key_square = key_planes(
                    store_keys, spacing, packed
                )
            packed.append(pack_rows(options, pick, maps[step], capacity, between))
            queries.append(exchange(packed[step], "ctx").reshape(-1, width))
    else:
        planes, planes_turned, key_square = key_planes(store_keys, spacing)
        packed = jnp.einsum(
            "ost,tw->osw", chosen_slots, final_rows, preferred_element_type=jnp.float32
        )
        queries = [exchange(packed.astype(jnp.bfloat16), everyone).reshape(slot_rows, width)]
    marked, stats = zip(
        *[
            near_scores(
                rows,
                planes_turned,
                key_square,
                value_planes,
                near_table,
                target_rows,
                orders[step],
                parts,
                spacing,
            )
            for step, rows in enumerate(queries)
        ]
    )
    if by_layer:
        inverse = jnp.argmin(
            jnp.abs(table[None, :] - jnp.arange(layer_count, dtype=jnp.int32)[:, None]), axis=1
        )
        stats = jnp.stack(stats)[inverse].reshape(stat_shape)
    else:
        stats = stats[0].transpose(1, 0, 2).reshape(8, shard_count, capacity).transpose(1, 0, 2)
    token_loss, send_coeff = mix_any(exchange(stats, everyone), slot_map, model_prob)
    got_coeff = exchange(send_coeff, everyone)
    if not by_layer:
        got_coeff = got_coeff.transpose(1, 0, 2).reshape(8, -1, piece).transpose(1, 0, 2)
    if by_layer:
        returned, above, below = {}, None, None
        for step in reversed(range(layer_count)):
            hop = layer_count - 1 - step
            partial_grad = near_back(
                marked[step],
                near_table,
                got_coeff,
                planes,
                orders[step],
                parts,
                spacing,
                [returned[step + 2]] if hop >= 2 else [],
            )
            back = exchange(partial_grad.reshape(ctx_count, capacity, width), "ctx")
            if hop > 0:
                above, below = layer_hop(hop, returned, above, below)
            returned[step] = unpack_rows(
                back,
                maps[step],
                jnp.bfloat16 if step > 0 else jnp.float32,
                [above, below] if 0 < hop < layer_count - 1 else [],
            )
        query_grad = returned[0] + above.astype(jnp.float32) + below.astype(jnp.float32)
    else:
        partial_grad = near_back(
            marked[0], near_table, got_coeff, planes, orders[0], parts, spacing
        )
        back = exchange(partial_grad.reshape(shard_count, capacity, width), everyone)
        query_grad = jnp.einsum(
            "ost,osw->tw", chosen_slots, back, preferred_element_type=jnp.float32
        )

    out_grad = cotangent[0].astype(jnp.float32) + query_grad
    final_vjp = jax.vjp(norm_rows, summed, gain_list[4], gain_list[5])[1]
    summed_grad, final_gain_grad, final_shift_grad = final_vjp(out_grad)
    branch_grad = summed_grad.astype(jnp.bfloat16)
    downward_grad = left_dot(active, branch_grad)
    active_grad = right_dot(branch_grad, down_full)
    gelu_vjp = jax.vjp(jax.nn.gelu, upper_rows)[1]
    upper_grad = gelu_vjp(active_grad)[0].astype(jnp.bfloat16)
    downward_half = reduce_cores(downward_grad)
    upper_grad = run_after([upper_grad], [downward_half])[0]
    second_vjp = jax.vjp(norm_rows, hidden, gain_list[2], gain_list[3])[1]
    hidden_part, second_gain_grad, second_shift_grad = second_vjp(right_dot(upper_grad, up_full))
    hidden_grad = summed_grad + hidden_part
    attn_grad = hidden_grad.astype(jnp.bfloat16)
    attended_grad = right_dot(attn_grad, out_full).astype(jnp.bfloat16)
    downward_half = ctx_reduce(downward_half)
    second_half = reduce_cores(
        jnp.concatenate(
            [
                left_dot(normed_two, upper_grad).astype(jnp.bfloat16),
                left_dot(attended, attn_grad).astype(jnp.bfloat16),
            ],
            axis=1,
        )
    )
    attended_grad = run_after([attended_grad], [downward_half])[0]
    grad_own = lax.all_to_all(attended_grad, "ctx", split_axis=1, concat_axis=0, tiled=True)
    second_half = run_after([second_half], [grad_own])[0]
    downward_half = run_after([downward_half], [second_half])[0]
    downward_total = layer_total(layer_blocks(downward_half))
    second_start = second_half
    second_half = ctx_reduce(second_half)
    proj_grad = jnp.concatenate(
        run_after(
            attend_back(
                query_own,
                key_own,
                value_own,
                grad_own,
                attended_own,
                log_total,
                start_rows,
                low_blocks,
                own_heads,
                attend_size,
                (second_start, downward_half),
            ),
            [downward_total],
        ),
        axis=1,
    )
    normed_terms = right_dot(proj_grad, proj_own).astype(jnp.bfloat16)
    normed_grad = lax.psum_scatter(normed_terms, "ctx", scatter_dimension=0, tiled=True)

    second_half = run_after([second_half], [normed_terms])[0]
    second_total = layer_total(layer_blocks(second_half))
    second_parts = layer_gather(second_total)
    plain_part = left_dot(plain_full, proj_grad)
    column_sums = jnp.sum(proj_grad.astype(jnp.float32), axis=0)
    proj_full = proj_own.astype(jnp.float32)
    first_gain_grad = jnp.sum(plain_part * proj_full, axis=1)
    first_shift_grad = jnp.sum(column_sums[None, :] * proj_full, axis=1)
    project_part = plain_part * gain_list[0][:, None] + column_sums[None, :] * gain_list[1][:, None]

    vector_part = jnp.stack(
        [
            first_gain_grad,
            first_shift_grad,
            second_gain_grad,
            second_shift_grad,
            final_gain_grad,
            final_shift_grad,
        ],
        axis=1,
    )
    vector_part = jnp.pad(vector_part, ((0, 0), (0, 128 - vector_part.shape[1])))
    project_part = jnp.concatenate([project_part, vector_part], axis=1).astype(jnp.bfloat16)
    project_part = reduce_cores(run_after([project_part], [second_total])[0])
    downward_parts = layer_gather(run_after([downward_total], [project_part])[0])
    project_part = in_ctx_order(
        ctx_trade(
            [
                lax.dynamic_index_in_dim(project_part, own_ctx ^ step, 0, keepdims=False)
                for step in range(ctx_count)
            ]
        )
    )
    vector_part = block_sum(project_part[:, :, 3 * own_width :]).astype(jnp.bfloat16)
    project_part = (
        project_part[:, :, : 3 * own_width]
        .reshape(ctx_count, own_rows // 2, 3, own_width)
        .transpose(1, 2, 0, 3)
        .reshape(own_rows // 2, 3 * width)
    )
    small_rows = jnp.concatenate([project_part, vector_part], axis=1)
    small_rows = run_after([small_rows], second_parts[1:])[0]
    small_total = layer_total(layer_blocks(small_rows))
    input_vjp = jax.vjp(lambda rows: norm_rows(rows, gain_list[0], gain_list[1]), inputs)[1]
    normed_grad = run_after([normed_grad], [small_total])[0]
    input_grad = hidden_grad + input_vjp(normed_grad.astype(jnp.float32))[0]
    small_grads = whole_shard(layer_gather(small_total))
    second_grads = whole_shard(second_parts)
    weight_grads = [
        small_grads[:, : 3 * width],
        second_grads[:, second_grads.shape[1] - width :],
        second_grads[:, : second_grads.shape[1] - width],
        whole_shard(downward_parts),
    ]
    vector_grads = small_grads[:, 3 * width : 3 * width + 6].T
    return (
        final_rows.reshape(group_seqs, block_len, width),
        token_loss.reshape(group_seqs, block_len),
        query_grad.reshape(group_seqs, block_len, width),
        input_grad.reshape(group_seqs, block_len, width),
        *weight_grads,
        *[vector_grads[row] for row in range(6)],
    )


def solution(mesh):
    placed = (
        P(("rep", "batch"), "ctx", None),
        P(("rep", "batch"), "ctx", None),
        P(("rep", "batch"), None),
        P("ctx"),
        P("ctx"),
        P("ctx"),
        P("ctx"),
        P("ctx"),
        P("ctx"),
        P("ctx", None),
        P("ctx", None),
        P("ctx", None),
        P("ctx", None),
        P(("batch", "ctx"), None),
        P(("batch", "ctx")),
        P(("rep", "batch"), "ctx", None),
        P("rep", ("batch", "ctx"), None, None, None),
        P(("rep", "batch"), "ctx"),
        P(("rep", "batch"), "ctx"),
    )
    return jax.shard_map(
        local,
        mesh=mesh,
        in_specs=placed,
        out_specs=(
            P(("rep", "batch"), "ctx", None),
            P(("rep", "batch"), "ctx"),
            P(("rep", "batch"), "ctx", None),
            P(("rep", "batch"), "ctx", None),
            P("ctx", None),
            P("ctx", None),
            P("ctx", None),
            P("ctx", None),
            P("ctx"),
            P("ctx"),
            P("ctx"),
            P("ctx"),
            P("ctx"),
            P("ctx"),
        ),
        check_vma=False,
    )
```

```python
import functools

import jax
import jax.numpy as jnp
from jax import lax
from jax.experimental import pallas as pl
from jax.experimental.pallas import tpu as pltpu
from jax.sharding import PartitionSpec as P

HEADS = 16


norm_eps = 1e-05
mix_weight = 0.25
masked_value = -1e30
vmem_limit = 60 * 1024 * 1024
small_cost = pl.CostEstimate(flops=1000, bytes_accessed=1000, transcendentals=0)


def norm_rows(values, scale_gain, shift_term):
    average = jnp.mean(values, axis=-1, keepdims=True)
    centred = values - average
    spread = jnp.mean(centred * centred, axis=-1, keepdims=True)
    return centred * lax.rsqrt(spread + norm_eps) * scale_gain + shift_term


def row_dot(left_side, right_side):
    return jnp.dot(left_side, right_side, preferred_element_type=jnp.float32)


def left_dot(left_side, right_side):
    return lax.dot_general(
        left_side, right_side, (((0,), (0,)), ((), ())), preferred_element_type=jnp.float32
    )


def right_dot(left_side, right_side):
    return lax.dot_general(
        left_side, right_side, (((1,), (1,)), ((), ())), preferred_element_type=jnp.float32
    )


def spec(shape, index_map):
    return pl.BlockSpec(shape, index_map)


def kernel_params(dims=1):
    return pltpu.CompilerParams(
        vmem_limit_bytes=vmem_limit, dimension_semantics=("arbitrary",) * dims
    )


def later(kernel, place, count):
    return lambda *refs: kernel(*refs[:place], *refs[place + count :])


def later_specs(after):
    return [pl.BlockSpec(memory_space=pl.ANY)] * len(after)


def run_after(arrays, after):
    def kernel(*refs):
        pass

    return pl.pallas_call(
        kernel,
        in_specs=later_specs((*arrays, *after)),
        out_specs=later_specs(arrays),
        out_shape=[jax.ShapeDtypeStruct(rows.shape, rows.dtype) for rows in arrays],
        input_output_aliases={place: place for place in range(len(arrays))},
        cost_estimate=small_cost,
        name="run_after",
    )(*arrays, *after)


def place_kernel(count, start_ref, *refs):
    rows = refs[0].shape[0]
    for place in range(count):
        there = pl.ds(pl.multiple_of(start_ref[place] * rows, rows), rows)
        refs[count][there, :] = refs[place][...]


def place_rows(pieces, places):
    count = len(pieces)
    rows, width = pieces[0].shape
    columns = row_chunk(width, (512, 256, 128))
    return pl.pallas_call(
        functools.partial(place_kernel, count),
        grid_spec=pltpu.PrefetchScalarGridSpec(
            num_scalar_prefetch=1,
            grid=(width // columns,),
            in_specs=[spec((rows, columns), lambda i, places: (0, i))] * count,
            out_specs=spec((count * rows, columns), lambda i, places: (0, i)),
        ),
        out_shape=jax.ShapeDtypeStruct((count * rows, width), pieces[0].dtype),
        compiler_params=kernel_params(),
        cost_estimate=small_cost,
        name="place_rows",
    )(places, *pieces)


def head_rows(head, size):
    return slice(head * size, (head + 1) * size)


def masked_heads(block, head_count, axis):
    size = block.shape[axis] // head_count
    index = lax.broadcasted_iota(jnp.int32, block.shape, axis) // size
    zero = jnp.zeros((), block.dtype)
    return [jnp.where(index == head, block, zero) for head in range(head_count)]


def block_mask(key_block, query_block, size, start_row):
    key_pos = key_block * size + lax.broadcasted_iota(jnp.int32, (size, size), 0)
    query_pos = query_block * size + lax.broadcasted_iota(jnp.int32, (size, size), 1)
    return (key_pos <= query_pos) & (key_pos >= start_row)


def attend_kernel(
    head_count, low_ref, q_ref, k_ref, v_ref, start_ref, o_ref, lse_ref, vt_ref, acc_ref
):
    step = pl.program_id(0)
    size, width = q_ref.shape
    head_size = width // head_count
    blocks = k_ref.shape[0] // size

    @pl.when(step == 0)
    def _():
        for block in range(blocks):
            rows = slice(block * size, (block + 1) * size)
            vt_ref[:, rows] = v_ref[rows, :].astype(jnp.float32).T.astype(jnp.bfloat16)

    scaled = q_ref[...].astype(jnp.float32) * (head_size ** (-0.5))
    turned = jnp.concatenate(
        [part.astype(jnp.bfloat16) for part in masked_heads(scaled.T, head_count, 0)], axis=1
    )
    start_row = start_ref[0:1, :]
    acc_ref[...] = jnp.zeros_like(acc_ref)
    first = (
        jnp.full((1, head_count * size), masked_value, jnp.float32),
        jnp.zeros((1, head_count * size), jnp.float32),
    )

    def body(masked, block, state):
        peak, total = state
        rows = pl.ds(pl.multiple_of(block * size, size), size)
        scores = row_dot(k_ref[rows, :], turned)
        if masked:
            allowed = block_mask(block, step, size, start_row)
            scores = jnp.concatenate(
                [
                    jnp.where(allowed, scores[:, head * size : (head + 1) * size], masked_value)
                    for head in range(head_count)
                ],
                axis=1,
            )
        new_peak = jnp.maximum(peak, jnp.max(scores, axis=0, keepdims=True))
        fade = jnp.exp(peak - new_peak)
        weights = jnp.exp(scores - new_peak)
        total = total * fade + jnp.sum(weights, axis=0, keepdims=True)
        weights = weights.astype(jnp.bfloat16)
        for head in range(head_count):
            part = head_rows(head, head_size)
            lanes = slice(head * size, (head + 1) * size)
            acc_ref[part, :] = acc_ref[part, :] * fade[:, lanes] + row_dot(
                vt_ref[part, rows], weights[:, lanes]
            )
        return new_peak, total

    low = low_ref[step]
    inner = low_ref[blocks + step]
    state = lax.fori_loop(low, inner, functools.partial(body, True), first)
    state = lax.fori_loop(inner, step, functools.partial(body, False), state)
    peak, total = body(True, step, state)
    for head in range(head_count):
        part = head_rows(head, head_size)
        lanes = slice(head * size, (head + 1) * size)
        acc_ref[part, :] = acc_ref[part, :] / total[:, lanes]
        lse_ref[head : head + 1, :] = peak[:, lanes] + jnp.log(total[:, lanes])
    o_ref[...] = acc_ref[...].T.astype(jnp.bfloat16)


def with_inner(low_blocks, start_rows, size):
    last = start_rows[0, size - 1 :: size]
    inner = jnp.minimum(-(-last // size), jnp.arange(low_blocks.shape[0], dtype=jnp.int32))
    return jnp.concatenate([low_blocks, inner])


def attend(query, key, value, start_rows, low_blocks, head_count, size, after=()):
    length, width = query.shape
    blocks = length // size
    stat_rows = -(-head_count // 8) * 8
    return pl.pallas_call(
        later(functools.partial(attend_kernel, head_count), 5, len(after)),
        grid_spec=pltpu.PrefetchScalarGridSpec(
            num_scalar_prefetch=1,
            grid=(blocks,),
            in_specs=[
                spec((size, width), lambda i, low: (i, 0)),
                spec((length, width), lambda i, low: (0, 0)),
                spec((length, width), lambda i, low: (0, 0)),
                spec((8, size), lambda i, low: (0, i)),
                *later_specs(after),
            ],
            out_specs=[
                spec((size, width), lambda i, low: (i, 0)),
                spec((stat_rows, size), lambda i, low: (0, i)),
            ],
            scratch_shapes=[
                pltpu.VMEM((width, length), jnp.bfloat16),
                pltpu.VMEM((width, size), jnp.float32),
            ],
        ),
        out_shape=[
            jax.ShapeDtypeStruct((length, width), jnp.bfloat16),
            jax.ShapeDtypeStruct((stat_rows, length), jnp.float32),
        ],
        compiler_params=kernel_params(),
        cost_estimate=pl.CostEstimate(
            flops=20_000_000_000, bytes_accessed=1000, transcendentals=0
        ),
        name="attend",
    )(with_inner(low_blocks, start_rows, size), query, key, value, start_rows, *after)


def attend_back_kernel(
    head_count,
    low_ref,
    q_ref,
    k_ref,
    v_ref,
    grad_ref,
    o_ref,
    lse_ref,
    start_ref,
    dq_ref,
    dk_ref,
    dv_ref,
    kt_ref,
    dkey_ref,
    dvalue_ref,
    dqt_ref,
    score_ref,
    weight_ref,
):
    step = pl.program_id(0)
    size, width = q_ref.shape
    head_size = width // head_count
    score_scale = head_size ** (-0.5)
    blocks = k_ref.shape[0] // size

    @pl.when(step == 0)
    def _():
        dkey_ref[...] = jnp.zeros_like(dkey_ref)
        dvalue_ref[...] = jnp.zeros_like(dvalue_ref)
        for block in range(blocks):
            rows = slice(block * size, (block + 1) * size)
            kt_ref[:, rows] = k_ref[rows, :].astype(jnp.float32).T.astype(jnp.bfloat16)

    scaled = q_ref[...].astype(jnp.float32) * score_scale
    grads = grad_ref[...].astype(jnp.float32)
    dots = (grads * o_ref[...].astype(jnp.float32)).T
    query_turned = [p.astype(jnp.bfloat16) for p in masked_heads(scaled.T, head_count, 0)]
    grad_turned = [p.astype(jnp.bfloat16) for p in masked_heads(grads.T, head_count, 0)]
    query_stack = jnp.concatenate(
        [p.astype(jnp.bfloat16) for p in masked_heads(scaled, head_count, 1)], axis=0
    )
    grad_stack = jnp.concatenate(
        [p.astype(jnp.bfloat16) for p in masked_heads(grads, head_count, 1)], axis=0
    )
    row_dots = [
        jnp.sum(dots[head_rows(head, head_size), :], axis=0, keepdims=True)
        for head in range(head_count)
    ]
    start_row = start_ref[0:1, :]
    dqt_ref[...] = jnp.zeros_like(dqt_ref)

    query_wide = jnp.concatenate(query_turned, axis=1)
    grad_wide = jnp.concatenate(grad_turned, axis=1)
    row_wide = jnp.concatenate(row_dots, axis=1)
    lse_wide = jnp.concatenate([lse_ref[head : head + 1, :] for head in range(head_count)], axis=1)

    def body(masked, block, carry):
        rows = pl.ds(pl.multiple_of(block * size, size), size)
        scores = row_dot(k_ref[rows, :], query_wide)
        if masked:
            allowed = block_mask(block, step, size, start_row)
            scores = jnp.concatenate(
                [
                    jnp.where(allowed, scores[:, head * size : (head + 1) * size], masked_value)
                    for head in range(head_count)
                ],
                axis=1,
            )
        weights = jnp.exp(scores - lse_wide)
        weight_grad = row_dot(v_ref[rows, :], grad_wide)
        score_grad = (weights * (weight_grad - row_wide)).astype(jnp.bfloat16)
        weights = weights.astype(jnp.bfloat16)
        for head in range(head_count):
            part = head_rows(head, head_size)
            lanes = slice(head * size, (head + 1) * size)
            dqt_ref[part, :] += row_dot(kt_ref[part, rows], score_grad[:, lanes])
        dkey_ref[rows, :] += row_dot(score_grad, query_stack)
        dvalue_ref[rows, :] += row_dot(weights, grad_stack)
        return carry

    low = low_ref[step]
    inner = low_ref[blocks + step]
    lax.fori_loop(low, inner, functools.partial(body, True), 0)
    lax.fori_loop(inner, step, functools.partial(body, False), 0)
    body(True, step, 0)
    dq_ref[...] = (dqt_ref[...] * score_scale).T.astype(jnp.bfloat16)

    @pl.when(step == blocks - 1)
    def _():
        dk_ref[...] = dkey_ref[...].astype(jnp.bfloat16)
        dv_ref[...] = dvalue_ref[...].astype(jnp.bfloat16)


def attend_back(
    query, key, value, grad, attended, lse, start_rows, low_blocks, head_count, size, after=()
):
    length, width = query.shape
    blocks = length // size
    stat_rows = lse.shape[0]
    block_spec = spec((size, width), lambda i, low: (i, 0))
    whole_spec = spec((length, width), lambda i, low: (0, 0))
    return pl.pallas_call(
        later(functools.partial(attend_back_kernel, head_count), 8, len(after)),
        grid_spec=pltpu.PrefetchScalarGridSpec(
            num_scalar_prefetch=1,
            grid=(blocks,),
            in_specs=[
                block_spec,
                whole_spec,
                whole_spec,
                block_spec,
                block_spec,
                spec((stat_rows, size), lambda i, low: (0, i)),
                spec((8, size), lambda i, low: (0, i)),
                *later_specs(after),
            ],
            out_specs=[block_spec, whole_spec, whole_spec],
            scratch_shapes=[
                pltpu.VMEM((width, length), jnp.bfloat16),
                pltpu.VMEM((length, width), jnp.float32),
                pltpu.VMEM((length, width), jnp.float32),
                pltpu.VMEM((width, size), jnp.float32),
                pltpu.VMEM((size, head_count * size), jnp.bfloat16),
                pltpu.VMEM((size, head_count * size), jnp.bfloat16),
            ],
        ),
        out_shape=[jax.ShapeDtypeStruct((length, width), jnp.bfloat16)] * 3,
        compiler_params=kernel_params(),
        cost_estimate=small_cost,
        name="attend_back",
    )(with_inner(low_blocks, start_rows, size), query, key, value, grad, attended, lse, start_rows, *after)


def project_kernel(count, own_width, order_ref, *refs):
    block_refs, weight_refs, vector_ref = refs[:count], refs[count : 2 * count], refs[2 * count]
    weight_ref, plain_ref, normed_ref, q_ref, k_ref, v_ref = refs[2 * count + 1 :]
    piece = weight_refs[0].shape[0]

    @pl.when(pl.program_id(0) == 0)
    def _():
        for place in range(count):
            rows = pl.ds(pl.multiple_of(order_ref[place] * piece, piece), piece)
            weight_ref[rows, :] = weight_refs[place][:, : 3 * own_width]

    for place in range(count):

        @pl.when(pl.program_id(0) == place)
        def _():
            rows = norm_rows(block_refs[place][...].astype(jnp.float32), 1.0, 0.0)
            plain_ref[...] = rows.astype(jnp.bfloat16)
            normed = (rows * vector_ref[0:1, :] + vector_ref[1:2, :]).astype(jnp.bfloat16)
            normed_ref[...] = normed
            projected = row_dot(normed, weight_ref[...]).astype(jnp.bfloat16)
            q_ref[...] = projected[:, :own_width]
            k_ref[...] = projected[:, own_width : 2 * own_width]
            v_ref[...] = projected[:, 2 * own_width :]


def project_rows(blocks, weights, order, vectors):
    count = len(blocks)
    size, width = blocks[0].shape
    weight_rows = weights[0].shape[0]
    own_width = width // count
    whole = lambda shape: spec(shape, lambda i, order: (0, 0))
    placed = lambda columns: spec((size, columns), lambda i, order: (order[i], 0))
    return pl.pallas_call(
        functools.partial(project_kernel, count, own_width),
        grid_spec=pltpu.PrefetchScalarGridSpec(
            num_scalar_prefetch=1,
            grid=(count,),
            in_specs=[
                *[whole((size, width))] * count,
                *[whole(weights[0].shape)] * count,
                whole(vectors.shape),
            ],
            out_specs=[whole((width, 3 * own_width))]
            + [placed(width)] * 2
            + [placed(own_width)] * 3,
        ),
        out_shape=[jax.ShapeDtypeStruct((width, 3 * own_width), jnp.bfloat16)]
        + [jax.ShapeDtypeStruct((count * size, width), jnp.bfloat16)] * 2
        + [jax.ShapeDtypeStruct((count * size, own_width), jnp.bfloat16)] * 3,
        compiler_params=kernel_params(),
        cost_estimate=pl.CostEstimate(
            flops=13_000_000_000, bytes_accessed=1000, transcendentals=0
        ),
        name="project_rows",
    )(order, *blocks, *weights, vectors)


def planes_kernel(spacing, keys_ref, planes_ref, turned_ref, square_ref, wide_ref):
    near_count = keys_ref.shape[0] // spacing

    @pl.when(pl.program_id(0) == 0)
    def _():
        square_ref[...] = jnp.zeros_like(square_ref)

    wide_ref[...] = keys_ref[...].astype(jnp.float32)
    for plane in range(spacing):
        rows = slice(plane * near_count, (plane + 1) * near_count)
        keys = wide_ref[pl.ds(plane, near_count, stride=spacing), :]
        planes_ref[rows, :] = keys.astype(jnp.bfloat16)
        turned = keys.T
        turned_ref[:, rows] = turned.astype(jnp.bfloat16)
        square_ref[plane : plane + 1, :] += jnp.sum(turned * turned, axis=0, keepdims=True)


def key_planes(keys, spacing, after=()):
    count, width = keys.shape
    columns = row_chunk(width, (128,))
    near_count = count // spacing
    return pl.pallas_call(
        later(functools.partial(planes_kernel, spacing), 1, len(after)),
        grid=(width // columns,),
        in_specs=[spec((count, columns), lambda i: (0, i)), *later_specs(after)],
        out_specs=[
            spec((count, columns), lambda i: (0, i)),
            spec((columns, count), lambda i: (i, 0)),
            spec((spacing, near_count), lambda i: (0, 0)),
        ],
        out_shape=[
            jax.ShapeDtypeStruct((count, width), jnp.bfloat16),
            jax.ShapeDtypeStruct((width, count), jnp.bfloat16),
            jax.ShapeDtypeStruct((spacing, near_count), jnp.float32),
        ],
        scratch_shapes=[pltpu.VMEM((count, columns), jnp.float32)],
        compiler_params=kernel_params(),
        cost_estimate=small_cost,
        name="key_planes",
    )(keys, *after)


def near_kernel(spacing, dist_scale, parts, *refs):
    order_ref, query_ref, keys_ref, square_ref, values_ref = refs[:5]
    near_refs, target_refs = refs[5 : 5 + parts], refs[5 + parts : 5 + 2 * parts]
    e_ref, s_ref = refs[5 + 2 * parts :]
    piece, near_count = near_refs[0].shape[1:]
    rows = parts * piece
    lane = lax.broadcasted_iota(jnp.int32, (rows, near_count), 1)
    near = jnp.concatenate([ref[0] for ref in near_refs], axis=0)
    offset = near - spacing * lane
    target = jnp.concatenate([ref[0].T for ref in target_refs], axis=0)[:, 0:1]
    picked = jnp.zeros((rows, near_count), jnp.float32)
    words = jnp.full((rows, near_count), -1.0, jnp.float32)
    queries = query_ref[...]
    for plane in range(spacing):
        lanes = slice(plane * near_count, (plane + 1) * near_count)
        inner = row_dot(queries, keys_ref[:, lanes])
        chosen = offset == plane
        picked = jnp.where(chosen, 2.0 * inner - square_ref[plane : plane + 1, :], picked)
        words = jnp.where(chosen, values_ref[plane : plane + 1, :], words)
    scores = picked * dist_scale
    matched = words == target
    peak = jnp.max(scores, axis=1, keepdims=True)
    raised = jnp.exp(scores - peak)
    total = jnp.sum(raised, axis=1, keepdims=True)
    hits = jnp.sum(jnp.where(matched, raised, 0.0), axis=1, keepdims=True)
    e_ref[...] = jnp.where(matched, raised, -raised)
    stat_lane = lax.broadcasted_iota(jnp.int32, (rows, 128), 1)
    stats = jnp.where(stat_lane == 0, peak, jnp.where(stat_lane == 1, total, hits))
    for part in range(parts):
        s_ref[part] = stats[part * piece : (part + 1) * piece, :].T[: s_ref.shape[1], :]


def picked_specs(shape, parts):
    return [
        spec((1,) + shape, functools.partial(lambda part, i, order: (order[i * parts + part], 0, 0), part))
        for part in range(parts)
    ]


def near_scores(queries, keys_turned, square, values, near, target_rows, order, parts, spacing):
    stat_rows, piece = target_rows.shape[1:]
    near_count = near.shape[2]
    slot_rows = queries.shape[0]
    width, keys = keys_turned.shape
    rows = parts * piece
    return pl.pallas_call(
        functools.partial(near_kernel, spacing, width ** (-0.5), parts),
        grid_spec=pltpu.PrefetchScalarGridSpec(
            num_scalar_prefetch=1,
            grid=(slot_rows // rows,),
            in_specs=[
                spec((rows, width), lambda i, order: (i, 0)),
                spec((width, keys), lambda i, order: (0, 0)),
                spec((spacing, near_count), lambda i, order: (0, 0)),
                spec((spacing, near_count), lambda i, order: (0, 0)),
            ]
            + picked_specs((piece, near_count), parts)
            + picked_specs((stat_rows, piece), parts),
            out_specs=[
                spec((rows, near_count), lambda i, order: (i, 0)),
                spec((parts, stat_rows, piece), lambda i, order: (i, 0, 0)),
            ],
        ),
        out_shape=[
            jax.ShapeDtypeStruct((slot_rows, near_count), jnp.float32),
            jax.ShapeDtypeStruct((slot_rows // piece, stat_rows, piece), jnp.float32),
        ],
        compiler_params=kernel_params(),
        cost_estimate=small_cost,
        name="near_scores",
    )(order, queries, keys_turned, square, values, *[near] * parts, *[target_rows] * parts)


def near_back_kernel(spacing, factor, parts, *refs):
    order_ref, e_ref = refs[:2]
    near_refs, coeff_refs = refs[2 : 2 + parts], refs[2 + parts : 2 + 2 * parts]
    keys_ref, out_ref, dense_ref = refs[2 + 2 * parts :]
    piece, near_count = near_refs[0].shape[1:]
    lane = lax.broadcasted_iota(jnp.int32, (piece, near_count), 1)
    for part in range(parts):
        rows = slice(part * piece, (part + 1) * piece)
        offset = near_refs[part][0] - spacing * lane
        columns = coeff_refs[part][0].T
        coefficient, probability = columns[:, 0:1], columns[:, 1:2]
        marked = e_ref[rows, :]
        matched = jnp.where(marked > 0.0, 1.0, 0.0)
        grads = coefficient * (matched - probability) * jnp.abs(marked) * factor
        for plane in range(spacing):
            lanes = slice(plane * near_count, (plane + 1) * near_count)
            dense_ref[rows, lanes] = jnp.where(offset == plane, grads, 0.0).astype(jnp.bfloat16)
    out_ref[...] = row_dot(dense_ref[...], keys_ref[...]).astype(out_ref.dtype)


def near_back(marked, near, coeff_rows, keys_planes, order, parts, spacing, after=()):
    stat_rows, piece = coeff_rows.shape[1:]
    slot_rows, near_count = marked.shape
    keys, width = keys_planes.shape
    rows = parts * piece
    return pl.pallas_call(
        later(
            functools.partial(near_back_kernel, spacing, 2.0 * width ** (-0.5), parts),
            3 + 2 * parts,
            len(after),
        ),
        grid_spec=pltpu.PrefetchScalarGridSpec(
            num_scalar_prefetch=1,
            grid=(slot_rows // rows,),
            in_specs=[spec((rows, near_count), lambda i, order: (i, 0))]
            + picked_specs((piece, near_count), parts)
            + picked_specs((stat_rows, piece), parts)
            + [spec((keys, width), lambda i, order: (0, 0))]
            + later_specs(after),
            out_specs=spec((rows, width), lambda i, order: (i, 0)),
            scratch_shapes=[pltpu.VMEM((rows, keys), jnp.bfloat16)],
        ),
        out_shape=jax.ShapeDtypeStruct((slot_rows, width), jnp.bfloat16),
        compiler_params=kernel_params(),
        cost_estimate=small_cost,
        name="near_back",
    )(order, marked, *[near] * parts, *[coeff_rows] * parts, keys_planes, *after)


def pack_kernel(options, pick_ref, *refs):
    row_refs, (map_ref, out_ref, chosen_ref) = refs[:options], refs[options:]
    owners, capacity = out_ref.shape[:2]
    tokens = map_ref.shape[1]

    @pl.when(pl.program_id(0) == 0)
    def _():
        slot = lax.broadcasted_iota(jnp.int32, (capacity, tokens), 0)
        for owner in range(owners):
            chosen = jnp.where(map_ref[owner : owner + 1, :] == slot, 1.0, 0.0)
            chosen_ref[owner * capacity : (owner + 1) * capacity, :] = chosen.astype(jnp.bfloat16)

    rows = row_refs[0][...]
    for place in range(1, options):
        rows = jnp.where(pick_ref[0] == place, row_refs[place][...], rows)
    packed = row_dot(chosen_ref[...], rows).astype(out_ref.dtype)
    out_ref[...] = packed.reshape(out_ref.shape)


def pack_rows(options, pick, slot_map, capacity, after=()):
    owners, tokens = slot_map.shape
    width = options[0].shape[1]
    columns = row_chunk(width, (256,))
    return pl.pallas_call(
        later(functools.partial(pack_kernel, len(options)), 2 + len(options), len(after)),
        grid_spec=pltpu.PrefetchScalarGridSpec(
            num_scalar_prefetch=1,
            grid=(width // columns,),
            in_specs=[
                *[spec((tokens, columns), lambda i, pick: (0, i))] * len(options),
                spec((owners, tokens), lambda i, pick: (0, 0)),
                *later_specs(after),
            ],
            out_specs=spec((owners, capacity, columns), lambda i, pick: (0, 0, i)),
            scratch_shapes=[pltpu.VMEM((owners * capacity, tokens), jnp.bfloat16)],
        ),
        out_shape=jax.ShapeDtypeStruct((owners, capacity, width), options[0].dtype),
        compiler_params=kernel_params(),
        cost_estimate=pl.CostEstimate(
            flops=30_000_000_000, bytes_accessed=1000, transcendentals=0
        ),
        name="pack_rows",
    )(pick, *options, slot_map, *after)


def unpack_kernel(back_ref, column_ref, out_ref, chosen_ref):
    owners, capacity, columns = back_ref.shape
    tokens = out_ref.shape[0]

    @pl.when(pl.program_id(0) == 0)
    def _():
        slot = lax.broadcasted_iota(jnp.int32, (capacity, tokens), 0)
        for owner in range(owners):
            chosen = jnp.where(column_ref[owner : owner + 1, :] == slot, 1.0, 0.0)
            chosen_ref[owner * capacity : (owner + 1) * capacity, :] = chosen.astype(jnp.bfloat16)

    back = back_ref[...].reshape(owners * capacity, columns)
    out_ref[...] = left_dot(chosen_ref[...], back).astype(out_ref.dtype)


def unpack_rows(returned, slot_map, kind, after=()):
    owners, capacity, width = returned.shape
    tokens = slot_map.shape[1]
    columns = row_chunk(width, (256,))
    return pl.pallas_call(
        later(unpack_kernel, 2, len(after)),
        grid=(width // columns,),
        in_specs=[
            spec((owners, capacity, columns), lambda i: (0, 0, i)),
            spec((owners, tokens), lambda i: (0, 0)),
            *later_specs(after),
        ],
        out_specs=spec((tokens, columns), lambda i: (0, i)),
        out_shape=jax.ShapeDtypeStruct((tokens, width), kind),
        scratch_shapes=[pltpu.VMEM((owners * capacity, tokens), jnp.bfloat16)],
        compiler_params=kernel_params(),
        cost_estimate=small_cost,
        name="unpack_rows",
    )(returned, slot_map, *after)


def mix_kernel(stats_ref, map_ref, prob_ref, loss_ref, send_ref, peak_ref, total_ref, hits_ref):
    owners, stat_rows, capacity = stats_ref.shape
    tokens = map_ref.shape[1]
    slot = lax.broadcasted_iota(jnp.int32, (capacity, tokens), 0)
    for owner in range(owners):
        chosen = map_ref[owner : owner + 1, :] == slot
        columns = stats_ref[owner].T
        for place, target in enumerate((peak_ref, total_ref, hits_ref)):
            target[owner : owner + 1, :] = jnp.sum(
                jnp.where(chosen, columns[:, place : place + 1], 0.0), axis=0, keepdims=True
            )
    member = map_ref[...] >= 0
    peaks = jnp.where(member, peak_ref[...], -3e38)
    best = jnp.max(peaks, axis=0, keepdims=True)
    rescale = jnp.where(member, jnp.exp(peaks - best), 0.0)
    knn_total = jnp.sum(total_ref[...] * rescale, axis=0, keepdims=True)
    knn_prob = jnp.sum(hits_ref[...] * rescale, axis=0, keepdims=True) / knn_total
    mixture = mix_weight * knn_prob + (1.0 - mix_weight) * prob_ref[...]
    loss_ref[...] = -jnp.log(mixture)
    peak_ref[...] = (-mix_weight / (mixture * knn_total)) * rescale
    for owner in range(owners):
        chosen = map_ref[owner : owner + 1, :] == slot
        coefficient = jnp.sum(
            jnp.where(chosen, peak_ref[owner : owner + 1, :], 0.0), axis=1, keepdims=True
        )
        probability = jnp.sum(jnp.where(chosen, knn_prob, 0.0), axis=1, keepdims=True)
        lane = lax.broadcasted_iota(jnp.int32, (capacity, 128), 1)
        both = jnp.where(lane == 0, coefficient, probability)
        send_ref[owner] = both.T[:stat_rows, :]


def mix_losses(stats, slot_map, model_prob):
    owners, stat_rows, capacity = stats.shape
    tokens = slot_map.shape[1]
    vmem = pl.BlockSpec(memory_space=pltpu.VMEM)
    return pl.pallas_call(
        mix_kernel,
        in_specs=[vmem] * 3,
        out_specs=[vmem] * 2,
        out_shape=[
            jax.ShapeDtypeStruct((1, tokens), jnp.float32),
            jax.ShapeDtypeStruct(stats.shape, jnp.float32),
        ],
        scratch_shapes=[pltpu.VMEM((owners, tokens), jnp.float32)] * 3,
        compiler_params=pltpu.CompilerParams(vmem_limit_bytes=vmem_limit),
        name="mix_losses",
    )(stats, slot_map, model_prob)


def row_chunk(total, choices):
    for choice in choices:
        if total % choice == 0:
            return choice
    return total


def slot_picker(slot_map, capacity):
    return slot_map[:, None, :] == jnp.arange(capacity, dtype=jnp.int32)[None, :, None]


def layer_table(count):
    return [
        sorted(range(count), key=lambda other: (abs(other - layer), (other ^ layer) != 1, other))
        for layer in range(count)
    ]


def own_choice(options):
    layer = lax.axis_index("batch")
    kept = options[0]
    for place in range(1, len(options)):
        if all(options[place] is not other for other in options[:place]):
            same = [i for i, other in enumerate(options) if other is options[place]]
            here = functools.reduce(jnp.logical_or, [layer == i for i in same])
            kept = jnp.where(here, options[place], kept)
    return kept


def layer_step(step, ups, downs):
    options, picks = [], []
    for layer, line in enumerate(layer_table(lax.axis_size("batch"))):
        there = line[step]
        block = ups[layer - there] if there < layer else downs[there - layer]
        places = [place for place, other in enumerate(options) if other is block]
        if not places:
            options.append(block)
        picks.append(places[0] if places else len(options) - 1)
    return options, jnp.array(picks, jnp.int32)[lax.axis_index("batch")][None]


def layer_hop(hop, blocks, above, below):
    count = lax.axis_size("batch")
    reach = count - hop
    table = layer_table(count)

    def bound(layer, to):
        return blocks[table[layer].index(to) if 0 <= to < count else hop_step]

    hop_step = reach
    up = own_choice([bound(layer, layer + reach) for layer in range(count)])
    down = own_choice([bound(layer, layer - reach) for layer in range(count)])
    if hop > 1:
        up = (up.astype(jnp.float32) + above).astype(up.dtype)
        down = (down.astype(jnp.float32) + below).astype(down.dtype)
    return (
        lax.ppermute(up, "batch", [(i, i + 1) for i in range(hop)]),
        lax.ppermute(down, "batch", [(i, i - 1) for i in range(reach, count)]),
    )


def across(rows, step):
    return lax.ppermute(rows, "ctx", [(i, i ^ step) for i in range(lax.axis_size("ctx"))])


def in_ctx_order(parts):
    count = len(parts)
    own = lax.axis_index("ctx")
    stacked = jnp.stack(parts)
    return stacked[jnp.arange(count, dtype=jnp.int32) ^ own]


def ctx_gather(rows):
    return in_ctx_order([rows] + [across(rows, step) for step in range(1, lax.axis_size("ctx"))])


def swap_cores(rows):
    return lax.ppermute(rows, "rep", [(0, 1), (1, 0)])


def reduce_cores(grad):
    count = lax.axis_size("ctx")
    parts = grad.astype(jnp.bfloat16).reshape(count, 2, grad.shape[0] // (2 * count), grad.shape[1])
    core = lax.axis_index("rep")
    keep = lax.dynamic_index_in_dim(parts, core, 1, keepdims=False)
    send = lax.dynamic_index_in_dim(parts, 1 - core, 1, keepdims=False)
    return (keep.astype(jnp.float32) + swap_cores(send)).astype(jnp.bfloat16)


def ctx_trade(blocks):
    return [part if step == 0 else across(part, step) for step, part in enumerate(blocks)]


def exchange(blocks, axis):
    return lax.all_to_all(blocks, axis, split_axis=0, concat_axis=0, tiled=True)


def block_sum(blocks):
    total = blocks[0].astype(jnp.float32)
    for place in range(1, len(blocks)):
        total = total + blocks[place].astype(jnp.float32)
    return total


def ctx_reduce(halves):
    return lax.psum_scatter(halves, "ctx", scatter_dimension=0)


def layer_total(blocks):
    return block_sum(exchange(blocks, "batch")).astype(jnp.bfloat16)


def layer_blocks(rows):
    return rows.reshape(lax.axis_size("batch"), -1, rows.shape[1])


def both_halves(half):
    other = swap_cores(half)
    first = lax.axis_index("rep") == 0
    both = jnp.stack([jnp.where(first, half, other), jnp.where(first, other, half)])
    return both.reshape(-1, half.shape[-1]).astype(jnp.float32)


def layer_gather(rows):
    count = lax.axis_size("batch")
    return [rows] + [
        lax.ppermute(rows, "batch", [(i, (i + hops) % count) for i in range(count)])
        for hops in range(1, count)
    ]


def whole_shard(parts):
    count, layer = len(parts), lax.axis_index("batch")
    return both_halves(jnp.stack(parts)[(layer - jnp.arange(count, dtype=jnp.int32)) % count])


def mix_any(stats, slot_map, model_prob):
    owners, stat_rows, capacity = stats.shape
    if capacity % 16 == 0:
        return mix_losses(stats, slot_map, model_prob)
    chosen = slot_picker(slot_map, capacity)
    peak, total, hits = [
        jnp.sum(jnp.where(chosen, stats[:, row, :, None], 0.0), axis=1) for row in range(3)
    ]
    member = slot_map >= 0
    peaks = jnp.where(member, peak, -3e38)
    best = jnp.max(peaks, axis=0, keepdims=True)
    rescale = jnp.where(member, jnp.exp(peaks - best), 0.0)
    knn_total = jnp.sum(total * rescale, axis=0, keepdims=True)
    knn_prob = jnp.sum(hits * rescale, axis=0, keepdims=True) / knn_total
    mixture = mix_weight * knn_prob + (1.0 - mix_weight) * model_prob
    coefficient = (-mix_weight / (mixture * knn_total)) * rescale
    sent = [
        jnp.sum(jnp.where(chosen, part[:, None, :], 0.0), axis=2)
        for part in (coefficient, jnp.broadcast_to(knn_prob, coefficient.shape))
    ]
    sent = jnp.stack(sent + [sent[1]] * (stat_rows - 2), axis=1)
    return -jnp.log(mixture), sent


def local(
    tokens,
    cotangent,
    segment_ids,
    first_gain,
    first_shift,
    second_gain,
    second_shift,
    final_gain,
    final_shift,
    project_weight,
    output_weight,
    upward_weight,
    downward_weight,
    store_keys,
    store_values,
    owners,
    neighbours,
    targets,
    model_prob,
):
    head_count = HEADS
    group_seqs, block_len, width = tokens.shape
    seq_len = segment_ids.shape[1]
    ctx_count = lax.axis_size("ctx")
    shard_count = lax.axis_size("batch") * ctx_count
    capacity = neighbours.shape[3]
    near_count = neighbours.shape[4]
    top_count = owners.shape[2]
    key_count = store_keys.shape[0]
    spacing = key_count // near_count
    slot_rows = shard_count * capacity
    everyone = ("batch", "ctx")
    own_heads = head_count // ctx_count
    own_width = width // ctx_count
    attend_size = row_chunk(seq_len, (256, 128))

    arrived = [tokens[0]] + [across(tokens[0], step) for step in range(1, ctx_count)]
    own_rows = project_weight.shape[0]
    own_ctx = lax.axis_index("ctx")
    vectors = jnp.stack(
        [first_gain, first_shift, second_gain, second_shift, final_gain, final_shift], axis=1
    )
    vectors = jnp.pad(vectors, ((0, 0), (0, 128 - vectors.shape[1])))
    proj_pieces = [
        jnp.concatenate(
            [
                lax.dynamic_slice_in_dim(
                    project_weight, part * width + (own_ctx ^ step) * own_width, own_width, 1
                )
                for part in range(3)
            ]
            + [vectors],
            axis=1,
        )
        for step in range(ctx_count)
    ]
    proj_pieces = ctx_trade(proj_pieces)
    vectors = in_ctx_order([piece[:, 3 * own_width :] for piece in proj_pieces])
    vectors = vectors.reshape(width, -1)[:, :6].T.astype(jnp.float32)
    gain_list = [vectors[row] for row in range(6)]

    member = jnp.any(
        owners[0][:, :, None] == jnp.arange(shard_count, dtype=jnp.int32)[None, None, :], axis=1
    )
    place = jnp.arange(block_len, dtype=jnp.int32)
    earlier = (place[:, None] <= place[None, :]).astype(jnp.bfloat16)
    running = left_dot(member.astype(jnp.bfloat16), earlier).astype(jnp.int32)
    slot_map = jnp.where(member.T, running - 1, -1)
    send_targets = jnp.sum(
        jnp.where(slot_picker(slot_map, capacity), targets.reshape(1, 1, -1), 0), axis=2
    )
    got_targets = exchange(send_targets.astype(jnp.int32), everyone).astype(jnp.float32)
    value_planes = store_values.astype(jnp.float32).reshape(near_count, spacing).T
    by_layer = capacity % 16 == 0
    if by_layer:
        piece, parts = capacity, 2 if ctx_count % 2 == 0 else 1
        layer_count = lax.axis_size("batch")
        maps = exchange(slot_map.reshape(layer_count, ctx_count, block_len), "batch")
        table = jnp.array(layer_table(layer_count), jnp.int32)[lax.axis_index("batch")]
        maps = maps[table]
        orders = table[:, None] * ctx_count + jnp.arange(ctx_count, dtype=jnp.int32)[None, :]
    else:
        piece, parts = row_chunk(slot_rows, (576, 512, 384, 256, 128)), 1
        orders = jnp.arange(slot_rows // piece, dtype=jnp.int32)[None, :]
        chosen_slots = slot_picker(slot_map, capacity).astype(jnp.bfloat16)
    near_table = neighbours.reshape(slot_rows // piece, piece, near_count)
    stat_shape = (slot_rows // piece, 8, piece)
    target_rows = jnp.broadcast_to(got_targets.reshape(stat_shape[0], 1, piece), stat_shape)

    early = proj_pieces[1:]
    core = lax.axis_index("rep")

    def own_half(weight):
        half = weight.shape[0] // 2
        mine = lax.dynamic_slice_in_dim(weight, core * half, half, 0)
        return run_after([mine], [*arrived[1:], *early])[0]

    def gather_weight(weight):
        return lax.all_gather(own_half(weight), ("ctx", "rep"), axis=0, tiled=True)

    out_full = gather_weight(output_weight)
    down_full = gather_weight(downward_weight)
    up_half = own_half(upward_weight)
    up_pieces = [across(up_half, step) for step in range(1, ctx_count)]
    sources = own_ctx ^ jnp.arange(ctx_count, dtype=jnp.int32)

    segments = segment_ids[0]
    start_rows = jnp.sum((segments[None, :] < segments[:, None]).astype(jnp.int32), axis=1)
    low_blocks = start_rows[::attend_size] // attend_size
    start_rows = jnp.broadcast_to(start_rows[None, :], (8, seq_len))
    proj_own, plain_full, normed_full, query_own, key_own, value_own = project_rows(
        arrived, proj_pieces, sources, vectors
    )
    attended_own, log_total = attend(
        query_own, key_own, value_own, start_rows, low_blocks, own_heads, attend_size
    )
    attended = lax.all_to_all(attended_own, "ctx", split_axis=0, concat_axis=1, tiled=True)
    attended = run_after([attended], [target_rows, maps] if by_layer else [target_rows])[0]
    up_pieces = [up_half, *run_after(up_pieces, [attended])]
    up_full = place_rows(
        up_pieces + [swap_cores(piece) for piece in up_pieces],
        jnp.concatenate([2 * sources + core, 2 * sources + 1 - core]),
    )
    inputs = tokens[0].astype(jnp.float32)
    hidden = inputs + row_dot(attended, out_full)
    normed_two = norm_rows(hidden, gain_list[2], gain_list[3]).astype(jnp.bfloat16)
    upper_rows = row_dot(normed_two, up_full)
    active = jax.nn.gelu(upper_rows).astype(jnp.bfloat16)
    summed = hidden + row_dot(active, down_full)
    final_rows = norm_rows(summed, gain_list[4], gain_list[5]).astype(jnp.bfloat16)

    if by_layer:
        ups, downs, packed, queries = [final_rows], [final_rows], [], []
        for step in range(layer_count):
            hop = step + 1
            if hop < layer_count:
                up, down = ups[-1], downs[-1]
                if hop == 2:
                    up, down = run_after([up, down], packed)
                    ups[-1], downs[-1] = up, down
                elif hop > 2:
                    up, down = run_after([up, down], [queries[hop - 3]])
                    ups[-1], downs[-1] = up, down
                ups.append(
                    lax.ppermute(up, "batch", [(i, i + 1) for i in range(step, layer_count - 1)])
                )
                downs.append(
                    lax.ppermute(down, "batch", [(i, i - 1) for i in range(1, layer_count - step)])
                )
            options, pick = layer_step(step, ups, downs)
            between = ()
            if step == 1:
                between = planes, planes_turned, key_square = key_planes(
                    store_keys, spacing, packed
                )
            packed.append(pack_rows(options, pick, maps[step], capacity, between))
            queries.append(exchange(packed[step], "ctx").reshape(-1, width))
    else:
        planes, planes_turned, key_square = key_planes(store_keys, spacing)
        packed = jnp.einsum(
            "ost,tw->osw", chosen_slots, final_rows, preferred_element_type=jnp.float32
        )
        queries = [exchange(packed.astype(jnp.bfloat16), everyone).reshape(slot_rows, width)]
    marked, stats = zip(
        *[
            near_scores(
                rows,
                planes_turned,
                key_square,
                value_planes,
                near_table,
                target_rows,
                orders[step],
                parts,
                spacing,
            )
            for step, rows in enumerate(queries)
        ]
    )
    if by_layer:
        inverse = jnp.argmin(
            jnp.abs(table[None, :] - jnp.arange(layer_count, dtype=jnp.int32)[:, None]), axis=1
        )
        stats = jnp.stack(stats)[inverse].reshape(stat_shape)
    else:
        stats = stats[0].transpose(1, 0, 2).reshape(8, shard_count, capacity).transpose(1, 0, 2)
    token_loss, send_coeff = mix_any(exchange(stats, everyone), slot_map, model_prob)
    got_coeff = exchange(send_coeff, everyone)
    if not by_layer:
        got_coeff = got_coeff.transpose(1, 0, 2).reshape(8, -1, piece).transpose(1, 0, 2)
    if by_layer:
        returned, above, below = {}, None, None
        for step in reversed(range(layer_count)):
            hop = layer_count - 1 - step
            partial_grad = near_back(
                marked[step],
                near_table,
                got_coeff,
                planes,
                orders[step],
                parts,
                spacing,
                [returned[step + 2]] if hop >= 2 else [],
            )
            back = exchange(partial_grad.reshape(ctx_count, capacity, width), "ctx")
            if hop > 0:
                above, below = layer_hop(hop, returned, above, below)
            returned[step] = unpack_rows(
                back,
                maps[step],
                jnp.bfloat16 if step > 0 else jnp.float32,
                [above, below] if 0 < hop < layer_count - 1 else [],
            )
        query_grad = returned[0] + above.astype(jnp.float32) + below.astype(jnp.float32)
    else:
        partial_grad = near_back(
            marked[0], near_table, got_coeff, planes, orders[0], parts, spacing
        )
        back = exchange(partial_grad.reshape(shard_count, capacity, width), everyone)
        query_grad = jnp.einsum(
            "ost,osw->tw", chosen_slots, back, preferred_element_type=jnp.float32
        )

    out_grad = cotangent[0].astype(jnp.float32) + query_grad
    final_vjp = jax.vjp(norm_rows, summed, gain_list[4], gain_list[5])[1]
    summed_grad, final_gain_grad, final_shift_grad = final_vjp(out_grad)
    branch_grad = summed_grad.astype(jnp.bfloat16)
    downward_grad = left_dot(active, branch_grad)
    active_grad = right_dot(branch_grad, down_full)
    gelu_vjp = jax.vjp(jax.nn.gelu, upper_rows)[1]
    upper_grad = gelu_vjp(active_grad)[0].astype(jnp.bfloat16)
    downward_half = reduce_cores(downward_grad)
    upper_grad = run_after([upper_grad], [downward_half])[0]
    second_vjp = jax.vjp(norm_rows, hidden, gain_list[2], gain_list[3])[1]
    hidden_part, second_gain_grad, second_shift_grad = second_vjp(right_dot(upper_grad, up_full))
    hidden_grad = summed_grad + hidden_part
    attn_grad = hidden_grad.astype(jnp.bfloat16)
    attended_grad = right_dot(attn_grad, out_full).astype(jnp.bfloat16)
    downward_half = ctx_reduce(downward_half)
    second_half = reduce_cores(
        jnp.concatenate(
            [
                left_dot(normed_two, upper_grad).astype(jnp.bfloat16),
                left_dot(attended, attn_grad).astype(jnp.bfloat16),
            ],
            axis=1,
        )
    )
    attended_grad = run_after([attended_grad], [downward_half])[0]
    grad_own = lax.all_to_all(attended_grad, "ctx", split_axis=1, concat_axis=0, tiled=True)
    second_half = run_after([second_half], [grad_own])[0]
    downward_half = run_after([downward_half], [second_half])[0]
    downward_total = layer_total(layer_blocks(downward_half))
    second_start = second_half
    second_half = ctx_reduce(second_half)
    proj_grad = jnp.concatenate(
        run_after(
            attend_back(
                query_own,
                key_own,
                value_own,
                grad_own,
                attended_own,
                log_total,
                start_rows,
                low_blocks,
                own_heads,
                attend_size,
                (second_start, downward_half),
            ),
            [downward_total],
        ),
        axis=1,
    )
    normed_terms = right_dot(proj_grad, proj_own).astype(jnp.bfloat16)
    normed_grad = lax.psum_scatter(normed_terms, "ctx", scatter_dimension=0, tiled=True)

    second_half = run_after([second_half], [normed_terms])[0]
    second_total = layer_total(layer_blocks(second_half))
    second_parts = layer_gather(second_total)
    plain_part = left_dot(plain_full, proj_grad)
    column_sums = jnp.sum(proj_grad.astype(jnp.float32), axis=0)
    proj_full = proj_own.astype(jnp.float32)
    first_gain_grad = jnp.sum(plain_part * proj_full, axis=1)
    first_shift_grad = jnp.sum(column_sums[None, :] * proj_full, axis=1)
    project_part = plain_part * gain_list[0][:, None] + column_sums[None, :] * gain_list[1][:, None]

    vector_part = jnp.stack(
        [
            first_gain_grad,
            first_shift_grad,
            second_gain_grad,
            second_shift_grad,
            final_gain_grad,
            final_shift_grad,
        ],
        axis=1,
    )
    vector_part = jnp.pad(vector_part, ((0, 0), (0, 128 - vector_part.shape[1])))
    project_part = jnp.concatenate([project_part, vector_part], axis=1).astype(jnp.bfloat16)
    project_part = reduce_cores(run_after([project_part], [second_total])[0])
    downward_parts = layer_gather(run_after([downward_total], [project_part])[0])
    project_part = in_ctx_order(
        ctx_trade(
            [
                lax.dynamic_index_in_dim(project_part, own_ctx ^ step, 0, keepdims=False)
                for step in range(ctx_count)
            ]
        )
    )
    vector_part = block_sum(project_part[:, :, 3 * own_width :]).astype(jnp.bfloat16)
    project_part = (
        project_part[:, :, : 3 * own_width]
        .reshape(ctx_count, own_rows // 2, 3, own_width)
        .transpose(1, 2, 0, 3)
        .reshape(own_rows // 2, 3 * width)
    )
    small_rows = jnp.concatenate([project_part, vector_part], axis=1)
    small_rows = run_after([small_rows], second_parts[1:])[0]
    small_total = layer_total(layer_blocks(small_rows))
    input_vjp = jax.vjp(lambda rows: norm_rows(rows, gain_list[0], gain_list[1]), inputs)[1]
    normed_grad = run_after([normed_grad], [small_total])[0]
    input_grad = hidden_grad + input_vjp(normed_grad.astype(jnp.float32))[0]
    small_grads = whole_shard(layer_gather(small_total))
    second_grads = whole_shard(second_parts)
    weight_grads = [
        small_grads[:, : 3 * width],
        second_grads[:, second_grads.shape[1] - width :],
        second_grads[:, : second_grads.shape[1] - width],
        whole_shard(downward_parts),
    ]
    vector_grads = small_grads[:, 3 * width : 3 * width + 6].T
    return (
        final_rows.reshape(group_seqs, block_len, width),
        token_loss.reshape(group_seqs, block_len),
        query_grad.reshape(group_seqs, block_len, width),
        input_grad.reshape(group_seqs, block_len, width),
        *weight_grads,
        *[vector_grads[row] for row in range(6)],
    )


def solution(mesh):
    placed = (
        P(("rep", "batch"), "ctx", None),
        P(("rep", "batch"), "ctx", None),
        P(("rep", "batch"), None),
        P("ctx"),
        P("ctx"),
        P("ctx"),
        P("ctx"),
        P("ctx"),
        P("ctx"),
        P("ctx", None),
        P("ctx", None),
        P("ctx", None),
        P("ctx", None),
        P(("batch", "ctx"), None),
        P(("batch", "ctx")),
        P(("rep", "batch"), "ctx", None),
        P("rep", ("batch", "ctx"), None, None, None),
        P(("rep", "batch"), "ctx"),
        P(("rep", "batch"), "ctx"),
    )
    return jax.shard_map(
        local,
        mesh=mesh,
        in_specs=placed,
        out_specs=(
            P(("rep", "batch"), "ctx", None),
            P(("rep", "batch"), "ctx"),
            P(("rep", "batch"), "ctx", None),
            P(("rep", "batch"), "ctx", None),
            P("ctx", None),
            P("ctx", None),
            P("ctx", None),
            P("ctx", None),
            P("ctx"),
            P("ctx"),
            P("ctx"),
            P("ctx"),
            P("ctx"),
            P("ctx"),
        ),
        check_vma=False,
    )
```
